32 devices in a mesh: dp: 8 (over z, x), mod: 4 (over y, core).
Axes of the slice: x: 2, y: 2, z: 4, core: 2. Of those that a mesh axis runs over, the one named last changes fastest.
Arguments:
- latents: float32 [16384, 16], P(('dp', 'mod')), may hold values from -6 to 6
- noise: float32 [16384, 16], P(('dp', 'mod')), may hold values from -6 to 6
- timesteps: int32 [64], P(('dp', 'mod')), may hold values from 0 to 999
- labels: int32 [64], P(('dp', 'mod')), may hold values from 0 to 999
- dropped: int32 [64], P(('dp', 'mod')), may hold values 0 or 1
- block_master: float32 [15980544], P(('dp', 'mod')), may hold values from -2 to 2
- block_m: float32 [15980544], P(('dp', 'mod')), may hold values from -1 to 1
- block_v: float32 [15980544], P(('dp', 'mod')), may hold values from 0 to 1, as said below
- stem_master: float32 [5439744], P(('dp', 'mod')), may hold values from -8 to 8
- stem_m: float32 [5439744], P(('dp', 'mod')), may hold values from -1 to 1
- stem_v: float32 [5439744], P(('dp', 'mod')), may hold values from 0 to 1, as said below
- ada_w: float32 [1152, 6912], P('dp', 'mod'), may hold values from -0.25 to 0.25
- ada_w_m: float32 [1152, 6912], P('dp', 'mod'), may hold values from -1 to 1
- ada_w_v: float32 [1152, 6912], P('dp', 'mod'), may hold values from 0 to 1, as said below
Outputs:
- loss_sum: float32 [], replicated
- grad_norm: float32 [], replicated
- block_new: float32 [15980544], P(('dp', 'mod'))
- block_m_new: float32 [15980544], P(('dp', 'mod'))
- block_v_new: float32 [15980544], P(('dp', 'mod'))
- stem_new: float32 [5439744], P(('dp', 'mod'))
- stem_m_new: float32 [5439744], P(('dp', 'mod'))
- stem_v_new: float32 [5439744], P(('dp', 'mod'))
- ada_w_new: float32 [1152, 6912], P('dp', 'mod')
- ada_w_m_new: float32 [1152, 6912], P('dp', 'mod')
- ada_w_v_new: float32 [1152, 6912], P('dp', 'mod')
The draws below stay inside these ranges and needn't reach their ends.
Inputs may be any that keep to these rules, and one draw needn't show every extreme that they name: `block_v`: positive. `stem_v`: positive. `ada_w_v`: positive.
All inputs are finite; a program needn't handle non-finite values. No bound on the sum of `dropped` on one device may be relied on, other than what follows from the above.
Results may differ from the reference program's by a relative error of at most 0.0024.
The reference program's roundings to bfloat16 on the way count: a program that leaves them out, or rounds other values in their place, can miss the bound.
Values may be sent and summed in bfloat16 or wider, within the bound.
No kernel may reach another device: no remote copies, remote signals or barrier semaphores. Data moves between devices by JAX's collectives and lax.ppermute only.
A program may use at most 320 MiB of HBM per device.

```python
import math
import jax
import jax.numpy as jnp
from jax import lax

D = 1152
HEADS = 16
HEAD_DIM = 72
FF = 4608
CLASSES = 1000
PATCH = 16
OUT = 32
GRID = 16
FREQ = 256
TSTEPS = 1000
STEP = 10
SEQ = 256
IMAGES = 64
TOKENS = 16384
WB = 13872
SROWS = 4722
NPARAM = 29382912
N_DP = 8


def gauss_or_flat(key, shape):
    first_key = jax.random.fold_in(key, 0)
    gaussian = jnp.clip(jax.random.normal(first_key, shape, jnp.float32), -3.5, 3.5)
    return gaussian


def first_moment(key, shape):
    return gauss_or_flat(key, shape) * (0.11 / math.sqrt(NPARAM))


def second_moment(key, shape, exponent):
    spread_level = jax.random.uniform(key, shape, jnp.float32)
    return jnp.exp(math.log(4.0) * spread_level ** exponent) * (0.001 / NPARAM)


def draw_block_master(key, part):
    key = jax.random.fold_in(key, 3)
    column_scales = jnp.concatenate([jnp.full((3 * D,), 0.7 / math.sqrt(D), jnp.float32), jnp.full((D,), 2.5 / math.sqrt(D), jnp.float32), jnp.full((FF,), 0.7 / math.sqrt(D), jnp.float32), jnp.full((FF,), 1.5 / math.sqrt(FF), jnp.float32), jnp.full((PATCH,), 0.25, jnp.float32), jnp.full((OUT,), 0.5 / math.sqrt(D), jnp.float32)])
    values = gauss_or_flat(key, (D, WB))
    return (values * column_scales[None, :]).reshape(D * WB)


def draw_stem_master(key, part):
    key = jax.random.fold_in(key, 5)
    row_scales = jnp.concatenate([jnp.full((FREQ,), 1.0 / math.sqrt(FREQ), jnp.float32), jnp.full((D,), 0.5 / math.sqrt(D), jnp.float32), jnp.full((CLASSES + 1,), 0.2, jnp.float32), jnp.full((2 * D,), 1.4 / math.sqrt(D), jnp.float32), jnp.full((3,), 0.3, jnp.float32)])
    values = gauss_or_flat(key, (SROWS, D))
    scale_rise = 2.0
    position = jnp.arange(D).astype(jnp.float32)[None, :] / D
    ramps = jnp.concatenate([0.0 * position, scale_rise * position, 0.5 + position] * 2, 0)
    jitter = jnp.array([0.3, 0.15, 0.15, 0.3, 0.15, 0.15], jnp.float32)[:, None]
    matrix_rows = values[:SROWS - 6] * row_scales[:, None]
    bias_rows = ramps + values[SROWS - 6:] * jitter
    return jnp.concatenate([matrix_rows, bias_rows], 0).reshape(SROWS * D)


def draw_block_m(key, part):
    key = jax.random.fold_in(key, 7)
    return first_moment(key, (D * WB,))


def draw_block_v(key, part):
    key = jax.random.fold_in(key, 11)
    return second_moment(key, (D * WB,), 1.0)


def draw_stem_m(key, part):
    key = jax.random.fold_in(key, 13)
    return first_moment(key, (SROWS * D,))


def draw_stem_v(key, part):
    key = jax.random.fold_in(key, 17)
    return second_moment(key, (SROWS * D,), 1.0)


def draw_ada_w_m(key, part):
    key = jax.random.fold_in(key, 19)
    return first_moment(key, (D, 6 * D))


def draw_ada_w_v(key, part):
    key = jax.random.fold_in(key, 23)
    return second_moment(key, (D, 6 * D), 1.0)


def with_ends(entries, own_key, low, high):
    spot = [jax.random.randint(jax.random.fold_in(own_key, axis), (), 0, length) for axis, length in enumerate(entries.shape)]
    longest = entries.shape.index(max(entries.shape))
    next_to = spot[:longest] + [(spot[longest] + 1) % entries.shape[longest]] + spot[longest + 1:]
    return entries.at[tuple(spot)].set(low).at[tuple(next_to)].set(high)


def block_scale(rng, shape, cuts, least, top_value):
    factor_of, own = 1.0, jax.random.fold_in(rng, 6)
    for dim, blocks in cuts:
        steps = jnp.exp(jax.random.uniform(jax.random.fold_in(own, dim), (blocks,), jnp.float32, least / len(cuts), top_value / len(cuts)))
        factor_of = factor_of * jnp.repeat(steps, shape[dim] // blocks).reshape([-1 if axis == dim else 1 for axis in range(len(shape))])
    return factor_of


def scatter_about(key, shape, width, most, shards=(), held_as=jnp.bfloat16):
    result = jax.random.normal(key, shape, jnp.float32) * width
    if len(shards) > 0:
        result = block_scale(key, shape, shards, -0.22, 0.18) * result
    return jnp.clip(result, min=-most, max=most).astype(held_as)


def setup_inputs(seed: int = 0) -> dict:
    keys = jax.random.split(jax.random.key(seed), 15)
    return {
        "latents": scatter_about(keys[0], (TOKENS, PATCH), 1.0, 6.0, ((0, 32),), jnp.float32),
        "noise": scatter_about(keys[1], (TOKENS, PATCH), 1.0, 6.0, ((0, 32),), jnp.float32),
        "timesteps": with_ends(jax.random.randint(keys[2], (IMAGES,), 0, TSTEPS), jax.random.fold_in(keys[2], 1), 0, TSTEPS - 1).astype(jnp.int32),
        "labels": with_ends(jax.random.randint(keys[3], (IMAGES,), 0, CLASSES), jax.random.fold_in(keys[3], 1), 0, CLASSES - 1).astype(jnp.int32),
        "dropped": with_ends((jax.random.randint(keys[4], (IMAGES,), 0, 10) < 1).astype(jnp.int32), jax.random.fold_in(keys[4], 1), 0, 1),
        "block_master": draw_block_master(jax.random.fold_in(keys[14], 71), 0),
        "block_m": draw_block_m(jax.random.fold_in(keys[14], 71), 0),
        "block_v": draw_block_v(jax.random.fold_in(keys[14], 71), 0),
        "stem_master": draw_stem_master(jax.random.fold_in(keys[14], 71), 0),
        "stem_m": draw_stem_m(jax.random.fold_in(keys[14], 71), 0),
        "stem_v": draw_stem_v(jax.random.fold_in(keys[14], 71), 0),
        "ada_w": scatter_about(keys[11], (D, 6 * D), (D // 2) ** -0.5, 0.25, ((0, 8), (1, 4)), jnp.float32),
        "ada_w_m": draw_ada_w_m(jax.random.fold_in(keys[14], 71), 0),
        "ada_w_v": draw_ada_w_v(jax.random.fold_in(keys[14], 71), 0),
    }


HIGHEST_PRECISION = lax.Precision.HIGHEST
LOG_TWO = math.log(2.0)
THRESHOLD = 1.0
LEARN_RATE = 0.05
BETA_ONE = 0.9
BETA_TWO = 0.999
EPSILON = 1e-08

@jax.custom_vjp
def low(v):
    return lax.optimization_barrier(v.astype(jnp.bfloat16)).astype(jnp.float32)

@jax.custom_vjp
def low_back(v):
    return v

def low_keep(v):
    return (low(v), None)

def low_pass(kept, grad):
    return (grad,)

def back_keep(v):
    return (v, None)

def back_low(kept, grad):
    return (low(grad),)
low.defvjp(low_keep, low_pass)
low_back.defvjp(back_keep, back_low)

def product(form, left, right):
    return jnp.einsum(form, left, right, precision=HIGHEST_PRECISION)

def plan(steps):
    step_index = jnp.arange(TSTEPS).astype(jnp.float32)
    beta_rows = 0.0001 + (0.02 - 0.0001) * step_index / (TSTEPS - 1)
    alpha_bar = jnp.cumprod(1.0 - beta_rows)
    previous = jnp.concatenate([jnp.ones((1,), jnp.float32), alpha_bar[:-1]])
    posterior = beta_rows * (1.0 - previous) / (1.0 - alpha_bar)
    clipped = jnp.concatenate([posterior[1:2], posterior[1:]])
    mean_factor = beta_rows * beta_rows * previous / ((1.0 - alpha_bar) * alpha_bar)
    plan_table = jnp.stack([jnp.sqrt(alpha_bar), jnp.sqrt(1.0 - alpha_bar), mean_factor, jnp.log(clipped), jnp.log(beta_rows)], 1)
    one_hot = (steps[:, None] == jnp.arange(TSTEPS)[None, :]).astype(jnp.float32)
    return jnp.dot(one_hot, plan_table, precision=HIGHEST_PRECISION)

def positions():
    quarter = D // 4
    omegas = 1.0 / 10000.0 ** (jnp.arange(quarter).astype(jnp.float32) / quarter)
    cells = jnp.arange(SEQ)
    column_angle = (cells % GRID).astype(jnp.float32)[:, None] * omegas[None, :]
    row_angle = (cells // GRID).astype(jnp.float32)[:, None] * omegas[None, :]
    return jnp.concatenate([jnp.sin(column_angle), jnp.cos(column_angle), jnp.sin(row_angle), jnp.cos(row_angle)], 1)

def frequencies(steps):
    half_count = FREQ // 2
    frequency = jnp.exp(-math.log(10000.0) * jnp.arange(half_count).astype(jnp.float32) / half_count)
    angles = steps.astype(jnp.float32)[:, None] * frequency[None, :]
    return jnp.concatenate([jnp.cos(angles), jnp.sin(angles)], 1)

def modulate(stream, shifts, scales):
    average = lax.optimization_barrier(jnp.mean(stream, -1, keepdims=True))
    centred = stream - average
    variance = lax.optimization_barrier(jnp.mean(centred * centred, -1, keepdims=True))
    return centred * lax.rsqrt(variance + 1e-06) * (1.0 + scales[:, None, :]) + shifts[:, None, :]

def loss_terms(prediction, target, sched):
    guessed = prediction[..., :PATCH]
    variance_raw = prediction[..., PATCH:]
    mean_factor = sched[:, 2][:, None, None]
    posterior_log = sched[:, 3][:, None, None]
    beta_log = sched[:, 4][:, None, None]
    blend = 0.5 * (variance_raw + 1.0)
    model_log = blend * beta_log + (1.0 - blend) * posterior_log
    errors = guessed - target
    bound_term = 0.5 * (-1.0 + model_log - posterior_log + jnp.exp(posterior_log - model_log) + mean_factor * errors * errors * jnp.exp(-model_log))
    return jnp.sum(errors * errors + bound_term / LOG_TWO)

def stem_split(stacked):
    pieces = []
    offset = 0
    for extent in [FREQ, D, CLASSES + 1, 2 * D, 1, 2, 6]:
        pieces.append(stacked[offset:offset + extent])
        offset = offset + extent
    return pieces

def block_split(block_rows):
    column_edges = [0, 3 * D, 4 * D, 4 * D + FF, 4 * D + 2 * FF, 4 * D + 2 * FF + PATCH, WB]
    return [block_rows[:, column_edges[index]:column_edges[index + 1]] for index in range(6)]

def layer_forward(stream, modulation, w_qkv, w_proj, w_up, w_down):
    images = stream.shape[0]
    shift_a, scale_a, gate_a, shift_b, scale_b, gate_b = jnp.split(modulation, 6, axis=1)
    normed = low(modulate(stream, shift_a, scale_a))
    triple = low(low_back(product('isd,de->ise', normed, w_qkv))).reshape(images, SEQ, 3, HEADS, HEAD_DIM)
    scores = low_back(product('iqhe,ikhe->ihqk', triple[:, :, 0], triple[:, :, 1]) * (1.0 / math.sqrt(HEAD_DIM)))
    weights = low(jax.nn.softmax(scores, axis=-1))
    mixed_heads = low(low_back(product('ihqk,ikhe->iqhe', weights, triple[:, :, 2]))).reshape(images, SEQ, D)
    branch = low_back(product('isd,od->iso', mixed_heads, w_proj))
    middle = stream + gate_a[:, None, :] * branch
    second = low(modulate(middle, shift_b, scale_b))
    inner_rows = low_back(product('isd,df->isf', second, w_up))
    active = low(jax.nn.gelu(inner_rows, approximate=True))
    branch = low_back(product('isf,of->iso', active, w_down))
    return middle + gate_b[:, None, :] * branch

def forward_group(block_master, stem_master, ada_w, latents, noise, steps, labels, dropped):
    w_qkv, w_proj, w_up, w_down, w_patch, w_head = block_split(low(block_master).reshape(D, WB))
    w_time, w_time2, w_table, w_final, b_patch, b_final, b_ada = stem_split(low(stem_master).reshape(SROWS, D))
    w_ada = low(ada_w)
    images = steps.shape[0]
    sched = plan(steps)
    clean_rows = latents.reshape(images, SEQ, PATCH)
    target = noise.reshape(images, SEQ, PATCH)
    noisy_rows = low(sched[:, 0][:, None, None] * clean_rows + sched[:, 1][:, None, None] * target)
    stream = low_back(product('isp,dp->isd', noisy_rows, w_patch)) + b_patch[0] + positions()[None]
    timing = low(frequencies(steps))
    before = low_back(product('if,fd->id', timing, w_time))
    time_hidden = low(jax.nn.silu(before))
    chosen = jnp.where(dropped == 1, CLASSES, labels)
    condition = low_back(product('ik,kd->id', time_hidden, w_time2)) + w_table[chosen]
    signal = low(jax.nn.silu(condition))
    modulation = low_back(low(product('id,de->ie', signal, w_ada) + b_ada.reshape(6 * D)))
    stream = layer_forward(stream, modulation, w_qkv, w_proj, w_up, w_down)
    final_mod = low_back(product('id,od->io', signal, w_final)) + b_final.reshape(2 * D)
    normed = low(modulate(stream, final_mod[:, :D], final_mod[:, D:]))
    prediction = low_back(product('isd,do->iso', normed, w_head))
    return loss_terms(prediction, target, sched)

def adam_update(weight, gradient, first, second):
    first_new = BETA_ONE * first + (1.0 - BETA_ONE) * gradient
    second_new = BETA_TWO * second + (1.0 - BETA_TWO) * gradient * gradient
    corrected = first_new / (1.0 - BETA_ONE ** STEP)
    spread = jnp.sqrt(second_new / (1.0 - BETA_TWO ** STEP))
    return (weight - LEARN_RATE * corrected / (spread + EPSILON), first_new, second_new)

def reference(latents, noise, timesteps, labels, dropped, block_master, block_m, block_v, stem_master, stem_m, stem_v, ada_w, ada_w_m, ada_w_v):
    groups = N_DP
    per_group = IMAGES // groups
    batches = (latents.reshape(groups, per_group * SEQ, PATCH), noise.reshape(groups, per_group * SEQ, PATCH), timesteps.reshape(groups, per_group), labels.reshape(groups, per_group), dropped.reshape(groups, per_group))
    masters = (block_master, stem_master, ada_w)

    def accumulate(state_pair, batch_data):
        value, pullback = jax.vjp(lambda *weights: forward_group(*weights, *batch_data), *masters)
        gradients = pullback(jnp.ones_like(value))
        return ((state_pair[0] + value, tuple((earlier + later for earlier, later in zip(state_pair[1], gradients)))), None)
    start_state = (jnp.zeros((), jnp.float32), tuple((jnp.zeros_like(weight) for weight in masters)))
    (total, gradients), unused = lax.scan(accumulate, start_state, batches)
    grad_norm = jnp.sqrt(jnp.sum(gradients[0] * gradients[0]) + jnp.sum(gradients[1] * gradients[1]) + jnp.sum(gradients[2] * gradients[2]))
    factor = THRESHOLD / jnp.maximum(grad_norm, THRESHOLD)
    block_new = adam_update(block_master, gradients[0] * factor, block_m, block_v)
    stem_new = adam_update(stem_master, gradients[1] * factor, stem_m, stem_v)
    ada_new = adam_update(ada_w, gradients[2] * factor, ada_w_m, ada_w_v)
    return (total, grad_norm, block_new[0], block_new[1], block_new[2], stem_new[0], stem_new[1], stem_new[2], ada_new[0], ada_new[1], ada_new[2])
```

```python
import functools
import math

import jax
import jax.numpy as jnp
from jax import lax
from jax.sharding import PartitionSpec as P

D = 1152
HEADS = 16
HEAD_DIM = 72
FF = 4608
CLASSES = 1000
PATCH = 16
GRID = 16
FREQ = 256
TSTEPS = 1000
STEP = 10
SEQ = 256
WB = 13872
SROWS = 4722


HIGHEST_PRECISION = lax.Precision.HIGHEST
AXES = ("dp", "mod")
LOG_TWO = math.log(2.0)
THRESHOLD = 1.0
LEARN_RATE = 0.05
BETA_ONE = 0.9
BETA_TWO = 0.999
EPSILON = 1e-08


def matmul(form, left, right):
    return jnp.einsum(form, left, right, preferred_element_type=jnp.float32)


def plan(steps):
    step_index = jnp.arange(TSTEPS).astype(jnp.float32)
    beta_rows = 0.0001 + (0.02 - 0.0001) * step_index / (TSTEPS - 1)
    alpha_bar = jnp.cumprod(1.0 - beta_rows)
    previous = jnp.concatenate([jnp.ones((1,), jnp.float32), alpha_bar[:-1]])
    posterior = beta_rows * (1.0 - previous) / (1.0 - alpha_bar)
    clipped = jnp.concatenate([posterior[1:2], posterior[1:]])
    mean_factor = beta_rows * beta_rows * previous / ((1.0 - alpha_bar) * alpha_bar)
    plan_table = jnp.stack(
        [
            jnp.sqrt(alpha_bar),
            jnp.sqrt(1.0 - alpha_bar),
            mean_factor,
            jnp.log(clipped),
            jnp.log(beta_rows),
        ],
        1,
    )
    one_hot = (steps[:, None] == jnp.arange(TSTEPS)[None, :]).astype(jnp.float32)
    return jnp.dot(one_hot, plan_table, precision=HIGHEST_PRECISION)


def positions():
    quarter = D // 4
    omegas = 1.0 / 10000.0 ** (jnp.arange(quarter).astype(jnp.float32) / quarter)
    cells = jnp.arange(SEQ)
    column_angle = (cells % GRID).astype(jnp.float32)[:, None] * omegas[None, :]
    row_angle = (cells // GRID).astype(jnp.float32)[:, None] * omegas[None, :]
    return jnp.concatenate(
        [jnp.sin(column_angle), jnp.cos(column_angle), jnp.sin(row_angle), jnp.cos(row_angle)], 1
    )


def frequencies(steps):
    half_count = FREQ // 2
    frequency = jnp.exp(
        -math.log(10000.0) * jnp.arange(half_count).astype(jnp.float32) / half_count
    )
    angles = steps.astype(jnp.float32)[:, None] * frequency[None, :]
    return jnp.concatenate([jnp.cos(angles), jnp.sin(angles)], 1)


def modulate(stream, shifts, scales):
    average = jnp.mean(stream, -1, keepdims=True)
    centred = stream - average
    variance = jnp.mean(centred * centred, -1, keepdims=True)
    return centred * lax.rsqrt(variance + 1e-06) * (1.0 + scales[:, None, :]) + shifts[:, None, :]


def modulate_back(stream, shifts, scales, cotangent):
    unused, pullback = jax.vjp(modulate, stream, shifts, scales)
    return pullback(cotangent)


def smooth_back(function, inputs, cotangent):
    unused, pullback = jax.vjp(function, inputs)
    return pullback(cotangent)[0]


def gelu_tanh(inputs):
    return jax.nn.gelu(inputs, approximate=True)


def loss_terms(prediction, target, sched):
    guessed = prediction[..., :PATCH]
    variance_raw = prediction[..., PATCH:]
    mean_factor = sched[:, 2][:, None, None]
    posterior_log = sched[:, 3][:, None, None]
    beta_log = sched[:, 4][:, None, None]
    blend = 0.5 * (variance_raw + 1.0)
    model_log = blend * beta_log + (1.0 - blend) * posterior_log
    errors = guessed - target
    bound_term = 0.5 * (
        -1.0
        + model_log
        - posterior_log
        + jnp.exp(posterior_log - model_log)
        + mean_factor * errors * errors * jnp.exp(-model_log)
    )
    return jnp.sum(errors * errors + bound_term / LOG_TWO)


class Links:
    def __init__(self, dp, mod):
        self.core = 2 if mod % 2 == 0 else 1
        self.y = mod // self.core
        self.x = self.y if dp % self.y == 0 else 1
        self.z = dp // self.x
        self.count = dp * mod
        self.size = {"z": self.z, "x": self.x, "y": self.y, "c": self.core}
        self.dim = {"z": 0, "x": 1, "y": 2}

    def place(self, axis):
        index = lax.axis_index(AXES)
        below = {"c": 1, "y": self.core, "x": self.core * self.y, "z": self.core * self.y * self.x}
        return index // below[axis] % self.size[axis]

    def send(self, block, axis, shift=1):
        pairs = []
        for index in range(self.count):
            spot = {
                "c": index % self.core,
                "y": index // self.core % self.y,
                "x": index // (self.core * self.y) % self.x,
                "z": index // (self.core * self.y * self.x),
            }
            spot[axis] = (spot[axis] + shift) % self.size[axis]
            target = ((spot["z"] * self.x + spot["x"]) * self.y + spot["y"]) * self.core + spot["c"]
            pairs.append((index, target))
        return lax.ppermute(block, AXES, pairs)

    def gather(self, block, axis):
        extent, dim = self.size[axis], self.dim[axis]
        if extent == 1:
            return block
        own = self.place(axis)
        pieces = [block] + [self.send(block, axis, shift) for shift in range(1, extent)]
        if extent == 2:
            return jnp.where(
                own == 0,
                jnp.concatenate(pieces, dim),
                jnp.concatenate(pieces[::-1], dim),
            )
        whole = jnp.concatenate(pieces, dim)
        for shift, piece in enumerate(pieces):
            whole = lax.dynamic_update_slice_in_dim(whole, piece, (own - shift) % extent, dim)
        return whole

    def reduce(self, block, axis, kind):
        extent, dim = self.size[axis], self.dim[axis]
        if extent == 1:
            return block
        own = self.place(axis)
        total = lax.dynamic_slice_in_dim(block, own, 1, dim)
        for shift in range(1, extent):
            part = lax.dynamic_slice_in_dim(block, (own + shift) % extent, 1, dim)
            total = total + self.send(part.astype(kind), axis, shift).astype(jnp.float32)
        return total

    def spread(self, block):
        copies = jnp.broadcast_to(block[None], (self.count, *block.shape))
        return lax.all_to_all(copies, AXES, split_axis=0, concat_axis=0, tiled=True)

    def deliver(self, blocks):
        return lax.all_to_all(blocks, AXES, split_axis=0, concat_axis=0, tiled=True)


def pick(own, first, second):
    return jnp.where(own == 0, first, second)


def joined(own, mine, other, dim):
    return pick(
        own, jnp.concatenate([mine, other], dim), jnp.concatenate([other, mine], dim)
    )


def column_half(rows, half):
    small = D // 2
    q_k_v_o = [rows[:, part * D + half * small : part * D + (half + 1) * small] for part in range(4)]
    up = rows[:, 4 * D + half * (FF // 2) : 4 * D + (half + 1) * (FF // 2)]
    down = rows[:, 4 * D + FF + half * (FF // 2) : 4 * D + FF + (half + 1) * (FF // 2)]
    return [
        jnp.concatenate(q_k_v_o[:2], 1),
        jnp.concatenate(q_k_v_o[2:], 1),
        up[:, :D],
        up[:, D:],
        down[:, :D],
        down[:, D:],
    ]


def whole_columns(first, second):
    small = D // 2
    pieces = [
        first[0][:, :small], second[0][:, :small],
        first[0][:, small:], second[0][:, small:],
        first[1][:, :small], second[1][:, :small],
        first[1][:, small:], second[1][:, small:],
        first[2], first[3], second[2], second[3],
        first[4], first[5], second[4], second[5],
    ]
    return jnp.concatenate(pieces, 1)


def chip_rows(links, flat):
    core = links.place("c")
    per_chip = D * links.core // links.count
    if (D % links.count) == 0:
        rows = flat.reshape(D // links.count, WB).astype(jnp.bfloat16)
        halves = [jnp.stack(column_half(rows, half)) for half in range(2)]
        small = rows[:, WB - PATCH - 2 * PATCH :]
        mine = pick(core, halves[0], halves[1])
        other = links.send(pick(core, halves[1], halves[0]), "c")
        both = joined(core, mine, other, 1)
        return both, joined(core, small, links.send(small, "c"), 0)
    low = flat.astype(jnp.bfloat16)
    rows = joined(core, low, links.send(low, "c"), 0).reshape(per_chip, WB)
    halves = [jnp.stack(column_half(rows, half)) for half in range(2)]
    return pick(core, halves[0], halves[1]), rows[:, WB - PATCH - 2 * PATCH :]


def gather_block(links, flat):
    chunks, small = chip_rows(links, flat)
    grid = lambda block: block[None, None, None]
    small = links.gather(links.gather(links.gather(grid(small), "z"), "x"), "y").reshape(D, -1)
    own = []
    for group in range(3):
        left, right = grid(chunks[2 * group]), grid(chunks[2 * group + 1])
        if group < 2:
            pair = links.gather(jnp.concatenate([left, right], 4), "z")
            left, right = pair[..., :D], pair[..., D:]
            left, right = links.gather(left, "x"), links.gather(right, "y")
        else:
            left, right = links.gather(left, "x"), links.gather(right, "y")
            left, right = links.gather(left, "z"), links.gather(right, "z")
        left, right = links.gather(left, "y"), links.gather(right, "x")
        own += [left.reshape(D, D), right.reshape(D, D)]
    other = [links.send(block, "c") for block in own]
    return own, other, small[:, :PATCH], small[:, PATCH:]


def reduce_pair(links, left, right, kind=jnp.bfloat16):
    per_chip = D * links.core // links.count
    shape = (links.z, links.x, links.y, per_chip)
    left, right = left.reshape(*shape, -1), right.reshape(*shape, -1)
    left, right = links.reduce(left, "y", kind), links.reduce(right, "x", kind)
    left, right = links.reduce(left, "x", kind), links.reduce(right, "y", kind)
    left, right = links.reduce(left, "z", kind), links.reduce(right, "z", kind)
    return left.reshape(per_chip, -1), right.reshape(per_chip, -1)


def flat_gradient(links, chunks, small):
    core = links.place("c")
    if (D % links.count) == 0:
        per_device = D // links.count
        stacked = jnp.stack(chunks)
        mine = lax.dynamic_slice_in_dim(stacked, core * per_device, per_device, 1)
        sent = lax.dynamic_slice_in_dim(stacked, (1 - core) * per_device, per_device, 1)
        other = links.send(sent, "c")
        rows = jnp.concatenate(
            [
                whole_columns(pick(core, mine, other), pick(core, other, mine)),
                lax.dynamic_slice_in_dim(small, core * per_device, per_device, 0),
            ],
            1,
        )
        return rows.reshape(per_device * WB)
    stacked = jnp.stack(chunks)
    other = links.send(stacked, "c")
    rows = jnp.concatenate(
        [whole_columns(pick(core, stacked, other), pick(core, other, stacked)), small], 1
    )
    flat = rows.reshape(-1)
    part = flat.shape[0] // 2
    return lax.dynamic_slice_in_dim(flat, core * part, part)


EXTENTS = [FREQ, D, CLASSES + 1, 2 * D, 1, 2, 6]
STARTS = [sum(EXTENTS[:index]) for index in range(len(EXTENTS) + 1)]


class Window:
    def __init__(self, links, length):
        self.length = length
        begins = [index * length for index in range(links.count)]
        rows = max((begin % D + length + D - 1) // D for begin in begins)
        self.rows = (rows + 15) // 16 * 16
        begin = lax.axis_index(AXES) * length
        self.first = begin // D
        self.offset = begin - self.first * D

    def fill(self, flat):
        padded = jnp.concatenate(
            [jnp.zeros((D,), flat.dtype), flat, jnp.zeros((self.rows * D,), flat.dtype)]
        )
        return lax.dynamic_slice_in_dim(padded, D - self.offset, self.rows * D).reshape(
            self.rows, D
        )

    def cut(self, columns, start):
        full = jnp.pad(columns, ((0, 0), (start, SROWS + self.rows - start - columns.shape[1])))
        return lax.dynamic_slice_in_dim(full, self.first, self.rows, 1)

    def put(self, columns, start, extent):
        full = jnp.zeros((columns.shape[0], SROWS + self.rows), columns.dtype)
        full = lax.dynamic_update_slice_in_dim(full, columns, self.first, 1)
        return full[:, start : start + extent]

    def flatten(self, rows):
        return lax.dynamic_slice_in_dim(rows.reshape(-1), self.offset, self.length)


def adam_update(weight, gradient, first, second):
    first_new = BETA_ONE * first + (1.0 - BETA_ONE) * gradient
    second_new = BETA_TWO * second + (1.0 - BETA_TWO) * gradient * gradient
    corrected = first_new / (1.0 - BETA_ONE**STEP)
    spread = jnp.sqrt(second_new / (1.0 - BETA_TWO**STEP))
    return (weight - LEARN_RATE * corrected / (spread + EPSILON), first_new, second_new)


def attend(normed, w_qk, w_v):
    images = normed.shape[0]
    heads = HEADS // 2
    low = jnp.bfloat16
    qk = matmul("isd,de->ise", normed, w_qk).astype(low).reshape(images, SEQ, 2, heads, HEAD_DIM)
    values = matmul("isd,de->ise", normed, w_v).astype(low).reshape(images, SEQ, heads, HEAD_DIM)
    queries, keys = qk[:, :, 0], qk[:, :, 1]
    scores = matmul("iqhe,ikhe->ihqk", queries, keys) * (1.0 / math.sqrt(HEAD_DIM))
    totals = jax.nn.logsumexp(scores, axis=-1)
    weights = jnp.exp(scores - totals[..., None]).astype(low)
    mixed = matmul("ihqk,ikhe->iqhe", weights, values).astype(low)
    return mixed.reshape(images, SEQ, D // 2), (queries, keys, values, totals)


def attend_back(kept, mixed_grad):
    queries, keys, values, totals = kept
    images = queries.shape[0]
    low = jnp.bfloat16
    mixed_grad = mixed_grad.astype(low).reshape(images, SEQ, HEADS // 2, HEAD_DIM)
    score_scale = 1.0 / math.sqrt(HEAD_DIM)
    softmax_rows = jnp.exp(
        matmul("iqhe,ikhe->ihqk", queries, keys) * score_scale - totals[..., None]
    )
    weight_grad = matmul("iqhe,ikhe->ihqk", mixed_grad, values)
    score_grad = (
        softmax_rows * (weight_grad - jnp.sum(weight_grad * softmax_rows, -1, keepdims=True))
    ).astype(low)
    query_grad = (matmul("ihqk,ikhe->iqhe", score_grad, keys) * score_scale).astype(low)
    key_grad = (matmul("ihqk,iqhe->ikhe", score_grad, queries) * score_scale).astype(low)
    value_grad = matmul("ihqk,iqhe->ikhe", softmax_rows.astype(low), mixed_grad).astype(low)
    return (
        jnp.stack([query_grad, key_grad], 2).reshape(images, SEQ, D),
        value_grad.reshape(images, SEQ, D // 2),
    )


def shards(
    links,
    latents,
    noise,
    timesteps,
    labels,
    dropped,
    block_master,
    block_m,
    block_v,
    stem_master,
    stem_m,
    stem_v,
    ada_w,
    ada_w_m,
    ada_w_v,
):
    low, wide = jnp.bfloat16, jnp.float32
    images = timesteps.shape[0]
    everyone = links.count * images
    own_cols = ada_w.shape[1]
    own_rows = ada_w.shape[0]
    row_at = lax.axis_index("dp") * own_rows
    col_at = lax.axis_index("mod") * own_cols
    groups = 6 * D // own_cols

    own, other, w_patch, w_head = gather_block(links, block_master)
    halves = (own, other)

    window = Window(links, stem_master.shape[0])
    stem = window.fill(stem_master.astype(low))
    ada_low = ada_w.astype(low)
    integers = links.spread(jnp.stack([timesteps, jnp.where(dropped == 1, CLASSES, labels)]))
    all_steps = integers[:, 0].reshape(everyone)
    chosen = integers[:, 1].reshape(everyone)
    timing = frequencies(all_steps).astype(low)
    one_hot = (chosen[:, None] == jnp.arange(CLASSES + 1)[None, :]).astype(low)
    bias_start, bias_extent = STARTS[4], 9
    bias_share = -(-bias_extent * D // links.count)
    mark = jnp.arange(bias_extent)[:, None] + bias_start == (
        window.first + jnp.arange(window.rows)
    )
    bias_part = matmul("br,rd->bd", mark.astype(low), stem).reshape(bias_extent * D)
    bias_part = jnp.pad(bias_part, (0, bias_share * links.count - bias_extent * D))

    before_part = matmul("ir,rd->id", window.cut(timing, STARTS[0]), stem)
    got = links.deliver(
        jnp.concatenate(
            [
                before_part.reshape(links.count, images * D),
                bias_part.reshape(links.count, bias_share),
            ],
            1,
        )
    ).sum(0)
    before = got[: images * D].reshape(images, D)
    time_hidden = jax.nn.silu(before).astype(low)
    got = links.spread(
        jnp.concatenate([time_hidden.reshape(images * D), got[images * D :].astype(low)])
    )
    all_hidden = got[:, : images * D].reshape(everyone, D)
    biases = got[:, images * D :].reshape(-1)[: bias_extent * D].reshape(bias_extent, D)
    biases = biases.astype(wide)
    left = window.cut(jnp.concatenate([all_hidden, one_hot], 1), STARTS[1])
    condition = links.deliver(
        matmul("ir,rd->id", left, stem).reshape(links.count, images, D)
    ).sum(0)
    signal = jax.nn.silu(condition).astype(low)
    all_signal = links.spread(signal).reshape(everyone, D)
    signal_rows = lax.dynamic_slice_in_dim(all_signal, row_at, own_rows, 1)
    parts = links.deliver(
        matmul("ir,rc->ic", signal_rows, ada_low).reshape(links.count, images, own_cols)
    )
    modulation = (
        parts.reshape(-1, groups, images, own_cols).sum(0).transpose(1, 0, 2).reshape(images, 6 * D)
        + biases[3:].reshape(6 * D)
    ).astype(low)
    pieces = jnp.split(modulation.astype(wide), 6, axis=1)
    final_part = window.put(matmul("id,rd->ir", all_signal, stem), STARTS[3], 2 * D)
    final_mod = links.deliver(final_part.reshape(links.count, images, 2 * D)).sum(0) + biases[
        1:3
    ].reshape(2 * D)
    final_shift, final_scale = final_mod[:, :D], final_mod[:, D:]

    sched = plan(timesteps)
    target = noise.reshape(images, SEQ, PATCH)
    noisy_rows = (
        sched[:, 0][:, None, None] * latents.reshape(images, SEQ, PATCH)
        + sched[:, 1][:, None, None] * target
    ).astype(low)
    stream = matmul("isp,dp->isd", noisy_rows, w_patch) + biases[0] + positions()[None]
    normed = modulate(stream, pieces[0], pieces[1]).astype(low)
    w_v = [half[1][:, : D // 2] for half in halves]
    w_proj = [half[1][:, D // 2 :] for half in halves]
    mixed, kept = [], []
    for half in range(2):
        rows, saved = attend(normed, halves[half][0], w_v[half])
        mixed.append(rows)
        kept.append(saved)
    attended = sum(matmul("isd,od->iso", mixed[half], w_proj[half]) for half in range(2))
    middle = stream + pieces[2][:, None, :] * attended
    second = modulate(middle, pieces[3], pieces[4]).astype(low)
    inner, active = [], []
    output = 0.0
    for half in range(2):
        for chunk in range(2):
            rows = matmul("isd,df->isf", second, halves[half][2 + chunk])
            inner.append(rows)
            active.append(gelu_tanh(rows).astype(low))
    for half in range(2):
        for chunk in range(2):
            output = output + matmul("isf,of->iso", active[2 * half + chunk], halves[half][4 + chunk])
    layer_out = middle + pieces[5][:, None, :] * output
    final_normed = modulate(layer_out, final_shift, final_scale).astype(low)
    prediction = matmul("isd,do->iso", final_normed, w_head)
    loss_local, loss_back = jax.vjp(
        lambda predicted: loss_terms(predicted, target, sched), prediction
    )

    def tokens(rows):
        return rows.reshape(images * SEQ, rows.shape[-1])

    def with_partner(mine, sent):
        return jnp.concatenate([tokens(mine), links.send(tokens(sent), "c")], 0)

    out_grad = loss_back(jnp.ones_like(loss_local))[0].astype(low)
    grad_head = matmul("iso,isd->do", out_grad, final_normed)
    upstream, shift_grad, scale_grad = modulate_back(
        layer_out, final_shift, final_scale, matmul("iso,do->isd", out_grad, w_head)
    )
    final_grad = jnp.concatenate([shift_grad, scale_grad], 1)
    down_in = (pieces[5][:, None, :] * upstream).astype(low)
    gate_b = jnp.sum(upstream * output, 1)
    down_both = with_partner(down_in, down_in)
    grad_down = [
        matmul("to,tf->of", down_both, with_partner(active[chunk], active[2 + chunk]))
        for chunk in range(2)
    ]
    reduced = [None] * 6
    reduced[4:] = reduce_pair(links, *grad_down)
    inner_grad = [
        smooth_back(
            gelu_tanh,
            inner[2 * half + chunk],
            matmul("iso,of->isf", down_in, halves[half][4 + chunk]),
        ).astype(low)
        for half in range(2)
        for chunk in range(2)
    ]
    second_both = with_partner(second, second)
    grad_up = [
        matmul("td,tf->df", second_both, with_partner(inner_grad[chunk], inner_grad[2 + chunk]))
        for chunk in range(2)
    ]
    reduced[2:4] = reduce_pair(links, *grad_up)
    second_grad = sum(
        matmul("isf,df->isd", inner_grad[2 * half + chunk], halves[half][2 + chunk])
        for half in range(2)
        for chunk in range(2)
    )
    back_mid, shift_b, scale_b = modulate_back(middle, pieces[3], pieces[4], second_grad)
    grad_mid = upstream + back_mid
    proj_in = (pieces[2][:, None, :] * grad_mid).astype(low)
    gate_a = jnp.sum(grad_mid * attended, 1)
    grad_proj = matmul("to,td->od", with_partner(proj_in, proj_in), with_partner(*mixed))
    qk_grad, v_grad = [], []
    for half in range(2):
        rows, more = attend_back(kept[half], matmul("iso,od->isd", proj_in, w_proj[half]))
        qk_grad.append(rows)
        v_grad.append(more)
    normed_both = with_partner(normed, normed)
    grad_qk = matmul("td,te->de", normed_both, with_partner(*qk_grad))
    grad_v = matmul("td,te->de", normed_both, with_partner(*v_grad))
    reduced[:2] = reduce_pair(links, grad_qk, jnp.concatenate([grad_v, grad_proj], 1))
    normed_grad = sum(
        matmul("ise,de->isd", qk_grad[half], halves[half][0])
        + matmul("ise,de->isd", v_grad[half], w_v[half])
        for half in range(2)
    )
    back_in, shift_a, scale_a = modulate_back(stream, pieces[0], pieces[1], normed_grad)
    stream_grad = grad_mid + back_in
    grad_patch = matmul("isp,isd->dp", noisy_rows, stream_grad.astype(low))
    small = jnp.concatenate([grad_patch, grad_head], 1)
    small = small + links.send(small, "c") if links.core == 2 else small
    small = small.reshape(links.z, links.x, links.y, -1, 3 * PATCH)
    for axis in "yxz":
        small = links.reduce(small, axis, wide)
    small = small.reshape(-1, 3 * PATCH)

    modulation_low = jnp.concatenate(
        [shift_a, scale_a, gate_a, shift_b, scale_b, gate_b], 1
    ).astype(low)
    final_low = final_grad.astype(low)
    sums = jnp.concatenate([jnp.sum(stream_grad, (0, 1)), jnp.sum(final_grad, 0)])
    all_sums = links.spread(sums).sum(0)
    all_final = links.spread(final_low).reshape(everyone, 2 * D)
    all_modulation = links.spread(modulation_low).reshape(everyone, 6 * D)
    own_modulation = lax.dynamic_slice_in_dim(all_modulation, col_at, own_cols, 1)
    ada_grad = matmul("ir,ic->rc", signal_rows, own_modulation)
    signal_part = matmul("ir,rd->id", window.cut(all_final, STARTS[3]), stem)
    ada_part = matmul("ic,rc->ir", own_modulation, ada_low)
    signal_part = lax.dynamic_update_slice_in_dim(
        signal_part,
        lax.dynamic_slice_in_dim(signal_part, row_at, own_rows, 1) + ada_part,
        row_at,
        1,
    )
    signal_grad = links.deliver(signal_part.reshape(links.count, images, D)).sum(0)
    condition_grad = smooth_back(jax.nn.silu, condition, signal_grad)
    all_condition = links.spread(condition_grad).reshape(everyone, D)
    condition_low = all_condition.astype(low)
    hidden_part = window.put(matmul("id,rd->ir", condition_low, stem), STARTS[1], D)
    hidden_grad = links.deliver(hidden_part.reshape(links.count, images, D)).sum(0)
    before_grad = smooth_back(jax.nn.silu, before, hidden_grad).astype(low)
    all_before = links.spread(before_grad).reshape(everyone, D)
    bias_rows = jnp.concatenate(
        [all_sums, jnp.sum(all_modulation.astype(wide), 0)]
    ).reshape(bias_extent, D)
    low_left = jnp.concatenate(
        [
            window.cut(timing, STARTS[0]),
            window.cut(all_hidden, STARTS[1]),
            window.cut(all_final, STARTS[3]),
        ],
        0,
    )
    low_right = jnp.concatenate([all_before, condition_low, all_signal], 0)
    stem_rows = matmul("ir,id->rd", low_left, low_right)
    wide_left = jnp.concatenate(
        [window.cut(one_hot.astype(wide), STARTS[2]), mark.astype(wide)], 0
    )
    wide_right = jnp.concatenate([all_condition, bias_rows], 0)
    stem_rows = stem_rows + jnp.dot(wide_left.T, wide_right, precision=HIGHEST_PRECISION)
    stem_grad = window.flatten(stem_rows)

    block_grad = flat_gradient(links, reduced, small)
    squares = (
        jnp.sum(block_grad * block_grad)
        + jnp.sum(stem_grad * stem_grad)
        + jnp.sum(ada_grad * ada_grad)
    )
    totals = links.spread(jnp.stack([loss_local, squares])).sum(0)
    loss_total = totals[0]
    grad_norm = jnp.sqrt(totals[1])
    factor = THRESHOLD / jnp.maximum(grad_norm, THRESHOLD)
    block_new = adam_update(block_master, block_grad * factor, block_m, block_v)
    stem_new = adam_update(stem_master, stem_grad * factor, stem_m, stem_v)
    ada_new = adam_update(ada_w, ada_grad * factor, ada_w_m, ada_w_v)
    return (loss_total, grad_norm, *block_new, *stem_new, *ada_new)


def solution(mesh):
    return jax.shard_map(
        functools.partial(shards, Links(mesh.shape["dp"], mesh.shape["mod"])),
        mesh=mesh,
        in_specs=(
            P(("dp", "mod"), None),
            P(("dp", "mod"), None),
            P(("dp", "mod")),
            P(("dp", "mod")),
            P(("dp", "mod")),
            P(("dp", "mod")),
            P(("dp", "mod")),
            P(("dp", "mod")),
            P(("dp", "mod")),
            P(("dp", "mod")),
            P(("dp", "mod")),
            P("dp", "mod"),
            P("dp", "mod"),
            P("dp", "mod"),
        ),
        out_specs=(
            P(),
            P(),
            P(("dp", "mod")),
            P(("dp", "mod")),
            P(("dp", "mod")),
            P(("dp", "mod")),
            P(("dp", "mod")),
            P(("dp", "mod")),
            P("dp", "mod"),
            P("dp", "mod"),
            P("dp", "mod"),
        ),
        check_vma=False,
    )
```

```python
import functools
import math

import jax
import jax.numpy as jnp
from jax import lax
from jax.sharding import PartitionSpec as P

D = 1152
HEADS = 16
HEAD_DIM = 72
FF = 4608
CLASSES = 1000
PATCH = 16
GRID = 16
FREQ = 256
TSTEPS = 1000
STEP = 10
SEQ = 256
WB = 13872
SMALL = 3 * PATCH
SROWS = 4722


HIGHEST_PRECISION = lax.Precision.HIGHEST
AXES = ("z", "x", "y", "c")
CORE_FIRST = ("c", "z", "x", "y")
LOG_TWO = math.log(2.0)
THRESHOLD = 1.0
LEARN_RATE = 0.05
BETA_ONE = 0.9
BETA_TWO = 0.999
EPSILON = 1e-08


def matmul(form, left, right):
    return jnp.einsum(form, left, right, preferred_element_type=jnp.float32)


def plan(steps):
    step_index = jnp.arange(TSTEPS).astype(jnp.float32)
    beta_rows = 0.0001 + (0.02 - 0.0001) * step_index / (TSTEPS - 1)
    alpha_bar = jnp.cumprod(1.0 - beta_rows)
    previous = jnp.concatenate([jnp.ones((1,), jnp.float32), alpha_bar[:-1]])
    posterior = beta_rows * (1.0 - previous) / (1.0 - alpha_bar)
    clipped = jnp.concatenate([posterior[1:2], posterior[1:]])
    mean_factor = beta_rows * beta_rows * previous / ((1.0 - alpha_bar) * alpha_bar)
    plan_table = jnp.stack(
        [
            jnp.sqrt(alpha_bar),
            jnp.sqrt(1.0 - alpha_bar),
            mean_factor,
            jnp.log(clipped),
            jnp.log(beta_rows),
        ],
        1,
    )
    one_hot = (steps[:, None] == jnp.arange(TSTEPS)[None, :]).astype(jnp.float32)
    return jnp.dot(one_hot, plan_table, precision=HIGHEST_PRECISION)


def positions():
    quarter = D // 4
    omegas = 1.0 / 10000.0 ** (jnp.arange(quarter).astype(jnp.float32) / quarter)
    cells = jnp.arange(SEQ)
    column_angle = (cells % GRID).astype(jnp.float32)[:, None] * omegas[None, :]
    row_angle = (cells // GRID).astype(jnp.float32)[:, None] * omegas[None, :]
    return jnp.concatenate(
        [jnp.sin(column_angle), jnp.cos(column_angle), jnp.sin(row_angle), jnp.cos(row_angle)], 1
    )


def frequencies(steps):
    half_count = FREQ // 2
    frequency = jnp.exp(
        -math.log(10000.0) * jnp.arange(half_count).astype(jnp.float32) / half_count
    )
    angles = steps.astype(jnp.float32)[:, None] * frequency[None, :]
    return jnp.concatenate([jnp.cos(angles), jnp.sin(angles)], 1)


def modulate(stream, shifts, scales):
    average = jnp.mean(stream, -1, keepdims=True)
    centred = stream - average
    variance = jnp.mean(centred * centred, -1, keepdims=True)
    return centred * lax.rsqrt(variance + 1e-06) * (1.0 + scales[:, None, :]) + shifts[:, None, :]


def modulate_back(stream, shifts, scales, cotangent):
    unused, pullback = jax.vjp(modulate, stream, shifts, scales)
    return pullback(cotangent)


def smooth_back(function, inputs, cotangent):
    unused, pullback = jax.vjp(function, inputs)
    return pullback(cotangent)[0]


def gelu_tanh(inputs):
    return jax.nn.gelu(inputs, approximate=True)


def loss_terms(prediction, target, sched):
    guessed = prediction[..., :PATCH]
    variance_raw = prediction[..., PATCH:]
    mean_factor = sched[:, 2][:, None, None]
    posterior_log = sched[:, 3][:, None, None]
    beta_log = sched[:, 4][:, None, None]
    blend = 0.5 * (variance_raw + 1.0)
    model_log = blend * beta_log + (1.0 - blend) * posterior_log
    errors = guessed - target
    bound_term = 0.5 * (
        -1.0
        + model_log
        - posterior_log
        + jnp.exp(posterior_log - model_log)
        + mean_factor * errors * errors * jnp.exp(-model_log)
    )
    return jnp.sum(errors * errors + bound_term / LOG_TWO)


class Links:
    def __init__(self, dp, mod):
        self.core = 2 if mod % 2 == 0 else 1
        self.y = mod // self.core
        self.x = self.y if dp % self.y == 0 else 1
        self.z = dp // self.x
        self.count = dp * mod
        self.size = {"z": self.z, "x": self.x, "y": self.y, "c": self.core}
        self.dim = {"z": 0, "x": 1, "y": 2}

    def place(self, axis):
        index = lax.axis_index(AXES)
        below = {"c": 1, "y": self.core, "x": self.core * self.y, "z": self.core * self.y * self.x}
        return index // below[axis] % self.size[axis]

    def send(self, block, axis, shift=1):
        pairs = []
        for index in range(self.count):
            spot = {
                "c": index % self.core,
                "y": index // self.core % self.y,
                "x": index // (self.core * self.y) % self.x,
                "z": index // (self.core * self.y * self.x),
            }
            spot[axis] = (spot[axis] + shift) % self.size[axis]
            target = ((spot["z"] * self.x + spot["x"]) * self.y + spot["y"]) * self.core + spot["c"]
            pairs.append((index, target))
        return lax.ppermute(block, AXES, pairs)

    def spread(self, block):
        copies = jnp.broadcast_to(block[None], (self.count, *block.shape))
        return lax.all_to_all(copies, AXES, split_axis=0, concat_axis=0, tiled=True)

    def deliver(self, blocks):
        return lax.all_to_all(blocks, AXES, split_axis=0, concat_axis=0, tiled=True)


def pick(own, first, second):
    return jnp.where(own == 0, first, second)


def joined(own, mine, other, dim):
    return pick(
        own, jnp.concatenate([mine, other], dim), jnp.concatenate([other, mine], dim)
    )


def column_half(rows, half):
    small = D // 2
    attention = [rows[:, part * D + half * small : part * D + (half + 1) * small] for part in range(4)]
    wide = FF // 2
    return [
        jnp.concatenate(attention, 1),
        rows[:, 4 * D + half * wide : 4 * D + (half + 1) * wide],
        rows[:, 4 * D + FF + half * wide : 4 * D + FF + (half + 1) * wide],
    ]


def whole_columns(first, second):
    small = D // 2
    pieces = [
        half[0][:, part * small : (part + 1) * small] for part in range(4) for half in (first, second)
    ]
    return jnp.concatenate([*pieces, first[1], second[1], first[2], second[2]], 1)


def chip_rows(links, flat):
    core = links.place("c")
    per_chip = D * links.core // links.count
    if (D % links.count) == 0:
        rows = flat.reshape(D // links.count, WB).astype(jnp.bfloat16)
        halves = [jnp.concatenate(column_half(rows, half), 1) for half in range(2)]
        mine = pick(core, halves[0], halves[1])
        other = links.send(pick(core, halves[1], halves[0]), "c")
        return joined(core, mine, other, 0), rows[:, WB - SMALL :].reshape(-1)
    low = flat.astype(jnp.bfloat16)
    rows = joined(core, low, links.send(low, "c"), 0).reshape(per_chip, WB)
    halves = [jnp.concatenate(column_half(rows, half), 1) for half in range(2)]
    small = rows[:, WB - SMALL :].reshape(2, -1)
    return pick(core, halves[0], halves[1]), pick(core, small[0], small[1])


def gather_halves(chunk):
    whole = lax.all_gather(chunk, CORE_FIRST, axis=0, tiled=True)
    return whole[:D], whole[D:]


class Reduction:
    def __init__(self, links, gradients, kind=jnp.bfloat16):
        self.links, self.kind = links, kind
        shape = (links.z, links.x, links.y, D * links.core // links.count)
        self.blocks = [rows.reshape(*shape, -1) for rows in gradients]
        total = sum(rows.shape[1] for rows in gradients)
        middle = total // 256 * 128
        self.spans = [[], []]
        for index, rows in enumerate(gradients):
            before = sum(earlier.shape[1] for earlier in gradients[:index])
            edge = min(max(middle - before, 0), rows.shape[1])
            if edge > 0:
                self.spans[0].append((index, 0, edge))
            if edge < rows.shape[1]:
                self.spans[1].append((index, edge, rows.shape[1]))

    def cut(self, sources, axis, spot):
        dim = self.links.dim[axis]
        parts = [
            lax.dynamic_slice_in_dim(self.blocks[index][..., low:high], spot, 1, dim)
            for index, low, high in sources
        ]
        return jnp.concatenate(parts, 4) if len(parts) > 1 else parts[0]

    def send(self, order):
        self.order = order
        self.got = []
        for sources, axis in zip(self.spans, order):
            extent, own = self.links.size[axis], self.links.place(axis)
            for shift in range(1, extent):
                part = self.cut(sources, axis, (own + shift) % extent).astype(self.kind)
                self.got.append(self.links.send(part, axis, shift))
        return self.got

    def add(self, got):
        got = list(got)
        blocks, spans = [], []
        for sources, axis in zip(self.spans, self.order):
            extent, own = self.links.size[axis], self.links.place(axis)
            total = self.cut(sources, axis, own).astype(jnp.float32)
            for _ in range(1, extent):
                total = total + got.pop(0).astype(jnp.float32)
            spans.append([(len(blocks), 0, total.shape[-1])])
            blocks.append(total)
        self.blocks, self.spans = blocks, spans

    def join(self):
        self.spans = [[span for sources in self.spans for span in sources]]

    def result(self):
        return self.blocks[0].reshape(-1, self.blocks[0].shape[-1])


def flat_gradient(links, joint, small):
    core = links.place("c")
    edges = [0, 2 * D, 4 * D, 6 * D]
    split = lambda rows: [rows[:, edges[part] : edges[part + 1]] for part in range(3)]
    per_device = D // links.count
    if (D % links.count) == 0:
        mine = lax.dynamic_slice_in_dim(joint, core * per_device, per_device, 0)
        sent = lax.dynamic_slice_in_dim(joint, (1 - core) * per_device, per_device, 0)
    else:
        mine, sent = joint, joint
        small = joined(core, small, links.send(small, "c"), 0)
    other = links.send(sent, "c")
    columns = whole_columns(split(pick(core, mine, other)), split(pick(core, other, mine)))
    flat = jnp.concatenate([columns, small.reshape(-1, SMALL)], 1).reshape(-1)
    if (D % links.count) == 0:
        return flat
    part = flat.shape[0] // 2
    return lax.dynamic_slice_in_dim(flat, core * part, part)


EXTENTS = [FREQ, D, CLASSES + 1, 2 * D, 1, 2, 6]
STARTS = [sum(EXTENTS[:index]) for index in range(len(EXTENTS) + 1)]


class Window:
    def __init__(self, links, length):
        self.length = length
        begins = [index * length for index in range(links.count)]
        rows = max((begin % D + length + D - 1) // D for begin in begins)
        self.rows = (rows + 15) // 16 * 16
        begin = lax.axis_index(AXES) * length
        self.first = begin // D
        self.firsts = [start // D for start in begins]
        self.offset = begin - self.first * D

    def fill(self, flat):
        padded = jnp.concatenate(
            [jnp.zeros((D,), flat.dtype), flat, jnp.zeros((self.rows * D,), flat.dtype)]
        )
        return lax.dynamic_slice_in_dim(padded, D - self.offset, self.rows * D).reshape(
            self.rows, D
        )

    def cut(self, columns, start):
        full = jnp.pad(columns, ((0, 0), (start, SROWS + self.rows - start - columns.shape[1])))
        return lax.dynamic_slice_in_dim(full, self.first, self.rows, 1)

    def put(self, columns, start, extent):
        full = jnp.zeros((columns.shape[0], SROWS + self.rows), columns.dtype)
        full = lax.dynamic_update_slice_in_dim(full, columns, self.first, 1)
        return full[:, start : start + extent]

    def assemble(self, windows, start, extent):
        inside = [
            index
            for index, first in enumerate(self.firsts)
            if first < start + extent and first + self.rows > start
        ]
        low, high = inside[0], inside[-1] + 1
        firsts = jnp.array(self.firsts[low:high])
        rows = firsts[:, None] + jnp.arange(self.rows)[None, :]
        chosen = jnp.arange(extent)[:, None, None] + start == rows[None]
        return matmul("kir,dkr->id", windows[low:high], chosen.astype(windows.dtype))

    def flatten(self, rows):
        return lax.dynamic_slice_in_dim(rows.reshape(-1), self.offset, self.length)


def adam_update(weight, gradient, first, second):
    first_new = BETA_ONE * first + (1.0 - BETA_ONE) * gradient
    second_new = BETA_TWO * second + (1.0 - BETA_TWO) * gradient * gradient
    corrected = first_new / (1.0 - BETA_ONE**STEP)
    spread = jnp.sqrt(second_new / (1.0 - BETA_TWO**STEP))
    return (weight - LEARN_RATE * corrected / (spread + EPSILON), first_new, second_new)


def attend(normed, w_qkv):
    images = normed.shape[0]
    heads = HEADS // 2
    low = jnp.bfloat16
    triple = matmul("isd,de->ise", normed, w_qkv).astype(low)
    triple = triple.reshape(images, SEQ, 3, heads, HEAD_DIM)
    queries, keys, values = triple[:, :, 0], triple[:, :, 1], triple[:, :, 2]
    scores = matmul("iqhe,ikhe->ihqk", queries, keys) * (1.0 / math.sqrt(HEAD_DIM))
    totals = jax.nn.logsumexp(scores, axis=-1)
    weights = jnp.exp(scores - totals[..., None]).astype(low)
    mixed = matmul("ihqk,ikhe->iqhe", weights, values).astype(low)
    return mixed.reshape(images, SEQ, D // 2), (queries, keys, values, totals)


def attend_back(kept, mixed_grad):
    queries, keys, values, totals = kept
    images = queries.shape[0]
    low = jnp.bfloat16
    mixed_grad = mixed_grad.astype(low).reshape(images, SEQ, HEADS // 2, HEAD_DIM)
    score_scale = 1.0 / math.sqrt(HEAD_DIM)
    softmax_rows = jnp.exp(
        matmul("iqhe,ikhe->ihqk", queries, keys) * score_scale - totals[..., None]
    )
    weight_grad = matmul("iqhe,ikhe->ihqk", mixed_grad, values)
    score_grad = (
        softmax_rows * (weight_grad - jnp.sum(weight_grad * softmax_rows, -1, keepdims=True))
    ).astype(low)
    query_grad = (matmul("ihqk,ikhe->iqhe", score_grad, keys) * score_scale).astype(low)
    key_grad = (matmul("ihqk,iqhe->ikhe", score_grad, queries) * score_scale).astype(low)
    value_grad = matmul("ihqk,iqhe->ikhe", softmax_rows.astype(low), mixed_grad).astype(low)
    return jnp.stack([query_grad, key_grad, value_grad], 2).reshape(images, SEQ, 3 * D // 2)


def shards(
    links,
    latents,
    noise,
    timesteps,
    labels,
    dropped,
    block_master,
    block_m,
    block_v,
    stem_master,
    stem_m,
    stem_v,
    ada_w,
    ada_w_m,
    ada_w_v,
):
    low, wide = jnp.bfloat16, jnp.float32
    images = timesteps.shape[0]
    everyone = links.count * images
    own_cols = ada_w.shape[1]
    own_rows = ada_w.shape[0]
    row_at = lax.axis_index(("z", "x")) * own_rows
    col_at = lax.axis_index(("y", "c")) * own_cols
    groups = 6 * D // own_cols

    core = links.place("c")
    chunks, small = chip_rows(links, block_master)
    w_attention = gather_halves(chunks[:, : 2 * D])
    w_mlp = gather_halves(chunks[:, 2 * D :])
    w_qkv = [half[:, : 3 * D // 2] for half in w_attention]
    w_proj = [half[:, 3 * D // 2 :] for half in w_attention]
    w_up = [half[:, : 2 * D] for half in w_mlp]
    w_down = [half[:, 2 * D :] for half in w_mlp]

    window = Window(links, stem_master.shape[0])
    stem = window.fill(stem_master.astype(low))
    ada_low = ada_w.astype(low)
    integers = jnp.stack([timesteps, jnp.where(dropped == 1, CLASSES, labels)])
    digits = jnp.stack([integers // 32, integers % 32]).astype(low).reshape(-1)
    got = links.spread(jnp.concatenate([digits, small]))
    digits = got[:, : 4 * images].astype(jnp.int32).reshape(links.count, 2, 2, images)
    integers = digits[:, 0] * 32 + digits[:, 1]
    small = got[:, 4 * images :].reshape(D, SMALL)
    w_patch, w_head = small[:, :PATCH], small[:, PATCH:]
    all_steps = integers[:, 0].reshape(everyone)
    chosen = integers[:, 1].reshape(everyone)
    timing = frequencies(all_steps).astype(low)
    one_hot = (chosen[:, None] == jnp.arange(CLASSES + 1)[None, :]).astype(low)
    bias_start, bias_extent = STARTS[4], 9
    bias_share = -(-bias_extent * D // links.count)
    mark = jnp.arange(bias_extent)[:, None] + bias_start == (
        window.first + jnp.arange(window.rows)
    )
    bias_part = matmul("br,rd->bd", mark.astype(low), stem).reshape(bias_extent * D)
    bias_part = jnp.pad(bias_part, (0, bias_share * links.count - bias_extent * D))

    before_part = matmul("ir,rd->id", window.cut(timing, STARTS[0]), stem)
    got = links.deliver(
        jnp.concatenate(
            [
                before_part.reshape(links.count, images * D),
                bias_part.reshape(links.count, bias_share),
            ],
            1,
        )
    ).sum(0)
    got = links.spread(got)
    all_before = got[:, : images * D].reshape(everyone, D)
    all_hidden = jax.nn.silu(all_before).astype(low)
    biases = got[:, images * D :].reshape(-1)[: bias_extent * D].reshape(bias_extent, D)
    left = window.cut(jnp.concatenate([all_hidden, one_hot], 1), STARTS[1])
    condition = links.deliver(
        matmul("ir,rd->id", left, stem).reshape(links.count, images, D)
    ).sum(0)
    signal = jax.nn.silu(condition).astype(low)
    all_signal = links.spread(signal).reshape(everyone, D)
    signal_rows = lax.dynamic_slice_in_dim(all_signal, row_at, own_rows, 1)
    parts = links.deliver(
        matmul("ir,rc->ic", signal_rows, ada_low).reshape(links.count, images, own_cols)
    )
    modulation = (
        parts.reshape(-1, groups, images, own_cols).sum(0).transpose(1, 0, 2).reshape(images, 6 * D)
        + biases[3:].reshape(6 * D)
    ).astype(low)
    pieces = jnp.split(modulation.astype(wide), 6, axis=1)
    final_part = window.put(matmul("id,rd->ir", all_signal, stem), STARTS[3], 2 * D)
    final_mod = links.deliver(final_part.reshape(links.count, images, 2 * D)).sum(0) + biases[
        1:3
    ].reshape(2 * D)
    final_shift, final_scale = final_mod[:, :D], final_mod[:, D:]

    sched = plan(timesteps)
    target = noise.reshape(images, SEQ, PATCH)
    noisy_rows = (
        sched[:, 0][:, None, None] * latents.reshape(images, SEQ, PATCH)
        + sched[:, 1][:, None, None] * target
    ).astype(low)
    stream = matmul("isp,dp->isd", noisy_rows, w_patch) + biases[0] + positions()[None]
    normed = modulate(stream, pieces[0], pieces[1]).astype(low)
    mixed, kept = [], []
    for half in range(2):
        rows, saved = attend(normed, w_qkv[half])
        mixed.append(rows)
        kept.append(saved)
    attended = sum(matmul("isd,od->iso", mixed[half], w_proj[half]) for half in range(2))
    middle = stream + pieces[2][:, None, :] * attended
    second = modulate(middle, pieces[3], pieces[4]).astype(low)
    inner = [matmul("isd,df->isf", second, w_up[half]) for half in range(2)]
    active = [gelu_tanh(rows).astype(low) for rows in inner]
    output = sum(matmul("isf,of->iso", active[half], w_down[half]) for half in range(2))
    layer_out = middle + pieces[5][:, None, :] * output
    final_normed = modulate(layer_out, final_shift, final_scale).astype(low)
    prediction = matmul("isd,do->iso", final_normed, w_head)
    loss_local, loss_back = jax.vjp(
        lambda predicted: loss_terms(predicted, target, sched), prediction
    )

    def tokens(rows):
        return rows.reshape(images * SEQ, rows.shape[-1])

    def with_partner(first, second=None):
        if second is None:
            mine, sent = tokens(first), tokens(first)
        else:
            first, second = tokens(first), tokens(second)
            mine, sent = pick(core, first, second), pick(core, second, first)
        return jnp.concatenate([mine, links.send(sent, "c")], 0)

    def together(*values):
        return lax.optimization_barrier(values)

    out_grad = loss_back(jnp.ones_like(loss_local))[0].astype(low)
    grad_head = matmul("iso,isd->do", out_grad, final_normed)
    upstream, shift_grad, scale_grad = modulate_back(
        layer_out, final_shift, final_scale, matmul("iso,do->isd", out_grad, w_head)
    )
    final_grad = jnp.concatenate([shift_grad, scale_grad], 1)
    down_in = (pieces[5][:, None, :] * upstream).astype(low)
    gate_b = jnp.sum(upstream * output, 1)
    active_both = with_partner(*active)
    second_both = with_partner(second)
    mixed_both = with_partner(*mixed)
    normed_both = with_partner(normed)
    down_both = with_partner(down_in)
    inner_grad = [
        smooth_back(
            gelu_tanh, inner[half], matmul("iso,of->isf", down_in, w_down[half])
        ).astype(low)
        for half in range(2)
    ]
    inner_grad, down_both, active_both = together(inner_grad, down_both, active_both)
    grad_down = matmul("to,tf->of", down_both, active_both).astype(low)
    inner_grad, grad_down = together(inner_grad, grad_down)
    reduced_down = lax.psum_scatter(
        grad_down, ("z", "x", "y"), scatter_dimension=0, tiled=True
    ).astype(wide)
    inner_both = with_partner(*inner_grad)
    second_grad = sum(
        matmul("isf,df->isd", inner_grad[half], w_up[half]) for half in range(2)
    )
    back_mid, shift_b, scale_b = modulate_back(middle, pieces[3], pieces[4], second_grad)
    grad_mid = upstream + back_mid
    proj_in = (pieces[2][:, None, :] * grad_mid).astype(low)
    gate_a = jnp.sum(grad_mid * attended, 1)
    proj_both = with_partner(proj_in)
    final_low = final_grad.astype(low)
    early = jnp.concatenate([gate_a, shift_b, scale_b, gate_b], 1).astype(low)
    early = links.spread(jnp.concatenate([early, final_low], 1)).reshape(everyone, 6 * D)
    proj_in, inner_both, proj_both = together(proj_in, inner_both, proj_both)
    grad_up = matmul("td,tf->df", second_both, inner_both)
    grad_proj = matmul("to,td->od", proj_both, mixed_both)
    proj_in, grad_up, grad_proj = together(proj_in, grad_up, grad_proj)
    first = Reduction(links, [grad_up, grad_proj])
    got = first.send("yx")
    qkv_grad = [
        attend_back(kept[half], matmul("iso,od->isd", proj_in, w_proj[half])) for half in range(2)
    ]
    qkv_grad, got = together(qkv_grad, got)
    first.add(got)
    got = first.send("xy")
    qkv_both = with_partner(*qkv_grad)
    normed_grad = sum(matmul("ise,de->isd", qkv_grad[half], w_qkv[half]) for half in range(2))
    back_in, shift_a, scale_a = modulate_back(stream, pieces[0], pieces[1], normed_grad)
    stream_grad = grad_mid + back_in
    late = jnp.concatenate([shift_a, scale_a], 1).astype(low)
    late, stream_grad, got, qkv_both = together(late, stream_grad, got, qkv_both)
    late = links.spread(late).reshape(everyone, 2 * D)
    first.add(got)
    first.join()
    got = first.send("z")
    grad_qkv = matmul("td,te->de", normed_both, qkv_both)
    grad_patch = matmul("isp,isd->dp", noisy_rows, stream_grad.astype(low))
    small_grad = jnp.concatenate([grad_patch, grad_head], 1).reshape(links.count, -1)
    grad_qkv, late = together(grad_qkv, late)
    second = Reduction(links, [grad_qkv])
    more = second.send("yx")

    all_final = early[:, 4 * D :]
    all_modulation = jnp.concatenate([late, early[:, : 4 * D]], 1)
    own_modulation = lax.dynamic_slice_in_dim(all_modulation, col_at, own_cols, 1)
    signal_part = matmul("ir,rd->id", window.cut(all_final, STARTS[3]), stem)
    ada_part = matmul("ic,rc->ir", own_modulation, ada_low)
    signal_part = lax.dynamic_update_slice_in_dim(
        signal_part,
        lax.dynamic_slice_in_dim(signal_part, row_at, own_rows, 1) + ada_part,
        row_at,
        1,
    )
    sums = jnp.concatenate([jnp.sum(stream_grad, (0, 1)), jnp.sum(final_grad, 0)])
    share = -(-sums.shape[0] // links.count)
    sums = jnp.pad(sums, (0, share * links.count - sums.shape[0])).reshape(links.count, share)
    summed = links.deliver(
        jnp.concatenate([signal_part.reshape(links.count, images * D), sums, small_grad], 1)
    ).sum(0)
    small = summed[images * D + share :]
    condition_grad = smooth_back(jax.nn.silu, condition, summed[: images * D].reshape(images, D))
    spreading = jnp.concatenate([condition_grad.reshape(-1), summed[images * D : images * D + share]])
    spreading, got, more = together(spreading, got, more)
    first.add(got)
    second.add(more)
    more = second.send("xy")
    spread = links.spread(spreading)
    all_condition = spread[:, : images * D].reshape(everyone, D)
    all_sums = spread[:, images * D :].reshape(-1)[: 3 * D]
    condition_low = all_condition.astype(low)
    hidden_part = matmul("id,rd->ir", condition_low, stem)
    before_part = window.cut(all_before, STARTS[1])
    before_part = smooth_back(jax.nn.silu, before_part, hidden_part)
    row = window.first + jnp.arange(window.rows)
    before_part = jnp.where((row >= STARTS[1]) & (row < STARTS[2]), before_part, 0.0).astype(low)
    before_part, more = together(before_part, more)
    second.add(more)
    second.join()
    more = second.send("z")
    before_low = window.assemble(links.spread(before_part), STARTS[1], D).astype(low)
    second.add(more)
    reduced_rest = first.result()
    joint = jnp.concatenate(
        [second.result(), reduced_rest[:, 2 * D :], reduced_rest[:, : 2 * D], reduced_down], 1
    )
    block_grad = flat_gradient(links, joint, small)
    totals = links.spread(jnp.stack([loss_local, jnp.sum(block_grad * block_grad)])).sum(0)
    loss_total, squares = totals[0], totals[1]
    bias_rows = jnp.concatenate(
        [all_sums, jnp.sum(all_modulation.astype(wide), 0)]
    ).reshape(bias_extent, D)

    def product_squares(left, right):
        left, right = left.astype(wide), right.astype(wide)
        grams = [jnp.dot(rows, rows.T, precision=HIGHEST_PRECISION) for rows in (left, right)]
        return jnp.sum(grams[0] * grams[1])

    squares = (
        squares
        + product_squares(all_signal, all_modulation)
        + product_squares(all_signal, all_final)
        + product_squares(one_hot, all_condition)
        + product_squares(all_hidden, condition_low)
        + product_squares(timing, before_low)
        + jnp.sum(bias_rows * bias_rows)
    )
    ada_grad = matmul("ir,ic->rc", signal_rows, own_modulation)
    low_left = jnp.concatenate(
        [
            window.cut(timing, STARTS[0]),
            window.cut(all_hidden, STARTS[1]),
            window.cut(all_final, STARTS[3]),
        ],
        0,
    )
    low_right = jnp.concatenate([before_low, condition_low, all_signal], 0)
    stem_rows = matmul("ir,id->rd", low_left, low_right)
    wide_left = jnp.concatenate(
        [window.cut(one_hot.astype(wide), STARTS[2]), mark.astype(wide)], 0
    )
    wide_right = jnp.concatenate([all_condition, bias_rows], 0)
    stem_rows = stem_rows + jnp.dot(wide_left.T, wide_right, precision=HIGHEST_PRECISION)
    stem_grad = window.flatten(stem_rows)
    grad_norm = jnp.sqrt(squares)
    factor = THRESHOLD / jnp.maximum(grad_norm, THRESHOLD)
    block_new = adam_update(block_master, block_grad * factor, block_m, block_v)
    stem_new = adam_update(stem_master, stem_grad * factor, stem_m, stem_v)
    ada_new = adam_update(ada_w, ada_grad * factor, ada_w_m, ada_w_v)
    return (loss_total, grad_norm, *block_new, *stem_new, *ada_new)


def solution(mesh):
    links = Links(mesh.shape["dp"], mesh.shape["mod"])
    grid = jax.sharding.Mesh(
        mesh.devices.reshape(links.z, links.x, links.y, links.core), AXES
    )
    flat, rows, ada = P(AXES), P(AXES, None), P(("z", "x"), ("y", "c"))
    return jax.shard_map(
        functools.partial(shards, links),
        mesh=grid,
        in_specs=(rows, rows) + (flat,) * 9 + (ada,) * 3,
        out_specs=(P(), P()) + (flat,) * 6 + (ada,) * 3,
        check_vma=False,
    )
```

```python
import functools
import math

import jax
import jax.numpy as jnp
from jax import lax
from jax.sharding import PartitionSpec as P

D = 1152
HEADS = 16
HEAD_DIM = 72
FF = 4608
CLASSES = 1000
PATCH = 16
GRID = 16
FREQ = 256
TSTEPS = 1000
STEP = 10
SEQ = 256
WB = 13872
SMALL = 3 * PATCH
SROWS = 4722


HIGHEST_PRECISION = lax.Precision.HIGHEST
AXES = ("z", "x", "y", "c")
LOG_TWO = math.log(2.0)
THRESHOLD = 1.0
LEARN_RATE = 0.05
BETA_ONE = 0.9
BETA_TWO = 0.999
EPSILON = 1e-08


def matmul(form, left, right):
    return jnp.einsum(form, left, right, preferred_element_type=jnp.float32)


def plan(steps):
    step_index = jnp.arange(TSTEPS).astype(jnp.float32)
    beta_rows = 0.0001 + (0.02 - 0.0001) * step_index / (TSTEPS - 1)
    alpha_bar = jnp.cumprod(1.0 - beta_rows)
    previous = jnp.concatenate([jnp.ones((1,), jnp.float32), alpha_bar[:-1]])
    posterior = beta_rows * (1.0 - previous) / (1.0 - alpha_bar)
    clipped = jnp.concatenate([posterior[1:2], posterior[1:]])
    mean_factor = beta_rows * beta_rows * previous / ((1.0 - alpha_bar) * alpha_bar)
    plan_table = jnp.stack(
        [
            jnp.sqrt(alpha_bar),
            jnp.sqrt(1.0 - alpha_bar),
            mean_factor,
            jnp.log(clipped),
            jnp.log(beta_rows),
        ],
        1,
    )
    one_hot = (steps[:, None] == jnp.arange(TSTEPS)[None, :]).astype(jnp.float32)
    return jnp.dot(one_hot, plan_table, precision=HIGHEST_PRECISION)


def positions():
    quarter = D // 4
    omegas = 1.0 / 10000.0 ** (jnp.arange(quarter).astype(jnp.float32) / quarter)
    cells = jnp.arange(SEQ)
    column_angle = (cells % GRID).astype(jnp.float32)[:, None] * omegas[None, :]
    row_angle = (cells // GRID).astype(jnp.float32)[:, None] * omegas[None, :]
    return jnp.concatenate(
        [jnp.sin(column_angle), jnp.cos(column_angle), jnp.sin(row_angle), jnp.cos(row_angle)], 1
    )


def frequencies(steps):
    half_count = FREQ // 2
    frequency = jnp.exp(
        -math.log(10000.0) * jnp.arange(half_count).astype(jnp.float32) / half_count
    )
    angles = steps.astype(jnp.float32)[:, None] * frequency[None, :]
    return jnp.concatenate([jnp.cos(angles), jnp.sin(angles)], 1)


def modulate(stream, shifts, scales):
    average = jnp.mean(stream, -1, keepdims=True)
    centred = stream - average
    variance = jnp.mean(centred * centred, -1, keepdims=True)
    return centred * lax.rsqrt(variance + 1e-06) * (1.0 + scales[:, None, :]) + shifts[:, None, :]


def modulate_back(stream, shifts, scales, cotangent):
    unused, pullback = jax.vjp(modulate, stream, shifts, scales)
    return pullback(cotangent)


def smooth_back(function, inputs, cotangent):
    unused, pullback = jax.vjp(function, inputs)
    return pullback(cotangent)[0]


def gelu_tanh(inputs):
    return jax.nn.gelu(inputs, approximate=True)


def loss_terms(prediction, target, sched):
    guessed = prediction[..., :PATCH]
    variance_raw = prediction[..., PATCH:]
    mean_factor = sched[:, 2][:, None, None]
    posterior_log = sched[:, 3][:, None, None]
    beta_log = sched[:, 4][:, None, None]
    blend = 0.5 * (variance_raw + 1.0)
    model_log = blend * beta_log + (1.0 - blend) * posterior_log
    errors = guessed - target
    bound_term = 0.5 * (
        -1.0
        + model_log
        - posterior_log
        + jnp.exp(posterior_log - model_log)
        + mean_factor * errors * errors * jnp.exp(-model_log)
    )
    return jnp.sum(errors * errors + bound_term / LOG_TWO)


class Links:
    def __init__(self, dp, mod):
        self.core = 2 if mod % 2 == 0 else 1
        self.y = mod // self.core
        self.x = self.y if dp % self.y == 0 else 1
        self.z = dp // self.x
        self.count = dp * mod
        self.size = {"z": self.z, "x": self.x, "y": self.y, "c": self.core}
        self.dim = {"x": 0, "y": 1, "z": 2}

    def place(self, axis):
        index = lax.axis_index(AXES)
        below = {"c": 1, "y": self.core, "x": self.core * self.y, "z": self.core * self.y * self.x}
        return index // below[axis] % self.size[axis]

    def send(self, block, axis, shift=1):
        pairs = []
        for index in range(self.count):
            spot = {
                "c": index % self.core,
                "y": index // self.core % self.y,
                "x": index // (self.core * self.y) % self.x,
                "z": index // (self.core * self.y * self.x),
            }
            spot[axis] = (spot[axis] + shift) % self.size[axis]
            target = ((spot["z"] * self.x + spot["x"]) * self.y + spot["y"]) * self.core + spot["c"]
            pairs.append((index, target))
        return lax.ppermute(block, AXES, pairs)

    def inner(self, values):
        shape = (*values.shape[:-1], self.z, self.x * self.y, -1)
        return values.reshape(shape).swapaxes(-3, -2).reshape(values.shape)

    def outer(self, values):
        shape = (*values.shape[:-1], self.x * self.y, self.z, -1)
        return values.reshape(shape).swapaxes(-3, -2).reshape(values.shape)

    def spread(self, block):
        copies = jnp.broadcast_to(block[None], (self.count, *block.shape))
        return lax.all_to_all(copies, AXES, split_axis=0, concat_axis=0, tiled=True)

    def deliver(self, blocks):
        return lax.all_to_all(blocks, AXES, split_axis=0, concat_axis=0, tiled=True)


def pick(own, first, second):
    return jnp.where(own == 0, first, second)


def joined(own, mine, other, dim):
    return pick(
        own, jnp.concatenate([mine, other], dim), jnp.concatenate([other, mine], dim)
    )


def column_half(rows, half):
    small = D // 2
    attention = [rows[:, part * D + half * small : part * D + (half + 1) * small] for part in range(4)]
    wide = FF // 2
    return [
        jnp.concatenate(attention, 1),
        rows[:, 4 * D + half * wide : 4 * D + (half + 1) * wide],
        rows[:, 4 * D + FF + half * wide : 4 * D + FF + (half + 1) * wide],
    ]


def whole_columns(first, second):
    small = D // 2
    pieces = [
        half[0][:, part * small : (part + 1) * small] for part in range(4) for half in (first, second)
    ]
    return jnp.concatenate([*pieces, first[1], second[1], first[2], second[2]], 1)


def chip_rows(links, flat):
    core = links.place("c")
    per_chip = D * links.core // links.count
    if (D % links.count) == 0:
        rows = flat.reshape(D // links.count, WB).astype(jnp.bfloat16)
        halves = [jnp.concatenate(column_half(rows, half), 1) for half in range(2)]
        mine = pick(core, halves[0], halves[1])
        other = links.send(pick(core, halves[1], halves[0]), "c")
        return joined(core, mine, other, 0), rows[:, WB - SMALL :].reshape(-1)
    low = flat.astype(jnp.bfloat16)
    rows = joined(core, low, links.send(low, "c"), 0).reshape(per_chip, WB)
    halves = [jnp.concatenate(column_half(rows, half), 1) for half in range(2)]
    small = rows[:, WB - SMALL :].reshape(2, -1)
    return pick(core, halves[0], halves[1]), pick(core, small[0], small[1])


def gather_halves(rows):
    whole = lax.all_gather(rows, ("c", "x", "y", "z"), axis=0, tiled=True)
    return whole[:D], whole[D:]


class Reduction:
    def __init__(self, links, gradients, kind=jnp.bfloat16):
        self.links, self.kind = links, kind
        shape = (links.x, links.y, links.z, D * links.core // links.count)
        self.blocks = [rows.reshape(*shape, -1) for rows in gradients]
        total = sum(rows.shape[1] for rows in gradients)
        middle = total // 256 * 128
        self.spans = [[], []]
        for index, rows in enumerate(gradients):
            before = sum(earlier.shape[1] for earlier in gradients[:index])
            edge = min(max(middle - before, 0), rows.shape[1])
            if edge > 0:
                self.spans[0].append((index, 0, edge))
            if edge < rows.shape[1]:
                self.spans[1].append((index, edge, rows.shape[1]))

    def cut(self, sources, axis, spot):
        dim = self.links.dim[axis]
        parts = [
            lax.dynamic_slice_in_dim(self.blocks[index][..., low:high], spot, 1, dim)
            for index, low, high in sources
        ]
        return jnp.concatenate(parts, 4) if len(parts) > 1 else parts[0]

    def send(self, order):
        self.order = order
        self.got = []
        for sources, axis in zip(self.spans, order):
            extent, own = self.links.size[axis], self.links.place(axis)
            for shift in range(1, extent):
                part = self.cut(sources, axis, (own + shift) % extent).astype(self.kind)
                self.got.append(self.links.send(part, axis, shift))
        return self.got

    def add(self, got):
        got = list(got)
        blocks, spans = [], []
        for sources, axis in zip(self.spans, self.order):
            extent, own = self.links.size[axis], self.links.place(axis)
            total = self.cut(sources, axis, own).astype(jnp.float32)
            for _ in range(1, extent):
                total = total + got.pop(0).astype(jnp.float32)
            spans.append([(len(blocks), 0, total.shape[-1])])
            blocks.append(total)
        self.blocks, self.spans = blocks, spans

    def join(self):
        self.spans = [[span for sources in self.spans for span in sources]]

    def result(self):
        return self.blocks[0].reshape(-1, self.blocks[0].shape[-1])


def flat_gradient(links, joint, small):
    core = links.place("c")
    edges = [0, 2 * D, 4 * D, 6 * D]
    split = lambda rows: [rows[:, edges[part] : edges[part + 1]] for part in range(3)]
    per_device = D // links.count
    if (D % links.count) == 0:
        mine = lax.dynamic_slice_in_dim(joint, core * per_device, per_device, 0)
        sent = lax.dynamic_slice_in_dim(joint, (1 - core) * per_device, per_device, 0)
    else:
        mine, sent = joint, joint
        small = joined(core, small, links.send(small, "c"), 0)
    other = links.send(sent, "c")
    columns = whole_columns(split(pick(core, mine, other)), split(pick(core, other, mine)))
    flat = jnp.concatenate([columns, small.reshape(-1, SMALL)], 1).reshape(-1)
    if (D % links.count) == 0:
        return flat
    part = flat.shape[0] // 2
    return lax.dynamic_slice_in_dim(flat, core * part, part)


EXTENTS = [FREQ, D, CLASSES + 1, 2 * D, 1, 2, 6]
STARTS = [sum(EXTENTS[:index]) for index in range(len(EXTENTS) + 1)]


class Window:
    def __init__(self, links, length):
        self.length = length
        begins = [index * length for index in range(links.count)]
        rows = max((begin % D + length + D - 1) // D for begin in begins)
        self.rows = (rows + 15) // 16 * 16
        begin = lax.axis_index(AXES) * length
        self.first = begin // D
        self.firsts = [start // D for start in begins]
        self.offset = begin - self.first * D

    def fill(self, flat):
        padded = jnp.concatenate(
            [jnp.zeros((D,), flat.dtype), flat, jnp.zeros((self.rows * D,), flat.dtype)]
        )
        return lax.dynamic_slice_in_dim(padded, D - self.offset, self.rows * D).reshape(
            self.rows, D
        )

    def cut(self, columns, start):
        full = jnp.pad(columns, ((0, 0), (start, SROWS + self.rows - start - columns.shape[1])))
        return lax.dynamic_slice_in_dim(full, self.first, self.rows, 1)

    def put(self, columns, start, extent):
        full = jnp.zeros((columns.shape[0], SROWS + self.rows), columns.dtype)
        full = lax.dynamic_update_slice_in_dim(full, columns, self.first, 1)
        return full[:, start : start + extent]

    def assemble(self, windows, start, extent):
        inside = [
            index
            for index, first in enumerate(self.firsts)
            if first < start + extent and first + self.rows > start
        ]
        low, high = inside[0], inside[-1] + 1
        firsts = jnp.array(self.firsts[low:high])
        rows = firsts[:, None] + jnp.arange(self.rows)[None, :]
        chosen = jnp.arange(extent)[:, None, None] + start == rows[None]
        return matmul("kir,dkr->id", windows[low:high], chosen.astype(windows.dtype))

    def flatten(self, rows):
        return lax.dynamic_slice_in_dim(rows.reshape(-1), self.offset, self.length)


def adam_update(weight, gradient, first, second):
    first_new = BETA_ONE * first + (1.0 - BETA_ONE) * gradient
    second_new = BETA_TWO * second + (1.0 - BETA_TWO) * gradient * gradient
    corrected = first_new / (1.0 - BETA_ONE**STEP)
    spread = jnp.sqrt(second_new / (1.0 - BETA_TWO**STEP))
    return (weight - LEARN_RATE * corrected / (spread + EPSILON), first_new, second_new)


def attend(normed, w_qkv):
    images = normed.shape[0]
    heads = HEADS // 2
    low = jnp.bfloat16
    triple = matmul("isd,de->ise", normed, w_qkv).astype(low)
    triple = triple.reshape(images, SEQ, 3, heads, HEAD_DIM)
    queries, keys, values = triple[:, :, 0], triple[:, :, 1], triple[:, :, 2]
    scores = matmul("iqhe,ikhe->ihqk", queries, keys) * (1.0 / math.sqrt(HEAD_DIM))
    totals = jax.nn.logsumexp(scores, axis=-1)
    weights = jnp.exp(scores - totals[..., None]).astype(low)
    mixed = matmul("ihqk,ikhe->iqhe", weights, values).astype(low)
    return mixed.reshape(images, SEQ, D // 2), (queries, keys, values, totals)


def attend_back(kept, mixed_grad):
    queries, keys, values, totals = kept
    images = queries.shape[0]
    low = jnp.bfloat16
    mixed_grad = mixed_grad.astype(low).reshape(images, SEQ, HEADS // 2, HEAD_DIM)
    score_scale = 1.0 / math.sqrt(HEAD_DIM)
    softmax_rows = jnp.exp(
        matmul("iqhe,ikhe->ihqk", queries, keys) * score_scale - totals[..., None]
    )
    weight_grad = matmul("iqhe,ikhe->ihqk", mixed_grad, values)
    score_grad = (
        softmax_rows * (weight_grad - jnp.sum(weight_grad * softmax_rows, -1, keepdims=True))
    ).astype(low)
    query_grad = (matmul("ihqk,ikhe->iqhe", score_grad, keys) * score_scale).astype(low)
    key_grad = (matmul("ihqk,iqhe->ikhe", score_grad, queries) * score_scale).astype(low)
    value_grad = matmul("ihqk,iqhe->ikhe", softmax_rows.astype(low), mixed_grad).astype(low)
    return jnp.stack([query_grad, key_grad, value_grad], 2).reshape(images, SEQ, 3 * D // 2)


def shards(
    links,
    latents,
    noise,
    timesteps,
    labels,
    dropped,
    block_master,
    block_m,
    block_v,
    stem_master,
    stem_m,
    stem_v,
    ada_w,
    ada_w_m,
    ada_w_v,
):
    low, wide = jnp.bfloat16, jnp.float32
    images = timesteps.shape[0]
    everyone = links.count * images
    own_cols = ada_w.shape[1]
    own_rows = ada_w.shape[0]
    row_at = lax.axis_index(("z", "x")) * own_rows
    col_at = lax.axis_index(("y", "c")) * own_cols
    groups = 6 * D // own_cols

    core = links.place("c")
    chunks, small = chip_rows(links, block_master)
    w_attention = gather_halves(chunks[:, : 2 * D])
    w_mlp = gather_halves(chunks[:, 2 * D :])
    w_qkv = [half[:, : 3 * D // 2] for half in w_attention]
    w_proj = [half[:, 3 * D // 2 :] for half in w_attention]
    w_up = [half[:, : 2 * D] for half in w_mlp]
    w_down = [half[:, 2 * D :] for half in w_mlp]

    window = Window(links, stem_master.shape[0])
    stem = window.fill(stem_master.astype(low))
    ada_low = ada_w.astype(low)
    integers = jnp.stack([timesteps, jnp.where(dropped == 1, CLASSES, labels)])
    digits = jnp.stack([integers // 32, integers % 32]).astype(low).reshape(-1)
    got = links.spread(jnp.concatenate([digits, small]))
    digits = got[:, : 4 * images].astype(jnp.int32).reshape(links.count, 2, 2, images)
    integers = digits[:, 0] * 32 + digits[:, 1]
    small = links.inner(got[:, 4 * images :].reshape(D, SMALL).T).T
    w_patch, w_head = small[:, :PATCH], small[:, PATCH:]
    all_steps = integers[:, 0].reshape(everyone)
    chosen = integers[:, 1].reshape(everyone)
    timing = frequencies(all_steps).astype(low)
    one_hot = (chosen[:, None] == jnp.arange(CLASSES + 1)[None, :]).astype(low)
    bias_start, bias_extent = STARTS[4], 9
    bias_share = -(-bias_extent * D // links.count)
    mark = jnp.arange(bias_extent)[:, None] + bias_start == (
        window.first + jnp.arange(window.rows)
    )
    bias_part = matmul("br,rd->bd", mark.astype(low), stem).reshape(bias_extent * D)
    bias_part = jnp.pad(bias_part, (0, bias_share * links.count - bias_extent * D))

    before_part = matmul("ir,rd->id", window.cut(timing, STARTS[0]), stem)
    got = links.deliver(
        jnp.concatenate(
            [
                before_part.reshape(links.count, images * D),
                bias_part.reshape(links.count, bias_share),
            ],
            1,
        )
    ).sum(0)
    got = links.spread(got)
    all_before = got[:, : images * D].reshape(everyone, D)
    all_hidden = jax.nn.silu(all_before).astype(low)
    biases = got[:, images * D :].reshape(-1)[: bias_extent * D].reshape(bias_extent, D)
    left = window.cut(jnp.concatenate([all_hidden, one_hot], 1), STARTS[1])
    condition = links.deliver(
        matmul("ir,rd->id", left, stem).reshape(links.count, images, D)
    ).sum(0)
    signal = jax.nn.silu(condition).astype(low)
    all_signal = links.spread(signal).reshape(everyone, D)
    signal_rows = lax.dynamic_slice_in_dim(all_signal, row_at, own_rows, 1)
    parts = links.deliver(
        matmul("ir,rc->ic", signal_rows, ada_low).reshape(links.count, images, own_cols)
    )
    modulation = (
        parts.reshape(-1, groups, images, own_cols).sum(0).transpose(1, 0, 2).reshape(images, 6 * D)
        + biases[3:].reshape(6 * D)
    ).astype(low)
    pieces = links.inner(modulation.astype(wide).reshape(images, 6, D))
    pieces = [pieces[:, part] for part in range(6)]
    final_part = window.put(matmul("id,rd->ir", all_signal, stem), STARTS[3], 2 * D)

    sched = plan(timesteps)
    target = noise.reshape(images, SEQ, PATCH)
    noisy_rows = (
        sched[:, 0][:, None, None] * latents.reshape(images, SEQ, PATCH)
        + sched[:, 1][:, None, None] * target
    ).astype(low)
    stream = matmul("isp,dp->isd", noisy_rows, w_patch) + links.inner(biases[0]) + links.inner(positions())[None]
    normed = modulate(stream, pieces[0], pieces[1]).astype(low)
    mixed, kept = [], []
    for half in range(2):
        rows, saved = attend(normed, w_qkv[half])
        mixed.append(rows)
        kept.append(saved)
    attended = sum(matmul("isd,od->iso", mixed[half], w_proj[half]) for half in range(2))
    middle = stream + pieces[2][:, None, :] * attended
    second = modulate(middle, pieces[3], pieces[4]).astype(low)
    second, final_part = lax.optimization_barrier((second, final_part))
    final_mod = links.deliver(final_part.reshape(links.count, images, 2 * D)).sum(0) + biases[
        1:3
    ].reshape(2 * D)
    final_mod = links.inner(final_mod.reshape(images, 2, D))
    final_shift, final_scale = final_mod[:, 0], final_mod[:, 1]
    inner = [matmul("isd,df->isf", second, w_up[half]) for half in range(2)]
    active = [gelu_tanh(rows).astype(low) for rows in inner]
    output = sum(matmul("isf,of->iso", active[half], w_down[half]) for half in range(2))
    layer_out = middle + pieces[5][:, None, :] * output
    final_normed = modulate(layer_out, final_shift, final_scale).astype(low)
    prediction = matmul("isd,do->iso", final_normed, w_head)
    loss_local, loss_back = jax.vjp(
        lambda predicted: loss_terms(predicted, target, sched), prediction
    )

    def tokens(rows):
        return rows.reshape(images * SEQ, rows.shape[-1])

    def with_partner(first, second=None):
        if second is None:
            mine, sent = tokens(first), tokens(first)
        else:
            first, second = tokens(first), tokens(second)
            mine, sent = pick(core, first, second), pick(core, second, first)
        return jnp.concatenate([mine, links.send(sent, "c")], 0)

    def sum_near(rows):
        return lax.psum_scatter(rows, ("x", "y"), scatter_dimension=0, tiled=True)

    def sum_far(rows):
        return lax.psum_scatter(rows, "z", scatter_dimension=0, tiled=True)

    def together(*values):
        return lax.optimization_barrier(values)

    out_grad = loss_back(jnp.ones_like(loss_local))[0].astype(low)
    grad_head = matmul("iso,isd->do", out_grad, final_normed)
    upstream, shift_grad, scale_grad = modulate_back(
        layer_out, final_shift, final_scale, matmul("iso,do->isd", out_grad, w_head)
    )
    final_grad = links.outer(jnp.stack([shift_grad, scale_grad], 1)).reshape(images, 2 * D)
    down_in = (pieces[5][:, None, :] * upstream).astype(low)
    gate_b = jnp.sum(upstream * output, 1)
    active_both = with_partner(*active)
    second_both = with_partner(second)
    mixed_both = with_partner(*mixed)
    normed_both = with_partner(normed)
    down_both = with_partner(down_in)
    inner_grad = [
        smooth_back(
            gelu_tanh, inner[half], matmul("iso,of->isf", down_in, w_down[half])
        ).astype(low)
        for half in range(2)
    ]
    inner_both = with_partner(*inner_grad)
    inner_grad, down_both, active_both = together(inner_grad, down_both, active_both)
    grad_down = matmul("to,tf->of", down_both, active_both).astype(low)
    inner_both, grad_down = together(inner_both, grad_down)
    grad_up = matmul("td,tf->df", second_both, inner_both).astype(low)
    grad_mlp = jnp.concatenate([grad_up, grad_down], 1)
    inner_grad, grad_mlp = together(inner_grad, grad_mlp)
    near_mlp = sum_near(grad_mlp)
    second_grad = sum(
        matmul("isf,df->isd", inner_grad[half], w_up[half]) for half in range(2)
    )
    back_mid, shift_b, scale_b = modulate_back(middle, pieces[3], pieces[4], second_grad)
    grad_mid = upstream + back_mid
    proj_in = (pieces[2][:, None, :] * grad_mid).astype(low)
    gate_a = jnp.sum(grad_mid * attended, 1)
    proj_both = with_partner(proj_in)
    final_low = final_grad.astype(low)
    early = links.outer(jnp.stack([gate_a, shift_b, scale_b, gate_b], 1)).reshape(images, 4 * D)
    early = early.astype(low)
    early = links.spread(jnp.concatenate([early, final_low], 1)).reshape(everyone, 6 * D)
    qkv_grad = [
        attend_back(kept[half], matmul("iso,od->isd", proj_in, w_proj[half])) for half in range(2)
    ]
    grad_proj = matmul("to,td->od", proj_both, mixed_both)
    qkv_both = with_partner(*qkv_grad)
    normed_grad = sum(matmul("ise,de->isd", qkv_grad[half], w_qkv[half]) for half in range(2))
    back_in, shift_a, scale_a = modulate_back(stream, pieces[0], pieces[1], normed_grad)
    stream_grad = grad_mid + back_in
    late = links.outer(jnp.stack([shift_a, scale_a], 1)).reshape(images, 2 * D).astype(low)
    late, stream_grad, qkv_both, early = together(late, stream_grad, qkv_both, early)
    late = links.spread(late).reshape(everyone, 2 * D)
    grad_qkv = matmul("td,te->de", normed_both, qkv_both)
    grad_patch = matmul("isp,isd->dp", noisy_rows, stream_grad.astype(low))
    small_grad = links.outer(jnp.concatenate([grad_patch, grad_head], 1).T).T
    small_grad = small_grad.reshape(links.count, -1)
    sums_of_attention = Reduction(links, [grad_qkv, grad_proj])
    more = sums_of_attention.send("yx")

    late, near_mlp = together(late, near_mlp)
    reduced_mlp = sum_far(near_mlp)
    all_final = early[:, 4 * D :]
    all_modulation = jnp.concatenate([late, early[:, : 4 * D]], 1)
    own_modulation = lax.dynamic_slice_in_dim(all_modulation, col_at, own_cols, 1)
    signal_part = matmul("ir,rd->id", window.cut(all_final, STARTS[3]), stem)
    ada_part = matmul("ic,rc->ir", own_modulation, ada_low)
    signal_part = lax.dynamic_update_slice_in_dim(
        signal_part,
        lax.dynamic_slice_in_dim(signal_part, row_at, own_rows, 1) + ada_part,
        row_at,
        1,
    )
    sums = jnp.concatenate([links.outer(jnp.sum(stream_grad, (0, 1))), jnp.sum(final_grad, 0)])
    share = -(-sums.shape[0] // links.count)
    sums = jnp.pad(sums, (0, share * links.count - sums.shape[0])).reshape(links.count, share)
    summed = links.deliver(
        jnp.concatenate([signal_part.reshape(links.count, images * D), sums, small_grad], 1)
    ).sum(0)
    small = summed[images * D + share :]
    condition_grad = smooth_back(jax.nn.silu, condition, summed[: images * D].reshape(images, D))
    spreading = jnp.concatenate([condition_grad.reshape(-1), summed[images * D : images * D + share]])
    spreading, more = together(spreading, more)
    sums_of_attention.add(more)
    more = sums_of_attention.send("xy")
    spread = links.spread(spreading)
    all_condition = spread[:, : images * D].reshape(everyone, D)
    all_sums = spread[:, images * D :].reshape(-1)[: 3 * D]
    condition_low = all_condition.astype(low)
    hidden_part = matmul("id,rd->ir", condition_low, stem)
    before_part = window.cut(all_before, STARTS[1])
    before_part = smooth_back(jax.nn.silu, before_part, hidden_part)
    row = window.first + jnp.arange(window.rows)
    before_part = jnp.where((row >= STARTS[1]) & (row < STARTS[2]), before_part, 0.0).astype(low)
    before_part, more = together(before_part, more)
    sums_of_attention.add(more)
    sums_of_attention.join()
    more = sums_of_attention.send("z")
    before_low = window.assemble(links.spread(before_part), STARTS[1], D).astype(low)
    sums_of_attention.add(more)
    joint = jnp.concatenate([sums_of_attention.result(), reduced_mlp.astype(wide)], 1)
    square = jnp.sum(joint * joint) + jnp.sum(small * small)
    totals = links.spread(jnp.stack([loss_local, square])).sum(0)
    block_grad = flat_gradient(links, joint, small)
    loss_total, squares = totals[0], totals[1]
    bias_rows = jnp.concatenate(
        [all_sums, jnp.sum(all_modulation.astype(wide), 0)]
    ).reshape(bias_extent, D)

    def product_squares(left, right):
        left, right = left.astype(wide), right.astype(wide)
        grams = [jnp.dot(rows, rows.T, precision=HIGHEST_PRECISION) for rows in (left, right)]
        return jnp.sum(grams[0] * grams[1])

    squares = (
        squares
        + product_squares(all_signal, all_modulation)
        + product_squares(all_signal, all_final)
        + product_squares(one_hot, all_condition)
        + product_squares(all_hidden, condition_low)
        + product_squares(timing, before_low)
        + jnp.sum(bias_rows * bias_rows)
    )
    ada_grad = matmul("ir,ic->rc", signal_rows, own_modulation)
    low_left = jnp.concatenate(
        [
            window.cut(timing, STARTS[0]),
            window.cut(all_hidden, STARTS[1]),
            window.cut(all_final, STARTS[3]),
        ],
        0,
    )
    low_right = jnp.concatenate([before_low, condition_low, all_signal], 0)
    stem_rows = matmul("ir,id->rd", low_left, low_right)
    wide_left = jnp.concatenate(
        [window.cut(one_hot.astype(wide), STARTS[2]), mark.astype(wide)], 0
    )
    wide_right = jnp.concatenate([all_condition, bias_rows], 0)
    stem_rows = stem_rows + jnp.dot(wide_left.T, wide_right, precision=HIGHEST_PRECISION)
    stem_grad = window.flatten(stem_rows)
    grad_norm = jnp.sqrt(squares)
    factor = THRESHOLD / jnp.maximum(grad_norm, THRESHOLD)
    block_new = adam_update(block_master, block_grad * factor, block_m, block_v)
    stem_new = adam_update(stem_master, stem_grad * factor, stem_m, stem_v)
    ada_new = adam_update(ada_w, ada_grad * factor, ada_w_m, ada_w_v)
    return (loss_total, grad_norm, *block_new, *stem_new, *ada_new)


def solution(mesh):
    links = Links(mesh.shape["dp"], mesh.shape["mod"])
    grid = jax.sharding.Mesh(
        mesh.devices.reshape(links.z, links.x, links.y, links.core), AXES
    )
    flat, rows, ada = P(AXES), P(AXES, None), P(("z", "x"), ("y", "c"))
    return jax.shard_map(
        functools.partial(shards, links),
        mesh=grid,
        in_specs=(rows, rows) + (flat,) * 9 + (ada,) * 3,
        out_specs=(P(), P()) + (flat,) * 6 + (ada,) * 3,
        check_vma=False,
    )
```

```python
import functools
import math

import jax
import jax.numpy as jnp
from jax import lax
from jax.experimental import pallas as pl
from jax.experimental.pallas import tpu as pltpu
from jax.sharding import PartitionSpec as P

D = 1152
HEADS = 16
HEAD_DIM = 72
FF = 4608
CLASSES = 1000
PATCH = 16
GRID = 16
FREQ = 256
TSTEPS = 1000
STEP = 10
SEQ = 256
WB = 13872
SMALL = 3 * PATCH
SROWS = 4722


HIGHEST_PRECISION = lax.Precision.HIGHEST
AXES = ("z", "x", "y", "c")
LOG_TWO = math.log(2.0)
THRESHOLD = 1.0
LEARN_RATE = 0.05
BETA_ONE = 0.9
BETA_TWO = 0.999
EPSILON = 1e-08


def matmul(form, left, right):
    return jnp.einsum(form, left, right, preferred_element_type=jnp.float32)


def plan(steps):
    step_index = jnp.arange(TSTEPS).astype(jnp.float32)
    beta_rows = 0.0001 + (0.02 - 0.0001) * step_index / (TSTEPS - 1)
    alpha_bar = jnp.cumprod(1.0 - beta_rows)
    previous = jnp.concatenate([jnp.ones((1,), jnp.float32), alpha_bar[:-1]])
    posterior = beta_rows * (1.0 - previous) / (1.0 - alpha_bar)
    clipped = jnp.concatenate([posterior[1:2], posterior[1:]])
    mean_factor = beta_rows * beta_rows * previous / ((1.0 - alpha_bar) * alpha_bar)
    plan_table = jnp.stack(
        [
            jnp.sqrt(alpha_bar),
            jnp.sqrt(1.0 - alpha_bar),
            mean_factor,
            jnp.log(clipped),
            jnp.log(beta_rows),
        ],
        1,
    )
    one_hot = (steps[:, None] == jnp.arange(TSTEPS)[None, :]).astype(jnp.float32)
    return jnp.dot(one_hot, plan_table, precision=HIGHEST_PRECISION)


def positions():
    quarter = D // 4
    omegas = 1.0 / 10000.0 ** (jnp.arange(quarter).astype(jnp.float32) / quarter)
    cells = jnp.arange(SEQ)
    column_angle = (cells % GRID).astype(jnp.float32)[:, None] * omegas[None, :]
    row_angle = (cells // GRID).astype(jnp.float32)[:, None] * omegas[None, :]
    return jnp.concatenate(
        [jnp.sin(column_angle), jnp.cos(column_angle), jnp.sin(row_angle), jnp.cos(row_angle)], 1
    )


def frequencies(steps):
    half_count = FREQ // 2
    frequency = jnp.exp(
        -math.log(10000.0) * jnp.arange(half_count).astype(jnp.float32) / half_count
    )
    angles = steps.astype(jnp.float32)[:, None] * frequency[None, :]
    return jnp.concatenate([jnp.cos(angles), jnp.sin(angles)], 1)


def modulate(stream, shifts, scales):
    average = jnp.mean(stream, -1, keepdims=True)
    centred = stream - average
    variance = jnp.mean(centred * centred, -1, keepdims=True)
    return centred * lax.rsqrt(variance + 1e-06) * (1.0 + scales[:, None, :]) + shifts[:, None, :]


def modulate_back(stream, shifts, scales, cotangent):
    unused, pullback = jax.vjp(modulate, stream, shifts, scales)
    return pullback(cotangent)


def smooth_back(function, inputs, cotangent):
    unused, pullback = jax.vjp(function, inputs)
    return pullback(cotangent)[0]


def gelu_tanh(inputs):
    return jax.nn.gelu(inputs, approximate=True)


def loss_terms(prediction, target, sched):
    guessed = prediction[..., :PATCH]
    variance_raw = prediction[..., PATCH:]
    mean_factor = sched[:, 2][:, None, None]
    posterior_log = sched[:, 3][:, None, None]
    beta_log = sched[:, 4][:, None, None]
    blend = 0.5 * (variance_raw + 1.0)
    model_log = blend * beta_log + (1.0 - blend) * posterior_log
    errors = guessed - target
    bound_term = 0.5 * (
        -1.0
        + model_log
        - posterior_log
        + jnp.exp(posterior_log - model_log)
        + mean_factor * errors * errors * jnp.exp(-model_log)
    )
    return jnp.sum(errors * errors + bound_term / LOG_TWO)


class Links:
    def __init__(self, dp, mod):
        self.core = 2 if mod % 2 == 0 else 1
        self.y = mod // self.core
        self.x = self.y if dp % self.y == 0 else 1
        self.z = dp // self.x
        self.count = dp * mod
        self.size = {"z": self.z, "x": self.x, "y": self.y, "c": self.core}
        self.dim = {"x": 0, "y": 1, "z": 2}

    def place(self, axis):
        index = lax.axis_index(AXES)
        below = {"c": 1, "y": self.core, "x": self.core * self.y, "z": self.core * self.y * self.x}
        return index // below[axis] % self.size[axis]

    def send(self, block, axis, shift=1):
        pairs = []
        for index in range(self.count):
            spot = {
                "c": index % self.core,
                "y": index // self.core % self.y,
                "x": index // (self.core * self.y) % self.x,
                "z": index // (self.core * self.y * self.x),
            }
            spot[axis] = (spot[axis] + shift) % self.size[axis]
            target = ((spot["z"] * self.x + spot["x"]) * self.y + spot["y"]) * self.core + spot["c"]
            pairs.append((index, target))
        return lax.ppermute(block, AXES, pairs)

    def inner(self, values):
        shape = (*values.shape[:-1], self.z, self.x * self.y, -1)
        return values.reshape(shape).swapaxes(-3, -2).reshape(values.shape)

    def outer(self, values):
        shape = (*values.shape[:-1], self.x * self.y, self.z, -1)
        return values.reshape(shape).swapaxes(-3, -2).reshape(values.shape)

    def spread(self, block):
        copies = jnp.broadcast_to(block[None], (self.count, *block.shape))
        return lax.all_to_all(copies, AXES, split_axis=0, concat_axis=0, tiled=True)

    def deliver(self, blocks):
        return lax.all_to_all(blocks, AXES, split_axis=0, concat_axis=0, tiled=True)


def pick(own, first, second):
    return jnp.where(own == 0, first, second)


def joined(own, mine, other, dim):
    return pick(
        own, jnp.concatenate([mine, other], dim), jnp.concatenate([other, mine], dim)
    )


def column_half(rows, half):
    small = D // 2
    attention = [rows[:, part * D + half * small : part * D + (half + 1) * small] for part in range(4)]
    wide = FF // 2
    return [
        jnp.concatenate(attention, 1),
        rows[:, 4 * D + half * wide : 4 * D + (half + 1) * wide],
        rows[:, 4 * D + FF + half * wide : 4 * D + FF + (half + 1) * wide],
    ]


def whole_columns(first, second):
    small = D // 2
    pieces = [
        half[0][:, part * small : (part + 1) * small] for part in range(4) for half in (first, second)
    ]
    return jnp.concatenate([*pieces, first[1], second[1], first[2], second[2]], 1)


def chip_rows(links, flat):
    core = links.place("c")
    per_chip = D * links.core // links.count
    if (D % links.count) == 0:
        rows = flat.reshape(D // links.count, WB).astype(jnp.bfloat16)
        halves = [jnp.concatenate(column_half(rows, half), 1) for half in range(2)]
        mine = pick(core, halves[0], halves[1])
        other = links.send(pick(core, halves[1], halves[0]), "c")
        return joined(core, mine, other, 0), rows[:, WB - SMALL :].reshape(-1)
    low = flat.astype(jnp.bfloat16)
    rows = joined(core, low, links.send(low, "c"), 0).reshape(per_chip, WB)
    halves = [jnp.concatenate(column_half(rows, half), 1) for half in range(2)]
    small = rows[:, WB - SMALL :].reshape(2, -1)
    return pick(core, halves[0], halves[1]), pick(core, small[0], small[1])


def gather_halves(rows):
    return lax.all_gather(rows, ("c", "x", "y", "z"), axis=0, tiled=True)


class Reduction:
    def __init__(self, links, gradients, kind=jnp.bfloat16):
        self.links, self.kind = links, kind
        shape = (links.x, links.y, links.z, D * links.core // links.count)
        self.blocks = [rows.reshape(*shape, -1) for rows in gradients]
        total = sum(rows.shape[1] for rows in gradients)
        middle = total // 256 * 128
        self.spans = [[], []]
        for index, rows in enumerate(gradients):
            before = sum(earlier.shape[1] for earlier in gradients[:index])
            edge = min(max(middle - before, 0), rows.shape[1])
            if edge > 0:
                self.spans[0].append((index, 0, edge))
            if edge < rows.shape[1]:
                self.spans[1].append((index, edge, rows.shape[1]))

    def cut(self, sources, axis, spot):
        dim = self.links.dim[axis]
        parts = [
            lax.dynamic_slice_in_dim(self.blocks[index][..., low:high], spot, 1, dim)
            for index, low, high in sources
        ]
        return jnp.concatenate(parts, 4) if len(parts) > 1 else parts[0]

    def send(self, order):
        self.order = order
        self.got = []
        for sources, axis in zip(self.spans, order):
            extent, own = self.links.size[axis], self.links.place(axis)
            for shift in range(1, extent):
                part = self.cut(sources, axis, (own + shift) % extent).astype(self.kind)
                self.got.append(self.links.send(part, axis, shift))
        return self.got

    def add(self, got):
        got = list(got)
        blocks, spans = [], []
        for sources, axis in zip(self.spans, self.order):
            extent, own = self.links.size[axis], self.links.place(axis)
            total = self.cut(sources, axis, own).astype(jnp.float32)
            for _ in range(1, extent):
                total = total + got.pop(0).astype(jnp.float32)
            spans.append([(len(blocks), 0, total.shape[-1])])
            blocks.append(total)
        self.blocks, self.spans = blocks, spans

    def join(self):
        self.spans = [[span for sources in self.spans for span in sources]]

    def result(self):
        return self.blocks[0].reshape(-1, self.blocks[0].shape[-1])


def flat_gradient(links, joint, small):
    core = links.place("c")
    edges = [0, 2 * D, 4 * D, 6 * D]
    split = lambda rows: [rows[:, edges[part] : edges[part + 1]] for part in range(3)]
    per_device = D // links.count
    if (D % links.count) == 0:
        mine = lax.dynamic_slice_in_dim(joint, core * per_device, per_device, 0)
        sent = lax.dynamic_slice_in_dim(joint, (1 - core) * per_device, per_device, 0)
    else:
        mine, sent = joint, joint
        small = joined(core, small, links.send(small, "c"), 0)
    other = links.send(sent, "c")
    columns = whole_columns(split(pick(core, mine, other)), split(pick(core, other, mine)))
    flat = jnp.concatenate([columns, small.reshape(-1, SMALL)], 1).reshape(-1)
    if (D % links.count) == 0:
        return flat
    part = flat.shape[0] // 2
    return lax.dynamic_slice_in_dim(flat, core * part, part)


EXTENTS = [FREQ, D, CLASSES + 1, 2 * D, 1, 2, 6]
STARTS = [sum(EXTENTS[:index]) for index in range(len(EXTENTS) + 1)]


class Window:
    def __init__(self, links, length):
        self.length = length
        begins = [index * length for index in range(links.count)]
        rows = max((begin % D + length + D - 1) // D for begin in begins)
        self.rows = (rows + 15) // 16 * 16
        begin = lax.axis_index(AXES) * length
        self.first = begin // D
        self.firsts = [start // D for start in begins]
        self.offset = begin - self.first * D

    def fill(self, flat):
        padded = jnp.concatenate(
            [jnp.zeros((D,), flat.dtype), flat, jnp.zeros((self.rows * D,), flat.dtype)]
        )
        return lax.dynamic_slice_in_dim(padded, D - self.offset, self.rows * D).reshape(
            self.rows, D
        )

    def cut(self, columns, start):
        full = jnp.pad(columns, ((0, 0), (start, SROWS + self.rows - start - columns.shape[1])))
        return lax.dynamic_slice_in_dim(full, self.first, self.rows, 1)

    def put(self, columns, start, extent):
        full = jnp.zeros((columns.shape[0], SROWS + self.rows), columns.dtype)
        full = lax.dynamic_update_slice_in_dim(full, columns, self.first, 1)
        return full[:, start : start + extent]

    def assemble(self, windows, start, extent):
        inside = [
            index
            for index, first in enumerate(self.firsts)
            if first < start + extent and first + self.rows > start
        ]
        low, high = inside[0], inside[-1] + 1
        firsts = jnp.array(self.firsts[low:high])
        rows = firsts[:, None] + jnp.arange(self.rows)[None, :]
        chosen = jnp.arange(extent)[:, None, None] + start == rows[None]
        return matmul("kir,dkr->id", windows[low:high], chosen.astype(windows.dtype))

    def flatten(self, rows):
        return lax.dynamic_slice_in_dim(rows.reshape(-1), self.offset, self.length)


def adam_update(weight, gradient, first, second):
    first_new = BETA_ONE * first + (1.0 - BETA_ONE) * gradient
    second_new = BETA_TWO * second + (1.0 - BETA_TWO) * gradient * gradient
    corrected = first_new / (1.0 - BETA_ONE**STEP)
    spread = jnp.sqrt(second_new / (1.0 - BETA_TWO**STEP))
    return (weight - LEARN_RATE * corrected / (spread + EPSILON), first_new, second_new)


def attend(normed, w_qkv):
    images = normed.shape[0]
    heads = HEADS // 2
    low = jnp.bfloat16
    triple = matmul("isd,de->ise", normed, w_qkv).astype(low)
    triple = triple.reshape(images, SEQ, 3, heads, HEAD_DIM)
    queries, keys, values = triple[:, :, 0], triple[:, :, 1], triple[:, :, 2]
    scores = matmul("iqhe,ikhe->ihqk", queries, keys) * (1.0 / math.sqrt(HEAD_DIM))
    totals = jax.nn.logsumexp(scores, axis=-1)
    weights = jnp.exp(scores - totals[..., None]).astype(low)
    mixed = matmul("ihqk,ikhe->iqhe", weights, values).astype(low)
    return mixed.reshape(images, SEQ, D // 2), (queries, keys, values, totals)


def attend_back(kept, mixed_grad):
    queries, keys, values, totals = kept
    images = queries.shape[0]
    low = jnp.bfloat16
    mixed_grad = mixed_grad.astype(low).reshape(images, SEQ, HEADS // 2, HEAD_DIM)
    score_scale = 1.0 / math.sqrt(HEAD_DIM)
    softmax_rows = jnp.exp(
        matmul("iqhe,ikhe->ihqk", queries, keys) * score_scale - totals[..., None]
    )
    weight_grad = matmul("iqhe,ikhe->ihqk", mixed_grad, values)
    score_grad = (
        softmax_rows * (weight_grad - jnp.sum(weight_grad * softmax_rows, -1, keepdims=True))
    ).astype(low)
    query_grad = (matmul("ihqk,ikhe->iqhe", score_grad, keys) * score_scale).astype(low)
    key_grad = (matmul("ihqk,iqhe->ikhe", score_grad, queries) * score_scale).astype(low)
    value_grad = matmul("ihqk,iqhe->ikhe", softmax_rows.astype(low), mixed_grad).astype(low)
    return jnp.stack([query_grad, key_grad, value_grad], 2).reshape(images, SEQ, 3 * D // 2)


def accumulate(total_ref, part):
    @pl.when(pl.program_id(0) == 0)
    def _():
        total_ref[...] = part

    @pl.when(pl.program_id(0) > 0)
    def _():
        total_ref[...] += part


def product(left, right, dims):
    return lax.dot_general(left, right, (dims, ((), ())), preferred_element_type=jnp.float32)


def mlp_kernel(rows_ref, up_ref, down_ref, inner_ref, active_ref, total_ref):
    inner = product(rows_ref[...], up_ref[...], ((1,), (0,)))
    inner_ref[...] = inner
    active = gelu_tanh(inner).astype(jnp.bfloat16)
    active_ref[...] = active
    accumulate(total_ref, product(active, down_ref[...], ((1,), (1,))))


def mlp_back_kernel(rows_ref, inner_ref, up_ref, down_ref, grad_ref, total_ref):
    back = product(rows_ref[...], down_ref[...], ((1,), (0,)))
    grad = smooth_back(gelu_tanh, inner_ref[...], back).astype(jnp.bfloat16)
    grad_ref[...] = grad
    accumulate(total_ref, product(grad, up_ref[...], ((1,), (1,))))


def mlp_call(kernel, operands, weights, outputs):
    count, per_half = FF // D, FF // 2 // D
    rows = operands[0].shape[0]
    whole = pl.BlockSpec((rows, D), lambda step: (0, 0))
    part = pl.BlockSpec((rows, D), lambda step: (0, step))
    up = pl.BlockSpec((D, D), lambda step: (step // per_half, step % per_half))
    down = pl.BlockSpec((D, D), lambda step: (step // per_half, per_half + step % per_half))
    return pl.pallas_call(
        kernel,
        grid=(count,),
        in_specs=[whole] + [part] * (len(operands) - 1) + [up, down],
        out_specs=[part] * len(outputs) + [whole],
        out_shape=[jax.ShapeDtypeStruct((rows, FF), kind) for kind in outputs]
        + [jax.ShapeDtypeStruct((rows, D), jnp.float32)],
        compiler_params=pltpu.CompilerParams(vmem_limit_bytes=52 * 1024 * 1024),
        cost_estimate=pl.CostEstimate(
            flops=4 * rows * D * FF, bytes_accessed=4 * D * FF + 6 * rows * FF, transcendentals=rows * FF
        ),
    )(*operands, weights, weights)


def shards(
    links,
    latents,
    noise,
    timesteps,
    labels,
    dropped,
    block_master,
    block_m,
    block_v,
    stem_master,
    stem_m,
    stem_v,
    ada_w,
    ada_w_m,
    ada_w_v,
):
    low, wide = jnp.bfloat16, jnp.float32
    images = timesteps.shape[0]
    everyone = links.count * images
    own_cols = ada_w.shape[1]
    own_rows = ada_w.shape[0]
    row_at = lax.axis_index(("z", "x")) * own_rows
    col_at = lax.axis_index(("y", "c")) * own_cols
    groups = 6 * D // own_cols

    core = links.place("c")
    chunks, small = chip_rows(links, block_master)
    w_attention = gather_halves(chunks[:, : 2 * D])
    w_attention = [w_attention[:D], w_attention[D:]]
    w_mlp = gather_halves(chunks[:, 2 * D :])
    w_qkv = [half[:, : 3 * D // 2] for half in w_attention]
    w_proj = [half[:, 3 * D // 2 :] for half in w_attention]

    window = Window(links, stem_master.shape[0])
    stem = window.fill(stem_master.astype(low))
    ada_low = ada_w.astype(low)
    integers = jnp.stack([timesteps, jnp.where(dropped == 1, CLASSES, labels)])
    digits = jnp.stack([integers // 32, integers % 32]).astype(low).reshape(-1)
    got = links.spread(jnp.concatenate([digits, small]))
    digits = got[:, : 4 * images].astype(jnp.int32).reshape(links.count, 2, 2, images)
    integers = digits[:, 0] * 32 + digits[:, 1]
    small = links.inner(got[:, 4 * images :].reshape(D, SMALL).T).T
    w_patch, w_head = small[:, :PATCH], small[:, PATCH:]
    all_steps = integers[:, 0].reshape(everyone)
    chosen = integers[:, 1].reshape(everyone)
    timing = frequencies(all_steps).astype(low)
    one_hot = (chosen[:, None] == jnp.arange(CLASSES + 1)[None, :]).astype(low)
    bias_start, bias_extent = STARTS[4], 9
    bias_share = -(-bias_extent * D // links.count)
    mark = jnp.arange(bias_extent)[:, None] + bias_start == (
        window.first + jnp.arange(window.rows)
    )
    bias_part = matmul("br,rd->bd", mark.astype(low), stem).reshape(bias_extent * D)
    bias_part = jnp.pad(bias_part, (0, bias_share * links.count - bias_extent * D))

    before_part = matmul("ir,rd->id", window.cut(timing, STARTS[0]), stem)
    got = links.deliver(
        jnp.concatenate(
            [
                before_part.reshape(links.count, images * D),
                bias_part.reshape(links.count, bias_share),
            ],
            1,
        )
    ).sum(0)
    got = links.spread(got)
    all_before = got[:, : images * D].reshape(everyone, D)
    all_hidden = jax.nn.silu(all_before).astype(low)
    biases = got[:, images * D :].reshape(-1)[: bias_extent * D].reshape(bias_extent, D)
    left = window.cut(jnp.concatenate([all_hidden, one_hot], 1), STARTS[1])
    condition = links.deliver(
        matmul("ir,rd->id", left, stem).reshape(links.count, images, D)
    ).sum(0)
    signal = jax.nn.silu(condition).astype(low)
    all_signal = links.spread(signal).reshape(everyone, D)
    signal_rows = lax.dynamic_slice_in_dim(all_signal, row_at, own_rows, 1)
    parts = links.deliver(
        matmul("ir,rc->ic", signal_rows, ada_low).reshape(links.count, images, own_cols)
    )
    modulation = (
        parts.reshape(-1, groups, images, own_cols).sum(0).transpose(1, 0, 2).reshape(images, 6 * D)
        + biases[3:].reshape(6 * D)
    ).astype(low)
    pieces = links.inner(modulation.astype(wide).reshape(images, 6, D))
    pieces = [pieces[:, part] for part in range(6)]
    final_part = window.put(matmul("id,rd->ir", all_signal, stem), STARTS[3], 2 * D)

    sched = plan(timesteps)
    target = noise.reshape(images, SEQ, PATCH)
    noisy_rows = (
        sched[:, 0][:, None, None] * latents.reshape(images, SEQ, PATCH)
        + sched[:, 1][:, None, None] * target
    ).astype(low)
    stream = matmul("isp,dp->isd", noisy_rows, w_patch) + links.inner(biases[0]) + links.inner(positions())[None]
    normed = modulate(stream, pieces[0], pieces[1]).astype(low)
    mixed, kept = [], []
    for half in range(2):
        rows, saved = attend(normed, w_qkv[half])
        mixed.append(rows)
        kept.append(saved)
    attended = sum(matmul("isd,od->iso", mixed[half], w_proj[half]) for half in range(2))
    middle = stream + pieces[2][:, None, :] * attended
    second = modulate(middle, pieces[3], pieces[4]).astype(low)
    second, final_part = lax.optimization_barrier((second, final_part))
    final_mod = links.deliver(final_part.reshape(links.count, images, 2 * D)).sum(0) + biases[
        1:3
    ].reshape(2 * D)
    final_mod = links.inner(final_mod.reshape(images, 2, D))
    final_shift, final_scale = final_mod[:, 0], final_mod[:, 1]
    inner, active, output = mlp_call(
        mlp_kernel, [second.reshape(images * SEQ, D)], w_mlp, [wide, low]
    )
    output = output.reshape(images, SEQ, D)
    layer_out = middle + pieces[5][:, None, :] * output
    final_normed = modulate(layer_out, final_shift, final_scale).astype(low)
    prediction = matmul("isd,do->iso", final_normed, w_head)
    loss_local, loss_back = jax.vjp(
        lambda predicted: loss_terms(predicted, target, sched), prediction
    )

    def tokens(rows):
        return rows.reshape(images * SEQ, rows.shape[-1])

    def with_partner(first, second=None):
        if second is None:
            mine, sent = tokens(first), tokens(first)
        else:
            first, second = tokens(first), tokens(second)
            mine, sent = pick(core, first, second), pick(core, second, first)
        return jnp.concatenate([mine, links.send(sent, "c")], 0)

    def half_with_partner(rows):
        rows = rows.reshape(images, SEQ, -1)
        return with_partner(rows[..., : FF // 2], rows[..., FF // 2 :])

    def sum_near(rows):
        return lax.psum_scatter(rows, ("x", "y"), scatter_dimension=0, tiled=True)

    def sum_far(rows):
        return lax.psum_scatter(rows, "z", scatter_dimension=0, tiled=True)

    def together(*values):
        return lax.optimization_barrier(values)

    out_grad = loss_back(jnp.ones_like(loss_local))[0].astype(low)
    grad_head = matmul("iso,isd->do", out_grad, final_normed)
    upstream, shift_grad, scale_grad = modulate_back(
        layer_out, final_shift, final_scale, matmul("iso,do->isd", out_grad, w_head)
    )
    final_grad = links.outer(jnp.stack([shift_grad, scale_grad], 1)).reshape(images, 2 * D)
    down_in = (pieces[5][:, None, :] * upstream).astype(low)
    gate_b = jnp.sum(upstream * output, 1)
    active_both = half_with_partner(active)
    second_both = with_partner(second)
    mixed_both = with_partner(*mixed)
    normed_both = with_partner(normed)
    down_both = with_partner(down_in)
    inner_grad, second_grad = mlp_call(
        mlp_back_kernel, [tokens(down_in), inner], w_mlp, [low]
    )
    second_grad = second_grad.reshape(images, SEQ, D)
    inner_both = half_with_partner(inner_grad)
    inner_grad, down_both, active_both = together(inner_grad, down_both, active_both)
    grad_down = matmul("to,tf->of", down_both, active_both).astype(low)
    inner_both, grad_down = together(inner_both, grad_down)
    grad_up = matmul("td,tf->df", second_both, inner_both).astype(low)
    grad_mlp = jnp.concatenate([grad_up, grad_down], 1)
    second_grad, grad_mlp = together(second_grad, grad_mlp)
    near_mlp = sum_near(grad_mlp)
    back_mid, shift_b, scale_b = modulate_back(middle, pieces[3], pieces[4], second_grad)
    grad_mid = upstream + back_mid
    proj_in = (pieces[2][:, None, :] * grad_mid).astype(low)
    gate_a = jnp.sum(grad_mid * attended, 1)
    proj_both = with_partner(proj_in)
    final_low = final_grad.astype(low)
    early = links.outer(jnp.stack([gate_a, shift_b, scale_b, gate_b], 1)).reshape(images, 4 * D)
    early = early.astype(low)
    early = links.spread(jnp.concatenate([early, final_low], 1)).reshape(everyone, 6 * D)
    qkv_grad = [
        attend_back(kept[half], matmul("iso,od->isd", proj_in, w_proj[half])) for half in range(2)
    ]
    grad_proj = matmul("to,td->od", proj_both, mixed_both)
    qkv_both = with_partner(*qkv_grad)
    normed_grad = sum(matmul("ise,de->isd", qkv_grad[half], w_qkv[half]) for half in range(2))
    back_in, shift_a, scale_a = modulate_back(stream, pieces[0], pieces[1], normed_grad)
    stream_grad = grad_mid + back_in
    late = links.outer(jnp.stack([shift_a, scale_a], 1)).reshape(images, 2 * D).astype(low)
    late, stream_grad, qkv_both, early = together(late, stream_grad, qkv_both, early)
    late = links.spread(late).reshape(everyone, 2 * D)
    grad_qkv = matmul("td,te->de", normed_both, qkv_both)
    grad_patch = matmul("isp,isd->dp", noisy_rows, stream_grad.astype(low))
    small_grad = links.outer(jnp.concatenate([grad_patch, grad_head], 1).T).T
    small_grad = small_grad.reshape(links.count, -1)
    sums_of_attention = Reduction(links, [grad_qkv, grad_proj])
    more = sums_of_attention.send("yx")

    late, near_mlp = together(late, near_mlp)
    reduced_mlp = sum_far(near_mlp).astype(wide)
    all_final = early[:, 4 * D :]
    all_modulation = jnp.concatenate([late, early[:, : 4 * D]], 1)
    own_modulation = lax.dynamic_slice_in_dim(all_modulation, col_at, own_cols, 1)
    signal_part = matmul("ir,rd->id", window.cut(all_final, STARTS[3]), stem)
    ada_part = matmul("ic,rc->ir", own_modulation, ada_low)
    signal_part = lax.dynamic_update_slice_in_dim(
        signal_part,
        lax.dynamic_slice_in_dim(signal_part, row_at, own_rows, 1) + ada_part,
        row_at,
        1,
    )
    sums = jnp.concatenate([links.outer(jnp.sum(stream_grad, (0, 1))), jnp.sum(final_grad, 0)])
    share = -(-sums.shape[0] // links.count)
    sums = jnp.pad(sums, (0, share * links.count - sums.shape[0])).reshape(links.count, share)
    summed = links.deliver(
        jnp.concatenate([signal_part.reshape(links.count, images * D), sums, small_grad], 1)
    ).sum(0)
    small = summed[images * D + share :]
    condition_grad = smooth_back(jax.nn.silu, condition, summed[: images * D].reshape(images, D))
    spreading = jnp.concatenate([condition_grad.reshape(-1), summed[images * D : images * D + share]])
    spreading, more = together(spreading, more)
    sums_of_attention.add(more)
    more = sums_of_attention.send("xy")
    spread = links.spread(spreading)
    all_condition = spread[:, : images * D].reshape(everyone, D)
    all_sums = spread[:, images * D :].reshape(-1)[: 3 * D]
    condition_low = all_condition.astype(low)
    hidden_part = matmul("id,rd->ir", condition_low, stem)
    before_part = window.cut(all_before, STARTS[1])
    before_part = smooth_back(jax.nn.silu, before_part, hidden_part)
    row = window.first + jnp.arange(window.rows)
    before_part = jnp.where((row >= STARTS[1]) & (row < STARTS[2]), before_part, 0.0).astype(low)
    before_part, more = together(before_part, more)
    sums_of_attention.add(more)
    sums_of_attention.join()
    more = sums_of_attention.send("z")
    windows = links.spread(before_part)
    sums_of_attention.add(more)
    reduced_attention = sums_of_attention.result()
    square = (
        jnp.sum(reduced_attention * reduced_attention)
        + jnp.sum(reduced_mlp * reduced_mlp)
        + jnp.sum(small * small)
    )
    windows, square = together(windows, square)
    totals = links.spread(jnp.stack([loss_local, square])).sum(0)
    before_low = window.assemble(windows, STARTS[1], D).astype(low)
    joint = jnp.concatenate([reduced_attention, reduced_mlp], 1)
    block_grad = flat_gradient(links, joint, small)
    loss_total, squares = totals[0], totals[1]
    bias_rows = jnp.concatenate(
        [all_sums, jnp.sum(all_modulation.astype(wide), 0)]
    ).reshape(bias_extent, D)

    def product_squares(left, right):
        left, right = left.astype(wide), right.astype(wide)
        grams = [jnp.dot(rows, rows.T, precision=HIGHEST_PRECISION) for rows in (left, right)]
        return jnp.sum(grams[0] * grams[1])

    squares = (
        squares
        + product_squares(all_signal, all_modulation)
        + product_squares(all_signal, all_final)
        + product_squares(one_hot, all_condition)
        + product_squares(all_hidden, condition_low)
        + product_squares(timing, before_low)
        + jnp.sum(bias_rows * bias_rows)
    )
    ada_grad = matmul("ir,ic->rc", signal_rows, own_modulation)
    low_left = jnp.concatenate(
        [
            window.cut(timing, STARTS[0]),
            window.cut(all_hidden, STARTS[1]),
            window.cut(all_final, STARTS[3]),
        ],
        0,
    )
    low_right = jnp.concatenate([before_low, condition_low, all_signal], 0)
    stem_rows = matmul("ir,id->rd", low_left, low_right)
    wide_left = jnp.concatenate(
        [window.cut(one_hot.astype(wide), STARTS[2]), mark.astype(wide)], 0
    )
    wide_right = jnp.concatenate([all_condition, bias_rows], 0)
    stem_rows = stem_rows + jnp.dot(wide_left.T, wide_right, precision=HIGHEST_PRECISION)
    stem_grad = window.flatten(stem_rows)
    grad_norm = jnp.sqrt(squares)
    factor = THRESHOLD / jnp.maximum(grad_norm, THRESHOLD)
    block_new = adam_update(block_master, block_grad * factor, block_m, block_v)
    stem_new = adam_update(stem_master, stem_grad * factor, stem_m, stem_v)
    ada_new = adam_update(ada_w, ada_grad * factor, ada_w_m, ada_w_v)
    return (loss_total, grad_norm, *block_new, *stem_new, *ada_new)


def solution(mesh):
    links = Links(mesh.shape["dp"], mesh.shape["mod"])
    grid = jax.sharding.Mesh(
        mesh.devices.reshape(links.z, links.x, links.y, links.core), AXES
    )
    flat, rows, ada = P(AXES), P(AXES, None), P(("z", "x"), ("y", "c"))
    return jax.shard_map(
        functools.partial(shards, links),
        mesh=grid,
        in_specs=(rows, rows) + (flat,) * 9 + (ada,) * 3,
        out_specs=(P(), P()) + (flat,) * 6 + (ada,) * 3,
        check_vma=False,
    )
```

```python
import functools
import math

import jax
import jax.numpy as jnp
from jax import lax
from jax.experimental import pallas as pl
from jax.experimental.pallas import tpu as pltpu
from jax.sharding import PartitionSpec as P

D = 1152
HEADS = 16
HEAD_DIM = 72
FF = 4608
CLASSES = 1000
PATCH = 16
GRID = 16
FREQ = 256
TSTEPS = 1000
STEP = 10
SEQ = 256
WB = 13872
SMALL = 3 * PATCH
SROWS = 4722


HIGHEST_PRECISION = lax.Precision.HIGHEST
AXES = ("z", "x", "y", "c")
LOG_TWO = math.log(2.0)
THRESHOLD = 1.0
LEARN_RATE = 0.05
BETA_ONE = 0.9
BETA_TWO = 0.999
EPSILON = 1e-08


def matmul(form, left, right):
    return jnp.einsum(form, left, right, preferred_element_type=jnp.float32)


def plan(steps):
    step_index = jnp.arange(TSTEPS).astype(jnp.float32)
    beta_rows = 0.0001 + (0.02 - 0.0001) * step_index / (TSTEPS - 1)
    alpha_bar = jnp.cumprod(1.0 - beta_rows)
    previous = jnp.concatenate([jnp.ones((1,), jnp.float32), alpha_bar[:-1]])
    posterior = beta_rows * (1.0 - previous) / (1.0 - alpha_bar)
    clipped = jnp.concatenate([posterior[1:2], posterior[1:]])
    mean_factor = beta_rows * beta_rows * previous / ((1.0 - alpha_bar) * alpha_bar)
    plan_table = jnp.stack(
        [
            jnp.sqrt(alpha_bar),
            jnp.sqrt(1.0 - alpha_bar),
            mean_factor,
            jnp.log(clipped),
            jnp.log(beta_rows),
        ],
        1,
    )
    one_hot = (steps[:, None] == jnp.arange(TSTEPS)[None, :]).astype(jnp.float32)
    return jnp.dot(one_hot, plan_table, precision=HIGHEST_PRECISION)


def positions():
    quarter = D // 4
    omegas = 1.0 / 10000.0 ** (jnp.arange(quarter).astype(jnp.float32) / quarter)
    cells = jnp.arange(SEQ)
    column_angle = (cells % GRID).astype(jnp.float32)[:, None] * omegas[None, :]
    row_angle = (cells // GRID).astype(jnp.float32)[:, None] * omegas[None, :]
    return jnp.concatenate(
        [jnp.sin(column_angle), jnp.cos(column_angle), jnp.sin(row_angle), jnp.cos(row_angle)], 1
    )


def frequencies(steps):
    half_count = FREQ // 2
    frequency = jnp.exp(
        -math.log(10000.0) * jnp.arange(half_count).astype(jnp.float32) / half_count
    )
    angles = steps.astype(jnp.float32)[:, None] * frequency[None, :]
    return jnp.concatenate([jnp.cos(angles), jnp.sin(angles)], 1)


def modulate(stream, shifts, scales):
    average = jnp.mean(stream, -1, keepdims=True)
    centred = stream - average
    variance = jnp.mean(centred * centred, -1, keepdims=True)
    return centred * lax.rsqrt(variance + 1e-06) * (1.0 + scales[:, None, :]) + shifts[:, None, :]


def modulate_back(stream, shifts, scales, cotangent):
    unused, pullback = jax.vjp(modulate, stream, shifts, scales)
    return pullback(cotangent)


def smooth_back(function, inputs, cotangent):
    unused, pullback = jax.vjp(function, inputs)
    return pullback(cotangent)[0]


def gelu_tanh(inputs):
    return jax.nn.gelu(inputs, approximate=True)


def loss_terms(prediction, target, sched):
    guessed = prediction[..., :PATCH]
    variance_raw = prediction[..., PATCH:]
    mean_factor = sched[:, 2][:, None, None]
    posterior_log = sched[:, 3][:, None, None]
    beta_log = sched[:, 4][:, None, None]
    blend = 0.5 * (variance_raw + 1.0)
    model_log = blend * beta_log + (1.0 - blend) * posterior_log
    errors = guessed - target
    bound_term = 0.5 * (
        -1.0
        + model_log
        - posterior_log
        + jnp.exp(posterior_log - model_log)
        + mean_factor * errors * errors * jnp.exp(-model_log)
    )
    return jnp.sum(errors * errors + bound_term / LOG_TWO)


class Links:
    def __init__(self, dp, mod):
        self.core = 2 if mod % 2 == 0 else 1
        self.y = mod // self.core
        self.x = self.y if dp % self.y == 0 else 1
        self.z = dp // self.x
        self.count = dp * mod
        self.size = {"z": self.z, "x": self.x, "y": self.y, "c": self.core}
        self.dim = {"x": 0, "y": 1, "z": 2}

    def place(self, axis):
        index = lax.axis_index(AXES)
        below = {"c": 1, "y": self.core, "x": self.core * self.y, "z": self.core * self.y * self.x}
        return index // below[axis] % self.size[axis]

    def send(self, block, axis, shift=1):
        pairs = []
        for index in range(self.count):
            spot = {
                "c": index % self.core,
                "y": index // self.core % self.y,
                "x": index // (self.core * self.y) % self.x,
                "z": index // (self.core * self.y * self.x),
            }
            spot[axis] = (spot[axis] + shift) % self.size[axis]
            target = ((spot["z"] * self.x + spot["x"]) * self.y + spot["y"]) * self.core + spot["c"]
            pairs.append((index, target))
        return lax.ppermute(block, AXES, pairs)

    def inner(self, values):
        shape = (*values.shape[:-1], self.z, self.x * self.y, -1)
        return values.reshape(shape).swapaxes(-3, -2).reshape(values.shape)

    def outer(self, values):
        shape = (*values.shape[:-1], self.x * self.y, self.z, -1)
        return values.reshape(shape).swapaxes(-3, -2).reshape(values.shape)

    def spread(self, block):
        copies = jnp.broadcast_to(block[None], (self.count, *block.shape))
        return lax.all_to_all(copies, AXES, split_axis=0, concat_axis=0, tiled=True)

    def deliver(self, blocks):
        return lax.all_to_all(blocks, AXES, split_axis=0, concat_axis=0, tiled=True)


def pick(own, first, second):
    return jnp.where(own == 0, first, second)


def joined(own, mine, other, dim):
    return pick(
        own, jnp.concatenate([mine, other], dim), jnp.concatenate([other, mine], dim)
    )


def column_half(rows, half):
    small = D // 2
    attention = [rows[:, part * D + half * small : part * D + (half + 1) * small] for part in range(4)]
    wide = FF // 2
    return [
        jnp.concatenate(attention, 1),
        rows[:, 4 * D + half * wide : 4 * D + (half + 1) * wide],
        rows[:, 4 * D + FF + half * wide : 4 * D + FF + (half + 1) * wide],
    ]


def whole_columns(first, second):
    small = D // 2
    pieces = [
        half[0][:, part * small : (part + 1) * small] for part in range(4) for half in (first, second)
    ]
    return jnp.concatenate([*pieces, first[1], second[1], first[2], second[2]], 1)


def chip_rows(links, flat):
    core = links.place("c")
    per_chip = D * links.core // links.count
    if (D % links.count) == 0:
        rows = flat.reshape(D // links.count, WB).astype(jnp.bfloat16)
        halves = [jnp.concatenate(column_half(rows, half), 1) for half in range(2)]
        mine = pick(core, halves[0], halves[1])
        other = links.send(pick(core, halves[1], halves[0]), "c")
        return joined(core, mine, other, 0), rows[:, WB - SMALL :].reshape(-1)
    low = flat.astype(jnp.bfloat16)
    rows = joined(core, low, links.send(low, "c"), 0).reshape(per_chip, WB)
    halves = [jnp.concatenate(column_half(rows, half), 1) for half in range(2)]
    small = rows[:, WB - SMALL :].reshape(2, -1)
    return pick(core, halves[0], halves[1]), pick(core, small[0], small[1])


def gather_halves(rows):
    return lax.all_gather(rows, ("c", "x", "y", "z"), axis=0, tiled=True)


class Reduction:
    def __init__(self, links, gradients, kind=jnp.bfloat16):
        self.links, self.kind = links, kind
        shape = (links.x, links.y, links.z, D * links.core // links.count)
        self.blocks = [rows.reshape(*shape, -1) for rows in gradients]
        total = sum(rows.shape[1] for rows in gradients)
        middle = total // 256 * 128
        self.spans = [[], []]
        for index, rows in enumerate(gradients):
            before = sum(earlier.shape[1] for earlier in gradients[:index])
            edge = min(max(middle - before, 0), rows.shape[1])
            if edge > 0:
                self.spans[0].append((index, 0, edge))
            if edge < rows.shape[1]:
                self.spans[1].append((index, edge, rows.shape[1]))

    def cut(self, sources, axis, spot):
        dim = self.links.dim[axis]
        parts = [
            lax.dynamic_slice_in_dim(self.blocks[index][..., low:high], spot, 1, dim)
            for index, low, high in sources
        ]
        return jnp.concatenate(parts, 4) if len(parts) > 1 else parts[0]

    def send(self, order):
        self.order = order
        self.got = []
        for sources, axis in zip(self.spans, order):
            extent, own = self.links.size[axis], self.links.place(axis)
            for shift in range(1, extent):
                part = self.cut(sources, axis, (own + shift) % extent).astype(self.kind)
                self.got.append(self.links.send(part, axis, shift))
        return self.got

    def add(self, got):
        got = list(got)
        blocks, spans = [], []
        for sources, axis in zip(self.spans, self.order):
            extent, own = self.links.size[axis], self.links.place(axis)
            total = self.cut(sources, axis, own).astype(jnp.float32)
            for _ in range(1, extent):
                total = total + got.pop(0).astype(jnp.float32)
            spans.append([(len(blocks), 0, total.shape[-1])])
            blocks.append(total)
        self.blocks, self.spans = blocks, spans

    def join(self):
        self.spans = [[span for sources in self.spans for span in sources]]

    def result(self):
        return self.blocks[0].reshape(-1, self.blocks[0].shape[-1])


def flat_gradient(links, joint, small):
    core = links.place("c")
    edges = [0, 2 * D, 4 * D, 6 * D]
    split = lambda rows: [rows[:, edges[part] : edges[part + 1]] for part in range(3)]
    per_device = D // links.count
    if (D % links.count) == 0:
        mine = lax.dynamic_slice_in_dim(joint, core * per_device, per_device, 0)
        sent = lax.dynamic_slice_in_dim(joint, (1 - core) * per_device, per_device, 0)
    else:
        mine, sent = joint, joint
        small = joined(core, small, links.send(small, "c"), 0)
    other = links.send(sent, "c")
    columns = whole_columns(split(pick(core, mine, other)), split(pick(core, other, mine)))
    flat = jnp.concatenate([columns, small.reshape(-1, SMALL)], 1).reshape(-1)
    if (D % links.count) == 0:
        return flat
    part = flat.shape[0] // 2
    return lax.dynamic_slice_in_dim(flat, core * part, part)


EXTENTS = [FREQ, D, CLASSES + 1, 2 * D, 1, 2, 6]
STARTS = [sum(EXTENTS[:index]) for index in range(len(EXTENTS) + 1)]


class Window:
    def __init__(self, links, length):
        self.length = length
        begins = [index * length for index in range(links.count)]
        rows = max((begin % D + length + D - 1) // D for begin in begins)
        self.rows = (rows + 15) // 16 * 16
        begin = lax.axis_index(AXES) * length
        self.first = begin // D
        self.firsts = [start // D for start in begins]
        self.offset = begin - self.first * D

    def fill(self, flat):
        padded = jnp.concatenate(
            [jnp.zeros((D,), flat.dtype), flat, jnp.zeros((self.rows * D,), flat.dtype)]
        )
        return lax.dynamic_slice_in_dim(padded, D - self.offset, self.rows * D).reshape(
            self.rows, D
        )

    def cut(self, columns, start):
        full = jnp.pad(columns, ((0, 0), (start, SROWS + self.rows - start - columns.shape[1])))
        return lax.dynamic_slice_in_dim(full, self.first, self.rows, 1)

    def put(self, columns, start, extent):
        full = jnp.zeros((columns.shape[0], SROWS + self.rows), columns.dtype)
        full = lax.dynamic_update_slice_in_dim(full, columns, self.first, 1)
        return full[:, start : start + extent]

    def assemble(self, windows, start, extent):
        inside = [
            index
            for index, first in enumerate(self.firsts)
            if first < start + extent and first + self.rows > start
        ]
        low, high = inside[0], inside[-1] + 1
        firsts = jnp.array(self.firsts[low:high])
        rows = firsts[:, None] + jnp.arange(self.rows)[None, :]
        chosen = jnp.arange(extent)[:, None, None] + start == rows[None]
        return matmul("kir,dkr->id", windows[low:high], chosen.astype(windows.dtype))

    def flatten(self, rows):
        return lax.dynamic_slice_in_dim(rows.reshape(-1), self.offset, self.length)


def adam_update(weight, gradient, first, second):
    first_new = BETA_ONE * first + (1.0 - BETA_ONE) * gradient
    second_new = BETA_TWO * second + (1.0 - BETA_TWO) * gradient * gradient
    corrected = first_new / (1.0 - BETA_ONE**STEP)
    spread = jnp.sqrt(second_new / (1.0 - BETA_TWO**STEP))
    return (weight - LEARN_RATE * corrected / (spread + EPSILON), first_new, second_new)


def attend(normed, w_qkv):
    images = normed.shape[0]
    heads = HEADS // 2
    low = jnp.bfloat16
    triple = matmul("isd,de->ise", normed, w_qkv).astype(low)
    triple = triple.reshape(images, SEQ, 3, heads, HEAD_DIM)
    queries, keys, values = triple[:, :, 0], triple[:, :, 1], triple[:, :, 2]
    scores = matmul("iqhe,ikhe->ihqk", queries, keys) * (1.0 / math.sqrt(HEAD_DIM))
    totals = jax.nn.logsumexp(scores, axis=-1)
    weights = jnp.exp(scores - totals[..., None]).astype(low)
    mixed = matmul("ihqk,ikhe->iqhe", weights, values).astype(low)
    return mixed.reshape(images, SEQ, D // 2), (queries, keys, values, totals)


def attend_back(kept, mixed_grad):
    queries, keys, values, totals = kept
    images = queries.shape[0]
    low = jnp.bfloat16
    mixed_grad = mixed_grad.astype(low).reshape(images, SEQ, HEADS // 2, HEAD_DIM)
    score_scale = 1.0 / math.sqrt(HEAD_DIM)
    softmax_rows = jnp.exp(
        matmul("iqhe,ikhe->ihqk", queries, keys) * score_scale - totals[..., None]
    )
    weight_grad = matmul("iqhe,ikhe->ihqk", mixed_grad, values)
    score_grad = (
        softmax_rows * (weight_grad - jnp.sum(weight_grad * softmax_rows, -1, keepdims=True))
    ).astype(low)
    query_grad = (matmul("ihqk,ikhe->iqhe", score_grad, keys) * score_scale).astype(low)
    key_grad = (matmul("ihqk,iqhe->ikhe", score_grad, queries) * score_scale).astype(low)
    value_grad = matmul("ihqk,iqhe->ikhe", softmax_rows.astype(low), mixed_grad).astype(low)
    return jnp.stack([query_grad, key_grad, value_grad], 2).reshape(images, SEQ, 3 * D // 2)


def accumulate(total_ref, part):
    @pl.when(pl.program_id(0) == 0)
    def _():
        total_ref[...] = part

    @pl.when(pl.program_id(0) > 0)
    def _():
        total_ref[...] += part


def product(left, right, dims):
    return lax.dot_general(left, right, (dims, ((), ())), preferred_element_type=jnp.float32)


def up_kernel(rows_ref, up_ref, inner_ref, active_ref):
    inner = product(rows_ref[...], up_ref[...], ((1,), (0,)))
    inner_ref[...] = inner
    active_ref[...] = gelu_tanh(inner).astype(jnp.bfloat16)


def down_kernel(active_ref, down_ref, total_ref):
    accumulate(total_ref, product(active_ref[...], down_ref[...], ((1,), (1,))))


def mlp_back_kernel(rows_ref, inner_ref, up_ref, down_ref, grad_ref, total_ref):
    back = product(rows_ref[...], down_ref[...], ((1,), (0,)))
    grad = smooth_back(gelu_tanh, inner_ref[...], back).astype(jnp.bfloat16)
    grad_ref[...] = grad
    accumulate(total_ref, product(grad, up_ref[...], ((1,), (1,))))


def mlp_call(kernel, operands, weights, outputs):
    per_half = FF // 2 // D
    rows = operands[0].shape[0]

    def spec(width):
        return pl.BlockSpec((rows, D), (lambda step: (0, step)) if width == FF else (lambda step: (0, 0)))

    def weight_spec(weight):
        before = weight.shape[1] // D - per_half
        return pl.BlockSpec((D, D), lambda step: (step // per_half, before + step % per_half))

    return pl.pallas_call(
        kernel,
        grid=(FF // D,),
        in_specs=[spec(rows_in.shape[1]) for rows_in in operands]
        + [weight_spec(weight) for weight in weights],
        out_specs=[spec(width) for width, _ in outputs],
        out_shape=[jax.ShapeDtypeStruct((rows, width), kind) for width, kind in outputs],
        compiler_params=pltpu.CompilerParams(vmem_limit_bytes=52 * 1024 * 1024),
        cost_estimate=pl.CostEstimate(
            flops=2 * len(weights) * rows * D * FF,
            bytes_accessed=len(weights) * 2 * D * FF + 3 * rows * FF,
            transcendentals=rows * FF,
        ),
    )(*operands, *weights)


def shards(
    links,
    latents,
    noise,
    timesteps,
    labels,
    dropped,
    block_master,
    block_m,
    block_v,
    stem_master,
    stem_m,
    stem_v,
    ada_w,
    ada_w_m,
    ada_w_v,
):
    low, wide = jnp.bfloat16, jnp.float32
    images = timesteps.shape[0]
    everyone = links.count * images
    own_cols = ada_w.shape[1]
    own_rows = ada_w.shape[0]
    row_at = lax.axis_index(("z", "x")) * own_rows
    col_at = lax.axis_index(("y", "c")) * own_cols
    groups = 6 * D // own_cols

    core = links.place("c")
    chunks, small = chip_rows(links, block_master)
    w_early = gather_halves(chunks[:, : 4 * D])
    w_attention = [w_early[:D, : 2 * D], w_early[D:, : 2 * D]]
    w_down = gather_halves(chunks[:, 4 * D :])
    w_qkv = [half[:, : 3 * D // 2] for half in w_attention]
    w_proj = [half[:, 3 * D // 2 :] for half in w_attention]

    window = Window(links, stem_master.shape[0])
    stem = window.fill(stem_master.astype(low))
    ada_low = ada_w.astype(low)
    integers = jnp.stack([timesteps, jnp.where(dropped == 1, CLASSES, labels)])
    digits = jnp.stack([integers // 32, integers % 32]).astype(low).reshape(-1)
    got = links.spread(jnp.concatenate([digits, small]))
    digits = got[:, : 4 * images].astype(jnp.int32).reshape(links.count, 2, 2, images)
    integers = digits[:, 0] * 32 + digits[:, 1]
    small = links.inner(got[:, 4 * images :].reshape(D, SMALL).T).T
    w_patch, w_head = small[:, :PATCH], small[:, PATCH:]
    all_steps = integers[:, 0].reshape(everyone)
    chosen = integers[:, 1].reshape(everyone)
    timing = frequencies(all_steps).astype(low)
    one_hot = (chosen[:, None] == jnp.arange(CLASSES + 1)[None, :]).astype(low)
    bias_start, bias_extent = STARTS[4], 9
    bias_share = -(-bias_extent * D // links.count)
    mark = jnp.arange(bias_extent)[:, None] + bias_start == (
        window.first + jnp.arange(window.rows)
    )
    bias_part = matmul("br,rd->bd", mark.astype(low), stem).reshape(bias_extent * D)
    bias_part = jnp.pad(bias_part, (0, bias_share * links.count - bias_extent * D))

    before_part = matmul("ir,rd->id", window.cut(timing, STARTS[0]), stem)
    got = links.deliver(
        jnp.concatenate(
            [
                before_part.reshape(links.count, images * D),
                bias_part.reshape(links.count, bias_share),
            ],
            1,
        )
    ).sum(0)
    got = links.spread(got)
    all_before = got[:, : images * D].reshape(everyone, D)
    all_hidden = jax.nn.silu(all_before).astype(low)
    biases = got[:, images * D :].reshape(-1)[: bias_extent * D].reshape(bias_extent, D)
    left = window.cut(jnp.concatenate([all_hidden, one_hot], 1), STARTS[1])
    condition = links.deliver(
        matmul("ir,rd->id", left, stem).reshape(links.count, images, D)
    ).sum(0)
    signal = jax.nn.silu(condition).astype(low)
    all_signal = links.spread(signal).reshape(everyone, D)
    signal_rows = lax.dynamic_slice_in_dim(all_signal, row_at, own_rows, 1)
    parts = links.deliver(
        matmul("ir,rc->ic", signal_rows, ada_low).reshape(links.count, images, own_cols)
    )
    modulation = (
        parts.reshape(-1, groups, images, own_cols).sum(0).transpose(1, 0, 2).reshape(images, 6 * D)
        + biases[3:].reshape(6 * D)
    ).astype(low)
    pieces = links.inner(modulation.astype(wide).reshape(images, 6, D))
    pieces = [pieces[:, part] for part in range(6)]
    final_part = window.put(matmul("id,rd->ir", all_signal, stem), STARTS[3], 2 * D)

    sched = plan(timesteps)
    target = noise.reshape(images, SEQ, PATCH)
    noisy_rows = (
        sched[:, 0][:, None, None] * latents.reshape(images, SEQ, PATCH)
        + sched[:, 1][:, None, None] * target
    ).astype(low)
    stream = matmul("isp,dp->isd", noisy_rows, w_patch) + links.inner(biases[0]) + links.inner(positions())[None]
    normed = modulate(stream, pieces[0], pieces[1]).astype(low)
    mixed, kept = [], []
    for half in range(2):
        rows, saved = attend(normed, w_qkv[half])
        mixed.append(rows)
        kept.append(saved)
    attended = sum(matmul("isd,od->iso", mixed[half], w_proj[half]) for half in range(2))
    middle = stream + pieces[2][:, None, :] * attended
    second = modulate(middle, pieces[3], pieces[4]).astype(low)
    second, final_part = lax.optimization_barrier((second, final_part))
    final_mod = links.deliver(final_part.reshape(links.count, images, 2 * D)).sum(0) + biases[
        1:3
    ].reshape(2 * D)
    final_mod = links.inner(final_mod.reshape(images, 2, D))
    final_shift, final_scale = final_mod[:, 0], final_mod[:, 1]
    inner, active = mlp_call(
        up_kernel, [second.reshape(images * SEQ, D)], [w_early], [(FF, wide), (FF, low)]
    )
    (output,) = mlp_call(down_kernel, [active], [w_down], [(D, wide)])
    output = output.reshape(images, SEQ, D)
    layer_out = middle + pieces[5][:, None, :] * output
    final_normed = modulate(layer_out, final_shift, final_scale).astype(low)
    prediction = matmul("isd,do->iso", final_normed, w_head)
    loss_local, loss_back = jax.vjp(
        lambda predicted: loss_terms(predicted, target, sched), prediction
    )

    def tokens(rows):
        return rows.reshape(images * SEQ, rows.shape[-1])

    def with_partner(first, second=None):
        if second is None:
            mine, sent = tokens(first), tokens(first)
        else:
            first, second = tokens(first), tokens(second)
            mine, sent = pick(core, first, second), pick(core, second, first)
        return jnp.concatenate([mine, links.send(sent, "c")], 0)

    def half_with_partner(rows):
        rows = rows.reshape(images, SEQ, -1)
        return with_partner(rows[..., : FF // 2], rows[..., FF // 2 :])

    def sum_near(rows):
        return lax.psum_scatter(rows, ("x", "y"), scatter_dimension=0, tiled=True)

    def sum_far(rows):
        return lax.psum_scatter(rows, "z", scatter_dimension=0, tiled=True)

    def together(*values):
        return lax.optimization_barrier(values)

    out_grad = loss_back(jnp.ones_like(loss_local))[0].astype(low)
    grad_head = matmul("iso,isd->do", out_grad, final_normed)
    upstream, shift_grad, scale_grad = modulate_back(
        layer_out, final_shift, final_scale, matmul("iso,do->isd", out_grad, w_head)
    )
    final_grad = links.outer(jnp.stack([shift_grad, scale_grad], 1)).reshape(images, 2 * D)
    down_in = (pieces[5][:, None, :] * upstream).astype(low)
    gate_b = jnp.sum(upstream * output, 1)
    active_both = half_with_partner(active)
    second_both = with_partner(second)
    mixed_both = with_partner(*mixed)
    normed_both = with_partner(normed)
    down_both = with_partner(down_in)
    inner_grad, second_grad = mlp_call(
        mlp_back_kernel, [tokens(down_in), inner], [w_early, w_down], [(FF, low), (D, wide)]
    )
    second_grad = second_grad.reshape(images, SEQ, D)
    inner_both = half_with_partner(inner_grad)
    inner_grad, down_both, active_both = together(inner_grad, down_both, active_both)
    grad_down = matmul("to,tf->of", down_both, active_both).astype(low)
    inner_both, grad_down = together(inner_both, grad_down)
    grad_up = matmul("td,tf->df", second_both, inner_both).astype(low)
    grad_mlp = jnp.concatenate([grad_up, grad_down], 1)
    second_grad, grad_mlp = together(second_grad, grad_mlp)
    near_mlp = sum_near(grad_mlp)
    back_mid, shift_b, scale_b = modulate_back(middle, pieces[3], pieces[4], second_grad)
    grad_mid = upstream + back_mid
    proj_in = (pieces[2][:, None, :] * grad_mid).astype(low)
    gate_a = jnp.sum(grad_mid * attended, 1)
    proj_both = with_partner(proj_in)
    final_low = final_grad.astype(low)
    early = links.outer(jnp.stack([gate_a, shift_b, scale_b, gate_b], 1)).reshape(images, 4 * D)
    early = early.astype(low)
    early = links.spread(jnp.concatenate([early, final_low], 1)).reshape(everyone, 6 * D)
    qkv_grad = [
        attend_back(kept[half], matmul("iso,od->isd", proj_in, w_proj[half])) for half in range(2)
    ]
    grad_proj = matmul("to,td->od", proj_both, mixed_both)
    qkv_both = with_partner(*qkv_grad)
    normed_grad = sum(matmul("ise,de->isd", qkv_grad[half], w_qkv[half]) for half in range(2))
    back_in, shift_a, scale_a = modulate_back(stream, pieces[0], pieces[1], normed_grad)
    stream_grad = grad_mid + back_in
    late = links.outer(jnp.stack([shift_a, scale_a], 1)).reshape(images, 2 * D).astype(low)
    late, stream_grad, qkv_both, early = together(late, stream_grad, qkv_both, early)
    late = links.spread(late).reshape(everyone, 2 * D)
    grad_qkv = matmul("td,te->de", normed_both, qkv_both)
    grad_patch = matmul("isp,isd->dp", noisy_rows, stream_grad.astype(low))
    small_grad = links.outer(jnp.concatenate([grad_patch, grad_head], 1).T).T
    small_grad = small_grad.reshape(links.count, -1)
    sums_of_attention = Reduction(links, [grad_qkv, grad_proj])
    more = sums_of_attention.send("yx")

    late, near_mlp = together(late, near_mlp)
    reduced_mlp = sum_far(near_mlp).astype(wide)
    all_final = early[:, 4 * D :]
    all_modulation = jnp.concatenate([late, early[:, : 4 * D]], 1)
    own_modulation = lax.dynamic_slice_in_dim(all_modulation, col_at, own_cols, 1)
    signal_part = matmul("ir,rd->id", window.cut(all_final, STARTS[3]), stem)
    ada_part = matmul("ic,rc->ir", own_modulation, ada_low)
    signal_part = lax.dynamic_update_slice_in_dim(
        signal_part,
        lax.dynamic_slice_in_dim(signal_part, row_at, own_rows, 1) + ada_part,
        row_at,
        1,
    )
    sums = jnp.concatenate([links.outer(jnp.sum(stream_grad, (0, 1))), jnp.sum(final_grad, 0)])
    share = -(-sums.shape[0] // links.count)
    sums = jnp.pad(sums, (0, share * links.count - sums.shape[0])).reshape(links.count, share)
    summed = links.deliver(
        jnp.concatenate([signal_part.reshape(links.count, images * D), sums, small_grad], 1)
    ).sum(0)
    small = summed[images * D + share :]
    condition_grad = smooth_back(jax.nn.silu, condition, summed[: images * D].reshape(images, D))
    spreading = jnp.concatenate([condition_grad.reshape(-1), summed[images * D : images * D + share]])
    spreading, more = together(spreading, more)
    sums_of_attention.add(more)
    more = sums_of_attention.send("xy")
    spread = links.spread(spreading)
    all_condition = spread[:, : images * D].reshape(everyone, D)
    all_sums = spread[:, images * D :].reshape(-1)[: 3 * D]
    condition_low = all_condition.astype(low)
    hidden_part = matmul("id,rd->ir", condition_low, stem)
    before_part = window.cut(all_before, STARTS[1])
    before_part = smooth_back(jax.nn.silu, before_part, hidden_part)
    row = window.first + jnp.arange(window.rows)
    before_part = jnp.where((row >= STARTS[1]) & (row < STARTS[2]), before_part, 0.0).astype(low)
    before_part, more = together(before_part, more)
    sums_of_attention.add(more)
    sums_of_attention.join()
    more = sums_of_attention.send("z")
    windows = links.spread(before_part)
    sums_of_attention.add(more)
    reduced_attention = sums_of_attention.result()
    square = (
        jnp.sum(reduced_attention * reduced_attention)
        + jnp.sum(reduced_mlp * reduced_mlp)
        + jnp.sum(small * small)
    )
    windows, square = together(windows, square)
    totals = links.spread(jnp.stack([loss_local, square])).sum(0)
    before_low = window.assemble(windows, STARTS[1], D).astype(low)
    joint = jnp.concatenate([reduced_attention, reduced_mlp], 1)
    block_grad = flat_gradient(links, joint, small)
    loss_total, squares = totals[0], totals[1]
    bias_rows = jnp.concatenate(
        [all_sums, jnp.sum(all_modulation.astype(wide), 0)]
    ).reshape(bias_extent, D)

    def product_squares(left, right):
        left, right = left.astype(wide), right.astype(wide)
        grams = [jnp.dot(rows, rows.T, precision=HIGHEST_PRECISION) for rows in (left, right)]
        return jnp.sum(grams[0] * grams[1])

    squares = (
        squares
        + product_squares(all_signal, all_modulation)
        + product_squares(all_signal, all_final)
        + product_squares(one_hot, all_condition)
        + product_squares(all_hidden, condition_low)
        + product_squares(timing, before_low)
        + jnp.sum(bias_rows * bias_rows)
    )
    ada_grad = matmul("ir,ic->rc", signal_rows, own_modulation)
    low_left = jnp.concatenate(
        [
            window.cut(timing, STARTS[0]),
            window.cut(all_hidden, STARTS[1]),
            window.cut(all_final, STARTS[3]),
        ],
        0,
    )
    low_right = jnp.concatenate([before_low, condition_low, all_signal], 0)
    stem_rows = matmul("ir,id->rd", low_left, low_right)
    wide_left = jnp.concatenate(
        [window.cut(one_hot.astype(wide), STARTS[2]), mark.astype(wide)], 0
    )
    wide_right = jnp.concatenate([all_condition, bias_rows], 0)
    stem_rows = stem_rows + jnp.dot(wide_left.T, wide_right, precision=HIGHEST_PRECISION)
    stem_grad = window.flatten(stem_rows)
    grad_norm = jnp.sqrt(squares)
    factor = THRESHOLD / jnp.maximum(grad_norm, THRESHOLD)
    block_new = adam_update(block_master, block_grad * factor, block_m, block_v)
    stem_new = adam_update(stem_master, stem_grad * factor, stem_m, stem_v)
    ada_new = adam_update(ada_w, ada_grad * factor, ada_w_m, ada_w_v)
    return (loss_total, grad_norm, *block_new, *stem_new, *ada_new)


def solution(mesh):
    links = Links(mesh.shape["dp"], mesh.shape["mod"])
    grid = jax.sharding.Mesh(
        mesh.devices.reshape(links.z, links.x, links.y, links.core), AXES
    )
    flat, rows, ada = P(AXES), P(AXES, None), P(("z", "x"), ("y", "c"))
    return jax.shard_map(
        functools.partial(shards, links),
        mesh=grid,
        in_specs=(rows, rows) + (flat,) * 9 + (ada,) * 3,
        out_specs=(P(), P()) + (flat,) * 6 + (ada,) * 3,
        check_vma=False,
    )
```

```python
import functools
import math

import jax
import jax.numpy as jnp
from jax import lax
from jax.experimental import pallas as pl
from jax.experimental.pallas import tpu as pltpu
from jax.sharding import PartitionSpec as P

D = 1152
HEADS = 16
HEAD_DIM = 72
FF = 4608
CLASSES = 1000
PATCH = 16
GRID = 16
FREQ = 256
TSTEPS = 1000
STEP = 10
SEQ = 256
WB = 13872
SMALL = 3 * PATCH
SROWS = 4722


HIGHEST_PRECISION = lax.Precision.HIGHEST
AXES = ("z", "x", "y", "c")
LOG_TWO = math.log(2.0)
THRESHOLD = 1.0
LEARN_RATE = 0.05
BETA_ONE = 0.9
BETA_TWO = 0.999
EPSILON = 1e-08


def matmul(form, left, right):
    return jnp.einsum(form, left, right, preferred_element_type=jnp.float32)


def plan(steps):
    step_index = jnp.arange(TSTEPS).astype(jnp.float32)
    beta_rows = 0.0001 + (0.02 - 0.0001) * step_index / (TSTEPS - 1)
    alpha_bar = jnp.cumprod(1.0 - beta_rows)
    previous = jnp.concatenate([jnp.ones((1,), jnp.float32), alpha_bar[:-1]])
    posterior = beta_rows * (1.0 - previous) / (1.0 - alpha_bar)
    clipped = jnp.concatenate([posterior[1:2], posterior[1:]])
    mean_factor = beta_rows * beta_rows * previous / ((1.0 - alpha_bar) * alpha_bar)
    plan_table = jnp.stack(
        [
            jnp.sqrt(alpha_bar),
            jnp.sqrt(1.0 - alpha_bar),
            mean_factor,
            jnp.log(clipped),
            jnp.log(beta_rows),
        ],
        1,
    )
    one_hot = (steps[:, None] == jnp.arange(TSTEPS)[None, :]).astype(jnp.float32)
    return jnp.dot(one_hot, plan_table, precision=HIGHEST_PRECISION)


def positions():
    quarter = D // 4
    omegas = 1.0 / 10000.0 ** (jnp.arange(quarter).astype(jnp.float32) / quarter)
    cells = jnp.arange(SEQ)
    column_angle = (cells % GRID).astype(jnp.float32)[:, None] * omegas[None, :]
    row_angle = (cells // GRID).astype(jnp.float32)[:, None] * omegas[None, :]
    return jnp.concatenate(
        [jnp.sin(column_angle), jnp.cos(column_angle), jnp.sin(row_angle), jnp.cos(row_angle)], 1
    )


def frequencies(steps):
    half_count = FREQ // 2
    frequency = jnp.exp(
        -math.log(10000.0) * jnp.arange(half_count).astype(jnp.float32) / half_count
    )
    angles = steps.astype(jnp.float32)[:, None] * frequency[None, :]
    return jnp.concatenate([jnp.cos(angles), jnp.sin(angles)], 1)


def modulate(stream, shifts, scales):
    average = jnp.mean(stream, -1, keepdims=True)
    centred = stream - average
    variance = jnp.mean(centred * centred, -1, keepdims=True)
    return centred * lax.rsqrt(variance + 1e-06) * (1.0 + scales[:, None, :]) + shifts[:, None, :]


def modulate_back(stream, shifts, scales, cotangent):
    unused, pullback = jax.vjp(modulate, stream, shifts, scales)
    return pullback(cotangent)


def smooth_back(function, inputs, cotangent):
    unused, pullback = jax.vjp(function, inputs)
    return pullback(cotangent)[0]


def gelu_tanh(inputs):
    return jax.nn.gelu(inputs, approximate=True)


def loss_terms(prediction, target, sched):
    guessed = prediction[..., :PATCH]
    variance_raw = prediction[..., PATCH:]
    mean_factor = sched[:, 2][:, None, None]
    posterior_log = sched[:, 3][:, None, None]
    beta_log = sched[:, 4][:, None, None]
    blend = 0.5 * (variance_raw + 1.0)
    model_log = blend * beta_log + (1.0 - blend) * posterior_log
    errors = guessed - target
    bound_term = 0.5 * (
        -1.0
        + model_log
        - posterior_log
        + jnp.exp(posterior_log - model_log)
        + mean_factor * errors * errors * jnp.exp(-model_log)
    )
    return jnp.sum(errors * errors + bound_term / LOG_TWO)


class Links:
    def __init__(self, dp, mod):
        self.core = 2 if mod % 2 == 0 else 1
        self.y = mod // self.core
        self.x = self.y if dp % self.y == 0 else 1
        self.z = dp // self.x
        self.count = dp * mod
        self.size = {"z": self.z, "x": self.x, "y": self.y, "c": self.core}
        self.dim = {"x": 0, "y": 1, "z": 2}

    def place(self, axis):
        index = lax.axis_index(AXES)
        below = {"c": 1, "y": self.core, "x": self.core * self.y, "z": self.core * self.y * self.x}
        return index // below[axis] % self.size[axis]

    def send(self, block, axis, shift=1):
        pairs = []
        for index in range(self.count):
            spot = {
                "c": index % self.core,
                "y": index // self.core % self.y,
                "x": index // (self.core * self.y) % self.x,
                "z": index // (self.core * self.y * self.x),
            }
            spot[axis] = (spot[axis] + shift) % self.size[axis]
            target = ((spot["z"] * self.x + spot["x"]) * self.y + spot["y"]) * self.core + spot["c"]
            pairs.append((index, target))
        return lax.ppermute(block, AXES, pairs)

    def inner(self, values):
        shape = (*values.shape[:-1], self.z, self.x * self.y, -1)
        return values.reshape(shape).swapaxes(-3, -2).reshape(values.shape)

    def outer(self, values):
        shape = (*values.shape[:-1], self.x * self.y, self.z, -1)
        return values.reshape(shape).swapaxes(-3, -2).reshape(values.shape)

    def spread(self, block):
        copies = jnp.broadcast_to(block[None], (self.count, *block.shape))
        return lax.all_to_all(copies, AXES, split_axis=0, concat_axis=0, tiled=True)

    def deliver(self, blocks):
        return lax.all_to_all(blocks, AXES, split_axis=0, concat_axis=0, tiled=True)


def pick(own, first, second):
    return jnp.where(own == 0, first, second)


def joined(own, mine, other, dim):
    return pick(
        own, jnp.concatenate([mine, other], dim), jnp.concatenate([other, mine], dim)
    )


def column_half(rows, half):
    small = D // 2
    attention = [rows[:, part * D + half * small : part * D + (half + 1) * small] for part in range(4)]
    wide = FF // 2
    return [
        jnp.concatenate(attention, 1),
        rows[:, 4 * D + half * wide : 4 * D + (half + 1) * wide],
        rows[:, 4 * D + FF + half * wide : 4 * D + FF + (half + 1) * wide],
    ]


def whole_columns(first, second):
    small = D // 2
    pieces = [
        half[0][:, part * small : (part + 1) * small] for part in range(4) for half in (first, second)
    ]
    return jnp.concatenate([*pieces, first[1], second[1], first[2], second[2]], 1)


def chip_rows(links, flat):
    core = links.place("c")
    per_chip = D * links.core // links.count
    if (D % links.count) == 0:
        rows = flat.reshape(D // links.count, WB).astype(jnp.bfloat16)
        halves = [jnp.concatenate(column_half(rows, half), 1) for half in range(2)]
        mine = pick(core, halves[0], halves[1])
        other = links.send(pick(core, halves[1], halves[0]), "c")
        return joined(core, mine, other, 0), rows[:, WB - SMALL :].reshape(-1)
    low = flat.astype(jnp.bfloat16)
    rows = joined(core, low, links.send(low, "c"), 0).reshape(per_chip, WB)
    halves = [jnp.concatenate(column_half(rows, half), 1) for half in range(2)]
    small = rows[:, WB - SMALL :].reshape(2, -1)
    return pick(core, halves[0], halves[1]), pick(core, small[0], small[1])


def gather_halves(rows):
    return lax.all_gather(rows, ("c", "x", "y", "z"), axis=0, tiled=True)


class Reduction:
    def __init__(self, links, gradients, kind=jnp.bfloat16):
        self.links, self.kind = links, kind
        shape = (links.x, links.y, links.z, D * links.core // links.count)
        self.blocks = [rows.reshape(*shape, -1) for rows in gradients]
        total = sum(rows.shape[1] for rows in gradients)
        middle = total // 256 * 128
        self.spans = [[], []]
        for index, rows in enumerate(gradients):
            before = sum(earlier.shape[1] for earlier in gradients[:index])
            edge = min(max(middle - before, 0), rows.shape[1])
            if edge > 0:
                self.spans[0].append((index, 0, edge))
            if edge < rows.shape[1]:
                self.spans[1].append((index, edge, rows.shape[1]))

    def cut(self, sources, axis, spot):
        dim = self.links.dim[axis]
        parts = [
            lax.dynamic_slice_in_dim(self.blocks[index][..., low:high], spot, 1, dim)
            for index, low, high in sources
        ]
        return jnp.concatenate(parts, 4) if len(parts) > 1 else parts[0]

    def send(self, order):
        self.order = order
        self.got = []
        for sources, axis in zip(self.spans, order):
            extent, own = self.links.size[axis], self.links.place(axis)
            for shift in range(1, extent):
                part = self.cut(sources, axis, (own + shift) % extent).astype(self.kind)
                self.got.append(self.links.send(part, axis, shift))
        return self.got

    def add(self, got):
        got = list(got)
        blocks, spans = [], []
        for sources, axis in zip(self.spans, self.order):
            extent, own = self.links.size[axis], self.links.place(axis)
            total = self.cut(sources, axis, own).astype(jnp.float32)
            for _ in range(1, extent):
                total = total + got.pop(0).astype(jnp.float32)
            spans.append([(len(blocks), 0, total.shape[-1])])
            blocks.append(total)
        self.blocks, self.spans = blocks, spans

    def join(self):
        self.spans = [[span for sources in self.spans for span in sources]]

    def result(self):
        return self.blocks[0].reshape(-1, self.blocks[0].shape[-1])


def flat_gradient(links, joint, small):
    core = links.place("c")
    edges = [0, 2 * D, 4 * D, 6 * D]
    split = lambda rows: [rows[:, edges[part] : edges[part + 1]] for part in range(3)]
    per_device = D // links.count
    if (D % links.count) == 0:
        mine = lax.dynamic_slice_in_dim(joint, core * per_device, per_device, 0)
        sent = lax.dynamic_slice_in_dim(joint, (1 - core) * per_device, per_device, 0)
    else:
        mine, sent = joint, joint
        small = joined(core, small, links.send(small, "c"), 0)
    other = links.send(sent, "c")
    columns = whole_columns(split(pick(core, mine, other)), split(pick(core, other, mine)))
    flat = jnp.concatenate([columns, small.reshape(-1, SMALL)], 1).reshape(-1)
    if (D % links.count) == 0:
        return flat
    part = flat.shape[0] // 2
    return lax.dynamic_slice_in_dim(flat, core * part, part)


EXTENTS = [FREQ, D, CLASSES + 1, 2 * D, 1, 2, 6]
STARTS = [sum(EXTENTS[:index]) for index in range(len(EXTENTS) + 1)]


class Window:
    def __init__(self, links, length):
        self.length = length
        begins = [index * length for index in range(links.count)]
        rows = max((begin % D + length + D - 1) // D for begin in begins)
        self.rows = (rows + 15) // 16 * 16
        begin = lax.axis_index(AXES) * length
        self.first = begin // D
        self.firsts = [start // D for start in begins]
        self.offset = begin - self.first * D

    def fill(self, flat):
        padded = jnp.concatenate(
            [jnp.zeros((D,), flat.dtype), flat, jnp.zeros((self.rows * D,), flat.dtype)]
        )
        return lax.dynamic_slice_in_dim(padded, D - self.offset, self.rows * D).reshape(
            self.rows, D
        )

    def cut(self, columns, start):
        full = jnp.pad(columns, ((0, 0), (start, SROWS + self.rows - start - columns.shape[1])))
        return lax.dynamic_slice_in_dim(full, self.first, self.rows, 1)

    def put(self, columns, start, extent):
        full = jnp.zeros((columns.shape[0], SROWS + self.rows), columns.dtype)
        full = lax.dynamic_update_slice_in_dim(full, columns, self.first, 1)
        return full[:, start : start + extent]

    def assemble(self, windows, start, extent):
        inside = [
            index
            for index, first in enumerate(self.firsts)
            if first < start + extent and first + self.rows > start
        ]
        low, high = inside[0], inside[-1] + 1
        firsts = jnp.array(self.firsts[low:high])
        rows = firsts[:, None] + jnp.arange(self.rows)[None, :]
        chosen = jnp.arange(extent)[:, None, None] + start == rows[None]
        return matmul("kir,dkr->id", windows[low:high], chosen.astype(windows.dtype))

    def flatten(self, rows):
        return lax.dynamic_slice_in_dim(rows.reshape(-1), self.offset, self.length)


def adam_update(weight, gradient, first, second):
    first_new = BETA_ONE * first + (1.0 - BETA_ONE) * gradient
    second_new = BETA_TWO * second + (1.0 - BETA_TWO) * gradient * gradient
    corrected = first_new / (1.0 - BETA_ONE**STEP)
    spread = jnp.sqrt(second_new / (1.0 - BETA_TWO**STEP))
    return (weight - LEARN_RATE * corrected / (spread + EPSILON), first_new, second_new)


def attend(normed, w_qkv):
    images = normed.shape[0]
    heads = HEADS // 2
    low = jnp.bfloat16
    triple = matmul("isd,de->ise", normed, w_qkv).astype(low)
    triple = triple.reshape(images, SEQ, 3, heads, HEAD_DIM)
    queries, keys, values = triple[:, :, 0], triple[:, :, 1], triple[:, :, 2]
    scores = matmul("iqhe,ikhe->ihqk", queries, keys) * (1.0 / math.sqrt(HEAD_DIM))
    totals = jax.nn.logsumexp(scores, axis=-1)
    weights = jnp.exp(scores - totals[..., None]).astype(low)
    mixed = matmul("ihqk,ikhe->iqhe", weights, values).astype(low)
    return mixed.reshape(images, SEQ, D // 2), (queries, keys, values, totals)


def attend_back(kept, mixed_grad):
    queries, keys, values, totals = kept
    images = queries.shape[0]
    low = jnp.bfloat16
    mixed_grad = mixed_grad.astype(low).reshape(images, SEQ, HEADS // 2, HEAD_DIM)
    score_scale = 1.0 / math.sqrt(HEAD_DIM)
    softmax_rows = jnp.exp(
        matmul("iqhe,ikhe->ihqk", queries, keys) * score_scale - totals[..., None]
    )
    weight_grad = matmul("iqhe,ikhe->ihqk", mixed_grad, values)
    score_grad = (
        softmax_rows * (weight_grad - jnp.sum(weight_grad * softmax_rows, -1, keepdims=True))
    ).astype(low)
    query_grad = (matmul("ihqk,ikhe->iqhe", score_grad, keys) * score_scale).astype(low)
    key_grad = (matmul("ihqk,iqhe->ikhe", score_grad, queries) * score_scale).astype(low)
    value_grad = matmul("ihqk,iqhe->ikhe", softmax_rows.astype(low), mixed_grad).astype(low)
    return jnp.stack([query_grad, key_grad, value_grad], 2).reshape(images, SEQ, 3 * D // 2)


def accumulate(total_ref, part):
    @pl.when(pl.program_id(0) == 0)
    def _():
        total_ref[...] = part

    @pl.when(pl.program_id(0) > 0)
    def _():
        total_ref[...] += part


def product(left, right, dims):
    return lax.dot_general(left, right, (dims, ((), ())), preferred_element_type=jnp.float32)


def mlp_kernel(rows_ref, up_ref, down_ref, inner_ref, active_ref, total_ref):
    inner = product(rows_ref[...], up_ref[...], ((1,), (0,)))
    inner_ref[...] = inner
    active = gelu_tanh(inner).astype(jnp.bfloat16)
    active_ref[...] = active
    accumulate(total_ref, product(active, down_ref[...], ((1,), (1,))))


def mlp_back_kernel(rows_ref, inner_ref, up_ref, down_ref, grad_ref, total_ref):
    back = product(rows_ref[...], down_ref[...], ((1,), (0,)))
    grad = smooth_back(gelu_tanh, inner_ref[...], back).astype(jnp.bfloat16)
    grad_ref[...] = grad
    accumulate(total_ref, product(grad, up_ref[...], ((1,), (1,))))


def mlp_call(kernel, operands, weights, outputs):
    count, per_half = FF // D, FF // 2 // D
    rows = operands[0].shape[0]
    whole = pl.BlockSpec((rows, D), lambda step: (0, 0))
    part = pl.BlockSpec((rows, D), lambda step: (0, step))
    up = pl.BlockSpec((D, D), lambda step: (step // per_half, step % per_half))
    down = pl.BlockSpec((D, D), lambda step: (step // per_half, per_half + step % per_half))
    return pl.pallas_call(
        kernel,
        grid=(count,),
        in_specs=[whole] + [part] * (len(operands) - 1) + [up, down],
        out_specs=[part] * len(outputs) + [whole],
        out_shape=[jax.ShapeDtypeStruct((rows, FF), kind) for kind in outputs]
        + [jax.ShapeDtypeStruct((rows, D), jnp.float32)],
        compiler_params=pltpu.CompilerParams(vmem_limit_bytes=52 * 1024 * 1024),
        cost_estimate=pl.CostEstimate(
            flops=4 * rows * D * FF, bytes_accessed=4 * D * FF + 6 * rows * FF, transcendentals=rows * FF
        ),
    )(*operands, weights, weights)


def shards(
    links,
    latents,
    noise,
    timesteps,
    labels,
    dropped,
    block_master,
    block_m,
    block_v,
    stem_master,
    stem_m,
    stem_v,
    ada_w,
    ada_w_m,
    ada_w_v,
):
    low, wide = jnp.bfloat16, jnp.float32
    images = timesteps.shape[0]
    everyone = links.count * images
    own_cols = ada_w.shape[1]
    own_rows = ada_w.shape[0]
    row_at = lax.axis_index(("z", "x")) * own_rows
    col_at = lax.axis_index(("y", "c")) * own_cols
    groups = 6 * D // own_cols

    core = links.place("c")
    chunks, small = chip_rows(links, block_master)
    w_attention = gather_halves(chunks[:, : 2 * D])
    w_attention = [w_attention[:D], w_attention[D:]]
    w_mlp = gather_halves(chunks[:, 2 * D :])
    w_qkv = [half[:, : 3 * D // 2] for half in w_attention]
    w_proj = [half[:, 3 * D // 2 :] for half in w_attention]

    window = Window(links, stem_master.shape[0])
    stem = window.fill(stem_master.astype(low))
    ada_low = ada_w.astype(low)
    integers = jnp.stack([timesteps, jnp.where(dropped == 1, CLASSES, labels)])
    digits = jnp.stack([integers // 32, integers % 32]).astype(low).reshape(-1)
    got = links.spread(jnp.concatenate([digits, small]))
    digits = got[:, : 4 * images].astype(jnp.int32).reshape(links.count, 2, 2, images)
    integers = digits[:, 0] * 32 + digits[:, 1]
    small = links.inner(got[:, 4 * images :].reshape(D, SMALL).T).T
    w_patch, w_head = small[:, :PATCH], small[:, PATCH:]
    all_steps = integers[:, 0].reshape(everyone)
    chosen = integers[:, 1].reshape(everyone)
    timing = frequencies(all_steps).astype(low)
    one_hot = (chosen[:, None] == jnp.arange(CLASSES + 1)[None, :]).astype(low)
    bias_start, bias_extent = STARTS[4], 9
    bias_share = -(-bias_extent * D // links.count)
    mark = jnp.arange(bias_extent)[:, None] + bias_start == (
        window.first + jnp.arange(window.rows)
    )
    bias_part = matmul("br,rd->bd", mark.astype(low), stem).reshape(bias_extent * D)
    bias_part = jnp.pad(bias_part, (0, bias_share * links.count - bias_extent * D))

    before_part = matmul("ir,rd->id", window.cut(timing, STARTS[0]), stem)
    got = links.deliver(
        jnp.concatenate(
            [
                before_part.reshape(links.count, images * D),
                bias_part.reshape(links.count, bias_share),
            ],
            1,
        )
    ).sum(0)
    got = links.spread(got)
    all_before = got[:, : images * D].reshape(everyone, D)
    all_hidden = jax.nn.silu(all_before).astype(low)
    biases = got[:, images * D :].reshape(-1)[: bias_extent * D].reshape(bias_extent, D)
    left = window.cut(jnp.concatenate([all_hidden, one_hot], 1), STARTS[1])
    condition = links.deliver(
        matmul("ir,rd->id", left, stem).reshape(links.count, images, D)
    ).sum(0)
    signal = jax.nn.silu(condition).astype(low)
    all_signal = links.spread(signal).reshape(everyone, D)
    signal_rows = lax.dynamic_slice_in_dim(all_signal, row_at, own_rows, 1)
    parts = links.deliver(
        matmul("ir,rc->ic", signal_rows, ada_low).reshape(links.count, images, own_cols)
    )
    modulation = (
        parts.reshape(-1, groups, images, own_cols).sum(0).transpose(1, 0, 2).reshape(images, 6 * D)
        + biases[3:].reshape(6 * D)
    ).astype(low)
    pieces = links.inner(modulation.astype(wide).reshape(images, 6, D))
    pieces = [pieces[:, part] for part in range(6)]
    final_part = window.put(matmul("id,rd->ir", all_signal, stem), STARTS[3], 2 * D)

    sched = plan(timesteps)
    target = noise.reshape(images, SEQ, PATCH)
    noisy_rows = (
        sched[:, 0][:, None, None] * latents.reshape(images, SEQ, PATCH)
        + sched[:, 1][:, None, None] * target
    ).astype(low)
    stream = matmul("isp,dp->isd", noisy_rows, w_patch) + links.inner(biases[0]) + links.inner(positions())[None]
    normed = modulate(stream, pieces[0], pieces[1]).astype(low)
    mixed, kept = [], []
    for half in range(2):
        rows, saved = attend(normed, w_qkv[half])
        mixed.append(rows)
        kept.append(saved)
    attended = sum(matmul("isd,od->iso", mixed[half], w_proj[half]) for half in range(2))
    middle = stream + pieces[2][:, None, :] * attended
    second = modulate(middle, pieces[3], pieces[4]).astype(low)
    second, final_part = lax.optimization_barrier((second, final_part))
    final_mod = links.deliver(final_part.reshape(links.count, images, 2 * D)).sum(0) + biases[
        1:3
    ].reshape(2 * D)
    final_mod = links.inner(final_mod.reshape(images, 2, D))
    final_shift, final_scale = final_mod[:, 0], final_mod[:, 1]
    inner, active, output = mlp_call(
        mlp_kernel, [second.reshape(images * SEQ, D)], w_mlp, [wide, low]
    )
    output = output.reshape(images, SEQ, D)
    layer_out = middle + pieces[5][:, None, :] * output
    final_normed = modulate(layer_out, final_shift, final_scale).astype(low)
    prediction = matmul("isd,do->iso", final_normed, w_head)
    loss_local, loss_back = jax.vjp(
        lambda predicted: loss_terms(predicted, target, sched), prediction
    )

    def tokens(rows):
        return rows.reshape(images * SEQ, rows.shape[-1])

    def with_partner(first, second=None):
        if second is None:
            mine, sent = tokens(first), tokens(first)
        else:
            first, second = tokens(first), tokens(second)
            mine, sent = pick(core, first, second), pick(core, second, first)
        return jnp.concatenate([mine, links.send(sent, "c")], 0)

    def half_with_partner(rows):
        rows = rows.reshape(images, SEQ, -1)
        return with_partner(rows[..., : FF // 2], rows[..., FF // 2 :])

    def sum_near(rows):
        return lax.psum_scatter(rows, ("x", "y"), scatter_dimension=0, tiled=True)

    def sum_far(rows):
        return lax.psum_scatter(rows, "z", scatter_dimension=0, tiled=True)

    def together(*values):
        return lax.optimization_barrier(values)

    out_grad = loss_back(jnp.ones_like(loss_local))[0].astype(low)
    grad_head = matmul("iso,isd->do", out_grad, final_normed)
    upstream, shift_grad, scale_grad = modulate_back(
        layer_out, final_shift, final_scale, matmul("iso,do->isd", out_grad, w_head)
    )
    final_grad = links.outer(jnp.stack([shift_grad, scale_grad], 1)).reshape(images, 2 * D)
    down_in = (pieces[5][:, None, :] * upstream).astype(low)
    gate_b = jnp.sum(upstream * output, 1)
    active_both = half_with_partner(active)
    second_both = with_partner(second)
    mixed_both = with_partner(*mixed)
    normed_both = with_partner(normed)
    down_both = with_partner(down_in)
    inner_grad, second_grad = mlp_call(
        mlp_back_kernel, [tokens(down_in), inner], w_mlp, [low]
    )
    second_grad = second_grad.reshape(images, SEQ, D)
    inner_both = half_with_partner(inner_grad)
    inner_grad, down_both, active_both = together(inner_grad, down_both, active_both)
    grad_down = matmul("to,tf->of", down_both, active_both).astype(low)
    inner_both, grad_down = together(inner_both, grad_down)
    grad_up = matmul("td,tf->df", second_both, inner_both).astype(low)
    grad_mlp = jnp.concatenate([grad_up, grad_down], 1)
    second_grad, grad_mlp = together(second_grad, grad_mlp)
    near_mlp = sum_near(grad_mlp)
    back_mid, shift_b, scale_b = modulate_back(middle, pieces[3], pieces[4], second_grad)
    grad_mid = upstream + back_mid
    proj_in = (pieces[2][:, None, :] * grad_mid).astype(low)
    gate_a = jnp.sum(grad_mid * attended, 1)
    proj_both = with_partner(proj_in)
    final_low = final_grad.astype(low)
    early = links.outer(jnp.stack([gate_a, shift_b, scale_b, gate_b], 1)).reshape(images, 4 * D)
    early = early.astype(low)
    early = links.spread(jnp.concatenate([early, final_low], 1)).reshape(everyone, 6 * D)
    qkv_grad = [
        attend_back(kept[half], matmul("iso,od->isd", proj_in, w_proj[half])) for half in range(2)
    ]
    grad_proj = matmul("to,td->od", proj_both, mixed_both)
    qkv_both = with_partner(*qkv_grad)
    normed_grad = sum(matmul("ise,de->isd", qkv_grad[half], w_qkv[half]) for half in range(2))
    back_in, shift_a, scale_a = modulate_back(stream, pieces[0], pieces[1], normed_grad)
    stream_grad = grad_mid + back_in
    late = links.outer(jnp.stack([shift_a, scale_a], 1)).reshape(images, 2 * D).astype(low)
    late, stream_grad, qkv_both, early = together(late, stream_grad, qkv_both, early)
    late = links.spread(late).reshape(everyone, 2 * D)
    grad_qkv = matmul("td,te->de", normed_both, qkv_both)
    grad_patch = matmul("isp,isd->dp", noisy_rows, stream_grad.astype(low))
    small_grad = links.outer(jnp.concatenate([grad_patch, grad_head], 1).T).T
    small_grad = small_grad.reshape(links.count, -1)
    sums_of_attention = Reduction(links, [grad_qkv, grad_proj])
    more = sums_of_attention.send("yx")

    late, near_mlp = together(late, near_mlp)
    reduced_mlp = sum_far(near_mlp).astype(wide)
    all_final = early[:, 4 * D :]
    all_modulation = jnp.concatenate([late, early[:, : 4 * D]], 1)
    own_modulation = lax.dynamic_slice_in_dim(all_modulation, col_at, own_cols, 1)
    signal_part = matmul("ir,rd->id", window.cut(all_final, STARTS[3]), stem)
    ada_part = matmul("ic,rc->ir", own_modulation, ada_low)
    signal_part = lax.dynamic_update_slice_in_dim(
        signal_part,
        lax.dynamic_slice_in_dim(signal_part, row_at, own_rows, 1) + ada_part,
        row_at,
        1,
    )
    sums = jnp.concatenate([links.outer(jnp.sum(stream_grad, (0, 1))), jnp.sum(final_grad, 0)])
    share = -(-sums.shape[0] // links.count)
    sums = jnp.pad(sums, (0, share * links.count - sums.shape[0])).reshape(links.count, share)
    summed = links.deliver(
        jnp.concatenate([signal_part.reshape(links.count, images * D), sums, small_grad], 1)
    ).sum(0)
    small = summed[images * D + share :]
    condition_grad = smooth_back(jax.nn.silu, condition, summed[: images * D].reshape(images, D))
    spreading = jnp.concatenate([condition_grad.reshape(-1), summed[images * D : images * D + share]])
    spreading, more = together(spreading, more)
    sums_of_attention.add(more)
    more = sums_of_attention.send("xy")
    spread = links.spread(spreading)
    all_condition = spread[:, : images * D].reshape(everyone, D)
    all_sums = spread[:, images * D :].reshape(-1)[: 3 * D]
    condition_low = all_condition.astype(low)
    hidden_part = matmul("id,rd->ir", condition_low, stem)
    before_part = window.cut(all_before, STARTS[1])
    before_part = smooth_back(jax.nn.silu, before_part, hidden_part)
    row = window.first + jnp.arange(window.rows)
    before_part = jnp.where((row >= STARTS[1]) & (row < STARTS[2]), before_part, 0.0).astype(low)
    before_part, more = together(before_part, more)
    sums_of_attention.add(more)
    sums_of_attention.join()
    more = sums_of_attention.send("z")
    windows = links.spread(before_part)
    sums_of_attention.add(more)
    reduced_attention = sums_of_attention.result()
    square = (
        jnp.sum(reduced_attention * reduced_attention)
        + jnp.sum(reduced_mlp * reduced_mlp)
        + jnp.sum(small * small)
    )
    windows, square = together(windows, square)
    totals = links.spread(jnp.stack([loss_local, square])).sum(0)
    before_low = window.assemble(windows, STARTS[1], D).astype(low)
    joint = jnp.concatenate([reduced_attention, reduced_mlp], 1)
    block_grad = flat_gradient(links, joint, small)
    totals, block_grad = together(totals, block_grad)
    loss_total, squares = totals[0], totals[1]
    bias_rows = jnp.concatenate(
        [all_sums, jnp.sum(all_modulation.astype(wide), 0)]
    ).reshape(bias_extent, D)

    def product_squares(left, right):
        left, right = left.astype(wide), right.astype(wide)
        grams = [jnp.dot(rows, rows.T, precision=HIGHEST_PRECISION) for rows in (left, right)]
        return jnp.sum(grams[0] * grams[1])

    squares = (
        squares
        + product_squares(all_signal, all_modulation)
        + product_squares(all_signal, all_final)
        + product_squares(one_hot, all_condition)
        + product_squares(all_hidden, condition_low)
        + product_squares(timing, before_low)
        + jnp.sum(bias_rows * bias_rows)
    )
    ada_grad = matmul("ir,ic->rc", signal_rows, own_modulation)
    low_left = jnp.concatenate(
        [
            window.cut(timing, STARTS[0]),
            window.cut(all_hidden, STARTS[1]),
            window.cut(all_final, STARTS[3]),
        ],
        0,
    )
    low_right = jnp.concatenate([before_low, condition_low, all_signal], 0)
    stem_rows = matmul("ir,id->rd", low_left, low_right)
    wide_left = jnp.concatenate(
        [window.cut(one_hot.astype(wide), STARTS[2]), mark.astype(wide)], 0
    )
    wide_right = jnp.concatenate([all_condition, bias_rows], 0)
    stem_rows = stem_rows + jnp.dot(wide_left.T, wide_right, precision=HIGHEST_PRECISION)
    stem_grad = window.flatten(stem_rows)
    grad_norm = jnp.sqrt(squares)
    factor = THRESHOLD / jnp.maximum(grad_norm, THRESHOLD)
    block_new = adam_update(block_master, block_grad * factor, block_m, block_v)
    stem_new = adam_update(stem_master, stem_grad * factor, stem_m, stem_v)
    ada_new = adam_update(ada_w, ada_grad * factor, ada_w_m, ada_w_v)
    return (loss_total, grad_norm, *block_new, *stem_new, *ada_new)


def solution(mesh):
    links = Links(mesh.shape["dp"], mesh.shape["mod"])
    grid = jax.sharding.Mesh(
        mesh.devices.reshape(links.z, links.x, links.y, links.core), AXES
    )
    flat, rows, ada = P(AXES), P(AXES, None), P(("z", "x"), ("y", "c"))
    return jax.shard_map(
        functools.partial(shards, links),
        mesh=grid,
        in_specs=(rows, rows) + (flat,) * 9 + (ada,) * 3,
        out_specs=(P(), P()) + (flat,) * 6 + (ada,) * 3,
        check_vma=False,
    )
```
